512 devices in a mesh: gx: 64 (over x, z), gz: 8 (over y, core).
Axes of the slice: x: 4, y: 4, z: 16, core: 2. Of those that a mesh axis runs over, the one named last changes fastest.
Arguments:
- right_side: float32 [512, 512, 128], P('gx', 'gz'), may hold values from -6 to 6
- conductivity: float32 [512, 512, 128], P('gx', 'gz'), may hold values from 0.5 to 8
Outputs:
- solution_field: float32 [512, 512, 128], P('gx', 'gz')
The draws below stay inside these ranges and needn't reach their ends.
All inputs are finite; a program needn't handle non-finite values.
Results may differ from the reference program's by a relative error of at most 0.0001.
Values sent between devices are 32-bit elements; how exact they have to be, the bound alone decides.
No kernel may reach another device: no remote copies, remote signals or barrier semaphores. Data moves between devices by JAX's collectives and lax.ppermute only.
A program may use at most 64 MiB of HBM per device.

```python
import math
import jax
import jax.numpy as jnp

NY = 128
SWEEPS = 2
COARSE_ITERS = 20
NX = 512
NZ = 512


def draw_right_side(key, part):
    key = jax.random.fold_in(key, 11)
    shape = (NX, NZ, NY)
    values = jnp.clip(jax.random.normal(key, shape, jnp.float32), -6.0, 6.0)
    return values.astype(jnp.float32)


def block_scale(stream_key, dims, shards, low, largest):
    def one(position, shards_of):
        draws = jax.random.uniform(jax.random.fold_in(jax.random.fold_in(stream_key, 6), position), (shards_of,), jnp.float32, low / len(shards), largest / len(shards))
        return jnp.repeat(jnp.exp(draws), dims[position] // shards_of).reshape((-1,) + (1,) * (len(dims) - position - 1))

    gain = one(*shards[0])
    for cut in shards[1:]:
        gain = gain * one(*cut)
    return gain


def setup_inputs(seed: int = 0) -> dict:
    arg_keys = jax.random.split(jax.random.key(seed), 3)
    return {
        "right_side": draw_right_side(jax.random.fold_in(arg_keys[2], 71), 0),
        "conductivity": jnp.clip(jnp.exp(math.log(8.0) - 2.7725887 * jax.random.uniform(arg_keys[1], (NX, NZ, NY), jnp.float32) ** block_scale(arg_keys[1], (NX, NZ, NY), ((0, 64), (1, 8)), -0.2, 0.2)), 0.5, 8.0),
    }


def coefs_from_padded(padded):
    face_zero = 0.5 * (padded[:-1, 1:-1, 1:-1] + padded[1:, 1:-1, 1:-1])
    face_one = 0.5 * (padded[1:-1, :-1, 1:-1] + padded[1:-1, 1:, 1:-1])
    face_two = 0.5 * (padded[1:-1, 1:-1, :-1] + padded[1:-1, 1:-1, 1:])
    diagonal = face_zero[:-1] + face_zero[1:] + face_one[:, :-1] + face_one[:, 1:] + face_two[:, :, :-1] + face_two[:, :, 1:]
    return (face_zero, face_one, face_two, diagonal)


def operate_padded(padded, coefs, scale):
    face_zero, face_one, face_two, diagonal = coefs
    center = padded[1:-1, 1:-1, 1:-1]
    beside = face_zero[:-1] * padded[:-2, 1:-1, 1:-1] + face_zero[1:] * padded[2:, 1:-1, 1:-1]
    beside = beside + face_one[:, :-1] * padded[1:-1, :-2, 1:-1] + face_one[:, 1:] * padded[1:-1, 2:, 1:-1]
    beside = beside + face_two[:, :, :-1] * padded[1:-1, 1:-1, :-2] + face_two[:, :, 1:] * padded[1:-1, 1:-1, 2:]
    return scale * (diagonal * center - beside)


def restrict(field):
    size_a, size_b, size_c = field.shape
    return field.reshape(size_a // 2, 2, size_b // 2, 2, size_c // 2, 2).mean(axis=(1, 3, 5))


def prolong(field):
    return jnp.repeat(jnp.repeat(jnp.repeat(field, 2, 0), 2, 1), 2, 2)


def cheb_weights(count, lower, upper):
    theta = 0.5 * (upper + lower)
    delta = 0.5 * (upper - lower)
    sigma = theta / delta
    rho_prev = 1.0 / sigma
    carry_terms = [0.0]
    gain_terms = [1.0 / theta]
    for step in range(1, count):
        rho_next = 1.0 / (2.0 * sigma - rho_prev)
        carry_terms.append(rho_next * rho_prev)
        gain_terms.append(2.0 * rho_next / delta)
        rho_prev = rho_next
    return carry_terms, gain_terms


def smooth(guess, source, coefs, scale, count, lower, upper):
    carry_terms, gain_terms = cheb_weights(count, lower, upper)
    inverse = 1.0 / (scale * coefs[3])
    update = jnp.zeros_like(guess)
    for step in range(count):
        remainder = source - operate_padded(jnp.pad(guess, 1), coefs, scale)
        update = carry_terms[step] * update + gain_terms[step] * (inverse * remainder)
        guess = guess + update
    return guess


def reference(right_side, conductivity):
    conds = [conductivity]
    for level in range(3):
        conds.append(restrict(conds[-1]))
    coefs = [coefs_from_padded(jnp.pad(cond, 1)) for cond in conds]
    sources = [right_side]
    guesses = []
    for level in range(3):
        scale = 0.25 ** level
        guess = smooth(jnp.zeros_like(sources[level]), sources[level], coefs[level], scale, SWEEPS, 0.25, 2.0)
        remainder = sources[level] - operate_padded(jnp.pad(guess, 1), coefs[level], scale)
        guesses.append(guess)
        sources.append(restrict(remainder))
    coarse = smooth(jnp.zeros_like(sources[3]), sources[3], coefs[3], 0.25 ** 3, COARSE_ITERS, 0.02, 2.0)
    for level in (2, 1, 0):
        start = guesses[level] + prolong(coarse)
        coarse = smooth(start, sources[level], coefs[level], 0.25 ** level, SWEEPS, 0.25, 2.0)
    return coarse
```

```python
import functools

import jax
import jax.numpy as jnp
from jax import lax
from jax.experimental import pallas as pl
from jax.experimental.pallas import tpu as pltpu
from jax.sharding import PartitionSpec as P

COARSE_ITERS = 20
LANES = 128
ROW = 16
VMEM_LIMIT = 48 * 1024 * 1024


def cheb_weights(count, lower, upper):
    theta = 0.5 * (upper + lower)
    delta = 0.5 * (upper - lower)
    sigma = theta / delta
    rho_prev = 1.0 / sigma
    carry_terms = [0.0]
    gain_terms = [1.0 / theta]
    for step in range(1, count):
        rho_next = 1.0 / (2.0 * sigma - rho_prev)
        carry_terms.append(rho_next * rho_prev)
        gain_terms.append(2.0 * rho_next / delta)
        rho_prev = rho_next
    return (carry_terms, gain_terms)


(_, CARRY), (GAIN_FIRST, GAIN) = cheb_weights(2, 0.25, 2.0)


def lanes_of(rows):
    return lax.broadcasted_iota(jnp.int32, (rows, LANES), 1)


def rows_of(rows):
    return lax.broadcasted_iota(jnp.int32, (rows, LANES), 0)


def roll(value, shift, axis=1):
    return pltpu.roll(value, shift % value.shape[axis], axis)


def pair_sum(value, stride):
    odd = (lanes_of(value.shape[0]) // stride) % 2 == 1
    return value + jnp.where(odd, roll(value, stride), roll(value, -stride))


class Level:
    def __init__(self, level, gx, gz, brick, cells, first_plane, refs):
        self.stride, self.scale = (2**level, 0.25**level)
        self.gx, self.gz, self.brick, self.cells, self.first_plane = (gx, gz, brick, cells, first_plane)
        self.half, self.fx, self.fz, self.left, self.right, self.diag, self.inverse = refs

    def coefs(self, planes, row, count):
        half, stride = (self.half, self.stride)
        lane = lanes_of(count)
        here = rows_of(count) + (row - ROW + self.gz * self.brick[1])
        first, last = (planes[0], planes[-1])
        for p in planes:
            self.fx[p, row : row + count, :] = half[p - 1, row : row + count, :] + half[p, row : row + count, :]
        p = last + 1
        self.fx[p, row : row + count, :] = half[p - 1, row : row + count, :] + half[p, row : row + count, :]
        more = count + 8
        for p in planes:
            self.fz[p, row : row + more, :] = half[p, row - 1 : row - 1 + more, :] + half[p, row : row + more, :]
        for p in planes:
            center = half[p, row : row + count, :]
            face_left = center + jnp.where(lane >= stride, roll(center, stride), 0.0)
            face_right = center + jnp.where(lane < LANES - stride, roll(center, -stride), 0.0)
            diagonal = (
                self.fx[p, row : row + count, :]
                + self.fx[p + 1, row : row + count, :]
                + self.fz[p, row : row + count, :]
                + self.fz[p, row + 1 : row + 1 + count, :]
                + face_left
                + face_right
            )
            self.left[p, row : row + count, :] = jnp.where(lane >= stride, face_left, 0.0)
            self.right[p, row : row + count, :] = jnp.where(lane < LANES - stride, face_right, 0.0)
            self.diag[p, row : row + count, :] = diagonal
            plane = p - self.first_plane + self.gx * self.brick[0]
            outside = jnp.where(jnp.logical_and(plane >= 0, plane < self.cells[0]), 0, 1 << 20)
            index = here + outside
            inside = (index >= 0) & (index < self.cells[1]) & (diagonal > 0.0)
            self.inverse[p, row : row + count, :] = jnp.where(inside, 1.0 / (self.scale * diagonal), 0.0)

    def remainder(self, source, guess, p, row, count):
        center = guess[p, row : row + count, :]
        beside = (
            self.fx[p, row : row + count, :] * guess[p - 1, row : row + count, :]
            + self.fx[p + 1, row : row + count, :] * guess[p + 1, row : row + count, :]
        )
        beside = beside + (
            self.fz[p, row : row + count, :] * guess[p, row - 1 : row - 1 + count, :]
            + self.fz[p, row + 1 : row + 1 + count, :] * guess[p, row + 1 : row + 1 + count, :]
        )
        beside = beside + (
            self.left[p, row : row + count, :] * roll(center, self.stride)
            + self.right[p, row : row + count, :] * roll(center, -self.stride)
        )
        applied = self.diag[p, row : row + count, :] * center - beside
        return source[p, row : row + count, :] - self.scale * applied

    def second_down(self, source, first, out, planes, row, count):
        for p in planes:
            rest = self.remainder(source, first, p, row, count)
            start = first[p, row : row + count, :]
            update = CARRY * start + GAIN * (self.inverse[p, row : row + count, :] * rest)
            out[p, row : row + count, :] = start + update

    def restricted_remainder(self, source, guess, temp, planes, rows):
        parts = []
        for p in planes[::2]:
            both = self.remainder(source, guess, p, ROW, rows) + self.remainder(source, guess, p + 1, ROW, rows)
            temp[0:rows, :] = pair_sum(both, self.stride)
            parts.append(0.125 * (temp[pl.ds(0, rows // 2, stride=2), :] + temp[pl.ds(1, rows // 2, stride=2), :]))
        return parts

    def up(self, source, start, middle, update, out, planes, row, count, out_row, out_count):
        for p in range(planes[0] - 1, planes[-1] + 2):
            first = GAIN_FIRST * (
                self.inverse[p, row : row + count, :] * self.remainder(source, start, p, row, count)
            )
            update[p, row : row + count, :] = first
            middle[p, row : row + count, :] = start[p, row : row + count, :] + first
        for p in planes:
            second = CARRY * update[p, out_row : out_row + out_count, :] + GAIN * (
                self.inverse[p, out_row : out_row + out_count, :]
                * self.remainder(source, middle, p, out_row, out_count)
            )
            out(p, middle[p, out_row : out_row + out_count, :] + second)


def restricted(half, temp, stride, planes, row, rows):
    parts = []
    for p in planes[::2]:
        both = half[p, row : row + rows, :] + half[p + 1, row : row + rows, :]
        temp[0:rows, :] = pair_sum(both, stride)
        parts.append(0.125 * (temp[pl.ds(0, rows // 2, stride=2), :] + temp[pl.ds(1, rows // 2, stride=2), :]))
    return parts


def first_iterate(source, half, p, row, count, level, stride):
    center = half[p][1 : 1 + count]
    lane = lanes_of(count)
    diagonal = 6.0 * center + half[p - 1][1 : 1 + count] + half[p + 1][1 : 1 + count]
    diagonal = diagonal + half[p][0:count] + half[p][2 : 2 + count]
    diagonal = diagonal + jnp.where(lane >= stride, roll(center, stride), 0.0)
    diagonal = diagonal + jnp.where(lane < LANES - stride, roll(center, -stride), 0.0)
    return GAIN_FIRST * source * (1.0 / (0.25**level * diagonal))


def cut(half_ref, planes, row, count):
    return [half_ref[p, row : row + count, :] for p in planes]


def edge_rows_0(source, cond, low, high, to_high, to_low):
    bx, bz = source.shape[0:2]
    zero = jnp.zeros((4, LANES), jnp.float32)
    for rows, out in ((slice(bz - 4, bz), to_high), (slice(0, 4), to_low)):
        out[0, 0:4, :] = zero
        out[bx + 7, 0:4, :] = zero
        for p in range(3):
            out[p + 1, 0:4, :] = low[p, rows, :]
            out[p + bx + 4, 0:4, :] = high[p, rows, :]
        for p in range(4):
            out[p, 4:8, :] = low[p + 3, rows, :]
            out[p + bx + 4, 4:8, :] = high[p + 3, rows, :]
        for p in range(bx):
            out[p + 4, 0:4, :] = source[p, rows, :]
            out[p + 4, 4:8, :] = cond[p, rows, :]


def down_0(cells, pos, source, cond, low, high, z_low, z_high, win_s, win_h, guess, message, fx, fz, left, right, diag, inverse, first, temp, next_half):
    gx, gz = (pos[0], pos[1])
    bx, bz = source.shape[0:2]
    planes = bx + 8
    zero = jnp.zeros((8, LANES), jnp.float32)
    end = ROW + bz
    for p in range(planes):
        for edge in (8, end, end + 8):
            win_s[p, edge : edge + 8, :] = zero
            win_h[p, edge : edge + 8, :] = zero
            guess[p, edge : edge + 8, :] = zero
            first[p, edge : edge + 8, :] = zero
        win_s[p, ROW - 4 : ROW, :] = z_low[p, 0:4, :]
        win_s[p, end : end + 4, :] = z_high[p, 0:4, :]
        win_h[p, ROW - 4 : ROW, :] = 0.5 * z_low[p, 4:8, :]
        win_h[p, end : end + 4, :] = 0.5 * z_high[p, 4:8, :]
    for p in range(bx):
        win_s[p + 4, ROW:end, :] = source[p, :, :]
        win_h[p + 4, ROW:end, :] = 0.5 * cond[p, :, :]
    for p in range(3):
        win_s[p + 1, ROW:end, :] = low[p, :, :]
        win_s[p + bx + 4, ROW:end, :] = high[p, :, :]
    for p in range(4):
        win_h[p, ROW:end, :] = 0.5 * low[p + 3, :, :]
        win_h[p + bx + 4, ROW:end, :] = 0.5 * high[p + 3, :, :]

    level = Level(0, gx, gz, (bx, bz), cells, 4, (win_h, fx, fz, left, right, diag, inverse))
    row, count = (ROW - 4, bz + 8)
    level.coefs(range(1, planes - 1), row, count)
    for p in range(1, planes - 1):
        first[p, row : row + count, :] = GAIN_FIRST * (
            inverse[p, row : row + count, :] * win_s[p, row : row + count, :]
        )
    level.second_down(win_s, first, guess, range(2, planes - 2), row, count)
    sources = level.restricted_remainder(win_s, guess, temp, range(4, 4 + bx), bz)
    halves = restricted(win_h, temp, 1, range(2, planes - 2), ROW - 8, bz + 16)
    for p, value in enumerate(halves):
        next_half[p, :, :] = value
    own = bz // 2
    odd = lanes_of(own) % 2 == 1
    padded = cut(next_half, range(bx // 2 + 2), 3, own + 2)
    for p, value in enumerate(sources):
        message[p, :, :] = jnp.where(odd, padded[p + 1][1 : 1 + own], value)
        message[p + bx // 2, :, :] = first_iterate(value, padded, p + 1, 0, own, 1, 2)


def edge_rows(*refs):
    parts, (to_high, to_low) = (refs[:-2], refs[-2:])
    at = 0
    for part in parts:
        count, rows = part.shape[0:2]
        to_high[at : at + count, :, :] = part[:, rows - 8 : rows, :]
        to_low[at : at + count, :, :] = part[:, 0:8, :]
        at += count


def down_1(cells, pos, own_ref, low, high, z_low, z_high, win_s, win_h, guess, message, fx, fz, left, right, diag, inverse, first, temp, next_half):
    gx, gz = (pos[0], pos[1])
    bx, bz = (own_ref.shape[0] // 2, own_ref.shape[1])
    planes = 3 * bx
    end = ROW + bz
    zero = jnp.zeros((8, LANES), jnp.float32)

    def unpack(p, start, rows, mixed, iterate):
        odd = lanes_of(rows) % 2 == 1
        win_s[p, start : start + rows, :] = jnp.where(odd, roll(mixed, 1), mixed)
        win_h[p, start : start + rows, :] = jnp.where(odd, mixed, roll(mixed, -1))
        first[p, start : start + rows, :] = iterate

    for b, part in enumerate((low, own_ref, high)):
        for p in range(bx):
            q = b * bx + p
            unpack(q, ROW, bz, part[p, :, :], part[p + bx, :, :])
            unpack(q, ROW - 8, 8, z_low[2 * b * bx + p, :, :], z_low[(2 * b + 1) * bx + p, :, :])
            unpack(q, end, 8, z_high[2 * b * bx + p, :, :], z_high[(2 * b + 1) * bx + p, :, :])
    for p in range(planes):
        for ref in (win_s, win_h, first):
            ref[p, 0:8, :] = zero
            ref[p, end + 8 : end + 16, :] = zero
        guess[p, 8:16, :] = zero
        guess[p, end : end + 8, :] = zero

    level = Level(1, gx, gz, (bx, bz), cells, bx, (win_h, fx, fz, left, right, diag, inverse))
    row, count = (ROW - 4, bz + 8)
    level.coefs(range(1, planes - 1), row, count)
    level.second_down(win_s, first, guess, range(1, planes - 1), row, count)
    sources = level.restricted_remainder(win_s, guess, temp, range(bx, 2 * bx), bz)
    halves = restricted(win_h, temp, 2, range(bx - 2, 2 * bx + 2), ROW - 8, bz + 16)
    for p, value in enumerate(halves):
        next_half[p, :, :] = value
    own = bz // 2
    lane = lanes_of(own) % 4
    padded = cut(next_half, range(bx // 2 + 2), 3, own + 2)
    for p, value in enumerate(sources):
        iterate = first_iterate(value, padded, p + 1, 0, own, 2, 4)
        mixed = jnp.where(lane == 0, value, jnp.where(lane == 1, padded[p + 1][1 : 1 + own], iterate))
        message[p, :, :] = mixed


def spread(mixed, which):
    only = jnp.where(lanes_of(mixed.shape[0]) % 4 == which, mixed, 0.0)
    only = roll(only, -which) if which else only
    twice = only + roll(only, 1)
    return twice + roll(twice, 2)


def down_2(cells, pos, *refs):
    bricks, refs = (refs[:7], refs[7:])
    z_low, z_high, win_s, win_h, guess, message, fx, fz, left, right, diag, inverse, first, temp = refs
    gx, gz = (pos[0], pos[1])
    bx, bz = bricks[0].shape[0:2]
    planes = 7 * bx
    end = ROW + bz
    zero = jnp.zeros((8, LANES), jnp.float32)

    def unpack(p, start, rows, mixed):
        win_s[p, start : start + rows, :] = spread(mixed, 0)
        win_h[p, start : start + rows, :] = spread(mixed, 1)
        first[p, start : start + rows, :] = spread(mixed, 2)

    for b, part in enumerate(bricks):
        for p in range(bx):
            q = b * bx + p
            unpack(q, ROW, bz, part[p, :, :])
            unpack(q, ROW - 8, 8, z_low[q, :, :])
            unpack(q, end, 8, z_high[q, :, :])
    for p in range(planes):
        for ref in (win_s, win_h, first):
            ref[p, 0:8, :] = zero
            ref[p, end + 8 : end + 16, :] = zero
    level = Level(2, gx, gz, (bx, bz), cells, 3 * bx, (win_h, fx, fz, left, right, diag, inverse))
    row, count = (ROW - 8, bz + 16)
    own = 3 * bx
    level.coefs(range(own - 4, own + bx + 4), row, count)
    level.second_down(win_s, first, guess, range(own - 4, own + bx + 4), row, count)
    sources = level.restricted_remainder(win_s, guess, temp, range(own, own + bx), bz)
    halves = restricted(win_h, temp, 4, range(own, own + bx), ROW, bz)
    rows = bz // 2
    cell = lax.broadcasted_iota(jnp.int32, (LANES, LANES), 0)
    lane = lax.broadcasted_iota(jnp.int32, (LANES, LANES), 1)
    pick = jnp.where((cell // 8 == lane % 16) & (cell % 8 == 0), 1.0, 0.0)
    keep = lanes_of(rows) // 16 == rows_of(rows)
    for at, value in enumerate((sources[0], halves[0])):
        dense = jnp.dot(value, pick, precision=lax.Precision.HIGHEST, preferred_element_type=jnp.float32)
        message[at : at + 1, :] = jnp.sum(jnp.where(keep, dense, 0.0), axis=0, keepdims=True)


def before_z(value):
    moved = roll(value, 16)
    return jnp.where(lanes_of(8) < 16, roll(moved, 1, 0), moved)


def after_z(value):
    moved = roll(value, -16)
    return jnp.where(lanes_of(8) >= LANES - 16, roll(moved, -1, 0), moved)


def solve_coarsest(gathered, source, half, base, weights, state, update):
    planes = gathered.shape[0] // 16
    for g in range(8):
        first = 2 * planes * g
        source[pl.ds(g, planes, stride=8), :] = gathered[pl.ds(first, planes, stride=2), :]
        half[pl.ds(g, planes, stride=8), :] = gathered[pl.ds(first + 1, planes, stride=2), :]
    lane, sub = (lanes_of(8), rows_of(8))
    in_left, in_right = (lane % 16 > 0, lane % 16 < 15)
    in_before = (lane >= 16) | (sub > 0)
    in_after = (lane < LANES - 16) | (sub < 7)
    zero = jnp.zeros((8, LANES), jnp.float32)
    first_gain = cheb_weights(COARSE_ITERS, 0.02, 2.0)[1][0]
    for buffer in range(2):
        state[buffer, 0, :, :] = zero
        state[buffer, planes + 1, :, :] = zero

    def at(ref, p):
        return ref[8 * p : 8 * p + 8, :]

    for p in range(planes):
        center = at(half, p)
        low = at(half, p - 1) if p else zero
        high = at(half, p + 1) if p < planes - 1 else zero
        neighbours = (
            (low, None),
            (high, None),
            (before_z(center), in_before),
            (after_z(center), in_after),
            (roll(center, 1), in_left),
            (roll(center, -1), in_right),
        )
        faces = [center + (value if mask is None else jnp.where(mask, value, 0.0)) for value, mask in neighbours]
        diagonal = faces[0] + faces[1] + faces[2] + faces[3] + faces[4] + faces[5]
        inverse = 1.0 / diagonal
        for which, (face, (_, mask)) in enumerate(zip(faces, neighbours)):
            scaled = face * inverse
            base[which, p, :, :] = scaled if mask is None else jnp.where(mask, scaled, 0.0)
        scaled = 64.0 * (at(source, p) * inverse)
        base[6, p, :, :] = scaled
        start = first_gain * scaled
        update[p, :, :] = start
        state[0, p + 1, :, :] = start

    def step(index, old, new):
        carry, gain = (weights[index, 0], weights[index, 1])
        before, center = (zero, state[old, 1, :, :])
        for p in range(planes):
            after = state[old, p + 2, :, :]
            beside = base[0, p, :, :] * before + base[1, p, :, :] * after
            beside = beside + (base[2, p, :, :] * before_z(center) + base[3, p, :, :] * after_z(center))
            beside = beside + (base[4, p, :, :] * roll(center, 1) + base[5, p, :, :] * roll(center, -1))
            change = carry * update[p, :, :] + gain * (base[6, p, :, :] - center + beside)
            update[p, :, :] = change
            state[new, p + 1, :, :] = center + change
            before, center = (center, after)

    def two_steps(pair, unused):
        step(2 * pair + 1, 0, 1)
        step(2 * pair + 2, 1, 0)
        return unused

    lax.fori_loop(0, (COARSE_ITERS - 1) // 2, two_steps, 0)
    step(COARSE_ITERS - 1, 0, 1)
    return 1


def finish(cells, pos, weights, gathered, s2, h2, g2, s1, h1, g1, s0, h0, g0, out, *scratch):
    gx, gz = (pos[0], pos[1])
    source3, half3, base, state, update3, coarse2, temp = scratch[:7]
    f2, f1, f0 = (scratch[7:16], scratch[16:25], scratch[25:34])
    planes3 = gathered.shape[0] // 16
    last = solve_coarsest(gathered, source3, half3, base, weights, state, update3)

    bx2, bz2 = (2, s2.shape[1] - 32)
    rows = bz2 + 8
    cell = lax.broadcasted_iota(jnp.int32, (LANES, LANES), 0)
    lane = lax.broadcasted_iota(jnp.int32, (LANES, LANES), 1)
    pick = jnp.where(cell % 16 == lane // 8, 1.0, 0.0)
    z3 = rows_of(rows) // 2 - 2
    keep = lanes_of(rows) // 16 == (z3 + 8) % 8
    sub = rows_of(8)
    for q in range(5):
        plane = gx + q - 2
        inside = jnp.logical_and(plane >= 0, plane < planes3)
        value = state[last, pl.ds(jnp.clip(plane, -1, planes3) + 1, 1), :, :][0]
        picked = [jnp.sum(jnp.where(sub == gz + d, value, 0.0), axis=0, keepdims=True) for d in (-1, 0, 1)]
        wide = jnp.where(z3 < 0, picked[0], jnp.where(z3 < 8, picked[1], picked[2]))
        coarse2[q * rows : (q + 1) * rows, :] = jnp.where(keep, wide, 0.0)
    spread_out = jnp.dot(coarse2[...], pick, precision=lax.Precision.HIGHEST, preferred_element_type=jnp.float32)
    coarse2[...] = spread_out

    half_planes = s2.shape[0] // 2
    start, middle, update = f2[6:9]
    own = half_planes - 1
    row, count = (ROW - 4, rows)
    zero = jnp.zeros((8, LANES), jnp.float32)
    for q in range(5):
        for p in (own - 4 + 2 * q, own - 3 + 2 * q):
            start[p, 8:16, :] = zero
            start[p, ROW + bz2 : ROW + bz2 + 8, :] = zero
            start[p, row : row + count, :] = g2[p, row : row + count, :] + coarse2[q * rows : (q + 1) * rows, :]
    level = Level(2, gx, gz, (bx2, bz2), cells[2], own, (h2,) + tuple(f2[0:6]))
    level.coefs(range(own - 3, own + 5), row, count)

    bx1, bz1 = (4, s1.shape[1] - 32)
    start1, middle1, update1 = f1[6:9]

    def to_level_1(p, value):
        q = 2 * (p - own) + 4
        temp[pl.ds(0, value.shape[0], stride=2), :] = value
        temp[pl.ds(1, value.shape[0], stride=2), :] = value
        for r in (q, q + 1):
            if 1 <= r <= 10:
                start1[r, ROW - 4 : ROW + bz1 + 4, :] = (
                    g1[r, ROW - 4 : ROW + bz1 + 4, :] + temp[0 : bz1 + 8, :]
                )

    for r in range(1, 11):
        start1[r, 8:16, :] = zero
        start1[r, ROW + bz1 : ROW + bz1 + 8, :] = zero
    level.up(s2, start, middle, update, to_level_1, range(own - 2, own + 4), row, count, ROW - 2, bz2 + 4)
    level = Level(1, gx, gz, (bx1, bz1), cells[1], 4, (h1,) + tuple(f1[0:6]))
    row, count = (ROW - 4, bz1 + 8)
    level.coefs(range(2, 10), row, count)

    bx0, bz0 = (out.shape[0], out.shape[1])
    start0, middle0, update0 = f0[6:9]
    for r in range(2, 14):
        start0[r, 8:16, :] = zero
        start0[r, ROW + bz0 : ROW + bz0 + 8, :] = zero

    def to_level_0(p, value):
        q = 2 * (p - 4) + 4
        temp[pl.ds(0, value.shape[0], stride=2), :] = value
        temp[pl.ds(1, value.shape[0], stride=2), :] = value
        for r in (q, q + 1):
            start0[r, ROW - 4 : ROW + bz0 + 4, :] = g0[r, ROW - 4 : ROW + bz0 + 4, :] + temp[0 : bz0 + 8, :]

    level.up(s1, start1, middle1, update1, to_level_0, range(3, 9), row, count, ROW - 2, bz1 + 4)
    level = Level(0, gx, gz, (bx0, bz0), cells[0], 4, (h0,) + tuple(f0[0:6]))
    level.coefs(range(3, 13), ROW - 4, bz0 + 8)

    def to_out(p, value):
        out[p - 4, :, :] = value

    level.up(s0, start0, middle0, update0, to_out, range(4, 12), ROW - 4, bz0 + 8, ROW, bz0)


def f32(*shape):
    return jax.ShapeDtypeStruct(shape, jnp.float32)


def scratch(*shape):
    return pltpu.VMEM(shape, jnp.float32)


def call(kernel, name, outs, scratches, scalars, *args):
    smem = pl.BlockSpec(memory_space=pltpu.SMEM)
    vmem = pl.BlockSpec(memory_space=pltpu.VMEM)
    return pl.pallas_call(
        kernel,
        name=name,
        out_shape=outs,
        in_specs=[smem] * scalars + [vmem] * (len(args) - scalars),
        out_specs=[vmem] * len(outs),
        scratch_shapes=scratches,
        compiler_params=pltpu.CompilerParams(vmem_limit_bytes=VMEM_LIMIT),
    )(*args)


def shift(array, axis, by):
    devices = lax.axis_size(axis)
    return lax.ppermute(array, axis, [(i, i + by) for i in range(devices) if 0 <= i + by < devices])


def on_device(right_side, conductivity):
    nx, nz = (lax.axis_size("gx"), lax.axis_size("gz"))
    bx, bz = right_side.shape[0:2]
    cells = [(nx * bx >> level, nz * bz >> level) for level in range(4)]
    pos = jnp.stack([lax.axis_index("gx"), lax.axis_index("gz")]).astype(jnp.int32)
    weights = jnp.asarray(list(zip(*cheb_weights(COARSE_ITERS, 0.02, 2.0))), jnp.float32)

    low = shift(jnp.concatenate([right_side[bx - 3 :], conductivity[bx - 4 :]]), "gx", 1)
    high = shift(jnp.concatenate([right_side[:3], conductivity[:4]]), "gx", -1)
    planes = bx + 8
    to_high, to_low = call(
        edge_rows_0, "edge_rows_0", [f32(planes, 8, LANES)] * 2, [], 0, right_side, conductivity, low, high
    )
    z_low, z_high = (shift(to_high, "gz", 1), shift(to_low, "gz", -1))
    window = (planes, bz + 32, LANES)
    s0, h0, g0, brick1 = call(
        functools.partial(down_0, cells[0]),
        "down_0",
        [f32(*window)] * 3 + [f32(bx, bz // 2, LANES)],
        [scratch(*window)] * 7 + [scratch(bz + 16, LANES), scratch(bx // 2 + 2, bz // 2 + 8, LANES)],
        1,
        pos,
        right_side,
        conductivity,
        low,
        high,
        z_low,
        z_high,
    )

    low, high = (shift(brick1, "gx", 1), shift(brick1, "gx", -1))
    to_high, to_low = call(edge_rows, "edge_rows_1", [f32(3 * bx, 8, LANES)] * 2, [], 0, low, brick1, high)
    z_low, z_high = (shift(to_high, "gz", 1), shift(to_low, "gz", -1))
    bx, bz = (bx // 2, bz // 2)
    window1 = (3 * bx, bz + 32, LANES)
    s1, h1, g1, brick2 = call(
        functools.partial(down_1, cells[1]),
        "down_1",
        [f32(*window1)] * 3 + [f32(bx // 2, bz // 2, LANES)],
        [scratch(*window1)] * 7 + [scratch(bz + 16, LANES), scratch(bx // 2 + 2, bz // 2 + 8, LANES)],
        1,
        pos,
        brick1,
        low,
        high,
        z_low,
        z_high,
    )

    bx, bz = (bx // 2, bz // 2)
    bricks = [shift(brick2, "gx", by) if by else brick2 for by in (3, 2, 1, 0, -1, -2, -3)]
    to_high, to_low = call(edge_rows, "edge_rows_2", [f32(7 * bx, 8, LANES)] * 2, [], 0, *bricks)
    z_low, z_high = (shift(to_high, "gz", 1), shift(to_low, "gz", -1))
    window2 = (7 * bx, bz + 32, LANES)
    s2, h2, g2, brick3 = call(
        functools.partial(down_2, cells[2]),
        "down_2",
        [f32(*window2)] * 3 + [f32(2, LANES)],
        [scratch(*window2)] * 7 + [scratch(bz + 16, LANES)],
        1,
        pos,
        *bricks,
        z_low,
        z_high,
    )

    everywhere = lax.all_to_all(jnp.broadcast_to(brick3[None], (nx, 2, LANES)), "gx", 0, 0, tiled=True)
    gathered = lax.all_gather(everywhere, "gz", axis=0).reshape(nz * 2 * nx, LANES)
    work = (
        [scratch(8 * nx, LANES)] * 2
        + [scratch(7, nx, 8, LANES), scratch(2, nx + 2, 8, LANES), scratch(nx, 8, LANES)]
        + [scratch(5 * (bz + 8), LANES), scratch(96, LANES)]
        + [scratch(*window2)] * 9
        + [scratch(*window1)] * 9
        + [scratch(*window)] * 9
    )
    (result,) = call(
        functools.partial(finish, cells), "finish", [f32(*right_side.shape)], work, 2, pos, weights, gathered,
        s2, h2, g2, s1, h1, g1, s0, h0, g0,
    )
    return result


def solution(mesh):
    return jax.shard_map(
        on_device,
        mesh=mesh,
        in_specs=(P("gx", "gz", None), P("gx", "gz", None)),
        out_specs=P("gx", "gz", None),
        check_vma=False,
    )
```

```python
import functools

import jax
import jax.numpy as jnp
from jax import lax
from jax.experimental import pallas as pl
from jax.experimental.pallas import tpu as pltpu
from jax.sharding import PartitionSpec as P

COARSE_ITERS = 20
LANES = 128
ROW = 16
VMEM_LIMIT = 48 * 1024 * 1024


def cheb_weights(count, lower, upper):
    theta = 0.5 * (upper + lower)
    delta = 0.5 * (upper - lower)
    sigma = theta / delta
    rho_prev = 1.0 / sigma
    carry_terms = [0.0]
    gain_terms = [1.0 / theta]
    for step in range(1, count):
        rho_next = 1.0 / (2.0 * sigma - rho_prev)
        carry_terms.append(rho_next * rho_prev)
        gain_terms.append(2.0 * rho_next / delta)
        rho_prev = rho_next
    return (carry_terms, gain_terms)


(_, CARRY), (GAIN_FIRST, GAIN) = cheb_weights(2, 0.25, 2.0)


def lanes_of(rows):
    return lax.broadcasted_iota(jnp.int32, (rows, LANES), 1)


def rows_of(rows):
    return lax.broadcasted_iota(jnp.int32, (rows, LANES), 0)


def roll(value, shift, axis=1):
    return pltpu.roll(value, shift % value.shape[axis], axis)


def pair_sum(value, stride):
    odd = (lanes_of(value.shape[0]) & stride) != 0
    return value + jnp.where(odd, roll(value, stride), roll(value, -stride))


class Level:
    def __init__(self, level, gx, gz, brick, cells, first_plane, refs):
        self.stride, self.scale = (2**level, 0.25**level)
        self.gx, self.gz, self.brick, self.cells, self.first_plane = (gx, gz, brick, cells, first_plane)
        self.half, self.fx, self.fz, self.left, self.right, self.diag, self.inverse = refs

    def coefs(self, planes, row, count):
        half, stride = (self.half, self.stride)
        lane = lanes_of(count)
        here = rows_of(count) + (row - ROW + self.gz * self.brick[1])
        first, last = (planes[0], planes[-1])
        for p in planes:
            self.fx[p, row : row + count, :] = half[p - 1, row : row + count, :] + half[p, row : row + count, :]
        p = last + 1
        self.fx[p, row : row + count, :] = half[p - 1, row : row + count, :] + half[p, row : row + count, :]
        more = count + 8
        for p in planes:
            self.fz[p, row : row + more, :] = half[p, row - 1 : row - 1 + more, :] + half[p, row : row + more, :]
        for p in planes:
            center = half[p, row : row + count, :]
            face_left = center + jnp.where(lane >= stride, roll(center, stride), 0.0)
            face_right = center + jnp.where(lane < LANES - stride, roll(center, -stride), 0.0)
            diagonal = (
                self.fx[p, row : row + count, :]
                + self.fx[p + 1, row : row + count, :]
                + self.fz[p, row : row + count, :]
                + self.fz[p, row + 1 : row + 1 + count, :]
                + face_left
                + face_right
            )
            self.left[p, row : row + count, :] = jnp.where(lane >= stride, face_left, 0.0)
            self.right[p, row : row + count, :] = jnp.where(lane < LANES - stride, face_right, 0.0)
            self.diag[p, row : row + count, :] = diagonal
            plane = p - self.first_plane + self.gx * self.brick[0]
            outside = jnp.where(jnp.logical_and(plane >= 0, plane < self.cells[0]), 0, 1 << 20)
            index = here + outside
            inside = (index >= 0) & (index < self.cells[1]) & (diagonal > 0.0)
            self.inverse[p, row : row + count, :] = jnp.where(inside, 1.0 / (self.scale * diagonal), 0.0)

    def remainder(self, source, guess, p, row, count):
        center = guess[p, row : row + count, :]
        beside = (
            self.fx[p, row : row + count, :] * guess[p - 1, row : row + count, :]
            + self.fx[p + 1, row : row + count, :] * guess[p + 1, row : row + count, :]
        )
        beside = beside + (
            self.fz[p, row : row + count, :] * guess[p, row - 1 : row - 1 + count, :]
            + self.fz[p, row + 1 : row + 1 + count, :] * guess[p, row + 1 : row + 1 + count, :]
        )
        beside = beside + (
            self.left[p, row : row + count, :] * roll(center, self.stride)
            + self.right[p, row : row + count, :] * roll(center, -self.stride)
        )
        applied = self.diag[p, row : row + count, :] * center - beside
        return source[p, row : row + count, :] - self.scale * applied

    def second_down(self, source, first, out, planes, row, count):
        for p in planes:
            rest = self.remainder(source, first, p, row, count)
            start = first[p, row : row + count, :]
            update = CARRY * start + GAIN * (self.inverse[p, row : row + count, :] * rest)
            out[p, row : row + count, :] = start + update

    def restricted_remainder(self, source, guess, temp, planes, rows):
        parts = []
        for p in planes[::2]:
            both = self.remainder(source, guess, p, ROW, rows) + self.remainder(source, guess, p + 1, ROW, rows)
            temp[0:rows, :] = pair_sum(both, self.stride)
            parts.append(0.125 * (temp[pl.ds(0, rows // 2, stride=2), :] + temp[pl.ds(1, rows // 2, stride=2), :]))
        return parts

    def up(self, source, start, middle, update, out, planes, row, count, out_row, out_count):
        for p in range(planes[0] - 1, planes[-1] + 2):
            first = GAIN_FIRST * (
                self.inverse[p, row : row + count, :] * self.remainder(source, start, p, row, count)
            )
            update[p, row : row + count, :] = first
            middle[p, row : row + count, :] = start[p, row : row + count, :] + first
        for p in planes:
            second = CARRY * update[p, out_row : out_row + out_count, :] + GAIN * (
                self.inverse[p, out_row : out_row + out_count, :]
                * self.remainder(source, middle, p, out_row, out_count)
            )
            out(p, middle[p, out_row : out_row + out_count, :] + second)


def restricted(half, temp, stride, planes, row, rows):
    parts = []
    for p in planes[::2]:
        both = half[p, row : row + rows, :] + half[p + 1, row : row + rows, :]
        temp[0:rows, :] = pair_sum(both, stride)
        parts.append(0.125 * (temp[pl.ds(0, rows // 2, stride=2), :] + temp[pl.ds(1, rows // 2, stride=2), :]))
    return parts


def first_iterate(source, half, p, row, count, level, stride):
    center = half[p][1 : 1 + count]
    lane = lanes_of(count)
    diagonal = 6.0 * center + half[p - 1][1 : 1 + count] + half[p + 1][1 : 1 + count]
    diagonal = diagonal + half[p][0:count] + half[p][2 : 2 + count]
    diagonal = diagonal + jnp.where(lane >= stride, roll(center, stride), 0.0)
    diagonal = diagonal + jnp.where(lane < LANES - stride, roll(center, -stride), 0.0)
    inverse = jnp.where(diagonal > 0.0, 1.0 / (0.25**level * diagonal), 0.0)
    return GAIN_FIRST * source * inverse


def cut(half_ref, planes, row, count):
    return [half_ref[p, row : row + count, :] for p in planes]


def edge_rows_0(source, cond, low, high, to_high, to_low):
    bx, bz = source.shape[0:2]
    zero = jnp.zeros((4, LANES), jnp.float32)
    for rows, out in ((slice(bz - 4, bz), to_high), (slice(0, 4), to_low)):
        out[0, 0:4, :] = zero
        out[bx + 7, 0:4, :] = zero
        for p in range(3):
            out[p + 1, 0:4, :] = low[p, rows, :]
            out[p + bx + 4, 0:4, :] = high[p, rows, :]
        for p in range(4):
            out[p, 4:8, :] = low[p + 3, rows, :]
            out[p + bx + 4, 4:8, :] = high[p + 3, rows, :]
        for p in range(bx):
            out[p + 4, 0:4, :] = source[p, rows, :]
            out[p + 4, 4:8, :] = cond[p, rows, :]


def down_0(cells, pos, source, cond, low, high, z_low, z_high, win_s, win_h, guess, message, fx, fz, left, right, diag, inverse, first, temp, next_half):
    gx, gz = (pos[0], pos[1])
    bx, bz = source.shape[0:2]
    planes = bx + 8
    zero = jnp.zeros((8, LANES), jnp.float32)
    end = ROW + bz
    has_low, has_high = inside_z(gz, cells[1] // bz)
    for p in range(planes):
        for edge in (8, end, end + 8):
            win_s[p, edge : edge + 8, :] = zero
            win_h[p, edge : edge + 8, :] = zero
            guess[p, edge : edge + 8, :] = zero
            first[p, edge : edge + 8, :] = zero
        win_s[p, ROW - 4 : ROW, :] = z_low[p, 0:4, :]
        win_s[p, end : end + 4, :] = z_high[p, 0:4, :]
        win_h[p, ROW - 4 : ROW, :] = (0.5 * has_low) * z_low[p, 4:8, :]
        win_h[p, end : end + 4, :] = (0.5 * has_high) * z_high[p, 4:8, :]
    for p in range(bx):
        win_s[p + 4, ROW:end, :] = source[p, :, :]
        win_h[p + 4, ROW:end, :] = 0.5 * cond[p, :, :]
    for p in range(3):
        win_s[p + 1, ROW:end, :] = low[p, :, :]
        win_s[p + bx + 4, ROW:end, :] = high[p, :, :]
    for p in range(4):
        win_h[p, ROW:end, :] = 0.5 * low[p + 3, :, :]
        win_h[p + bx + 4, ROW:end, :] = 0.5 * high[p + 3, :, :]

    level = Level(0, gx, gz, (bx, bz), cells, 4, (win_h, fx, fz, left, right, diag, inverse))
    row, count = (ROW - 4, bz + 8)
    level.coefs(range(1, planes - 1), row, count)
    for p in range(1, planes - 1):
        first[p, row : row + count, :] = GAIN_FIRST * (
            inverse[p, row : row + count, :] * win_s[p, row : row + count, :]
        )
    level.second_down(win_s, first, guess, range(2, planes - 2), row, count)
    sources = level.restricted_remainder(win_s, guess, temp, range(4, 4 + bx), bz)
    halves = restricted(win_h, temp, 1, range(2, planes - 2), ROW - 8, bz + 16)
    for p, value in enumerate(halves):
        next_half[p, :, :] = value
    own = bz // 2
    odd = (lanes_of(own) & 1) == 1
    padded = cut(next_half, range(bx // 2 + 2), 3, own + 2)
    for p, value in enumerate(sources):
        message[p, :, :] = jnp.where(odd, padded[p + 1][1 : 1 + own], value)
        message[p + bx // 2, :, :] = first_iterate(value, padded, p + 1, 0, own, 1, 2)


def inside_z(gz, count):
    return (jnp.where(gz > 0, 1.0, 0.0), jnp.where(gz < count - 1, 1.0, 0.0))


def edge_rows(*refs):
    parts, (to_high, to_low) = (refs[:-2], refs[-2:])
    at = 0
    for part in parts:
        count, rows = part.shape[0:2]
        to_high[at : at + count, :, :] = part[:, rows - 8 : rows, :]
        to_low[at : at + count, :, :] = part[:, 0:8, :]
        at += count


def down_1(cells, pos, own_ref, low, high, z_low, z_high, win_s, win_h, guess, to_next, to_prev, fx, fz, left, right, diag, inverse, first, temp, next_half):
    gx, gz = (pos[0], pos[1])
    bx, bz = (own_ref.shape[0] // 2, own_ref.shape[1])
    planes = 3 * bx
    end = ROW + bz
    zero = jnp.zeros((8, LANES), jnp.float32)
    has_low, has_high = inside_z(gz, cells[1] // bz)

    def unpack(p, start, rows, mixed, iterate):
        odd = (lanes_of(rows) & 1) == 1
        win_s[p, start : start + rows, :] = jnp.where(odd, roll(mixed, 1), mixed)
        win_h[p, start : start + rows, :] = jnp.where(odd, mixed, roll(mixed, -1))
        first[p, start : start + rows, :] = iterate

    for b, part in enumerate((low, own_ref, high)):
        for p in range(bx):
            q = b * bx + p
            unpack(q, ROW, bz, part[p, :, :], part[p + bx, :, :])
            unpack(q, ROW - 8, 8, has_low * z_low[2 * b * bx + p, :, :], has_low * z_low[(2 * b + 1) * bx + p, :, :])
            unpack(q, end, 8, has_high * z_high[2 * b * bx + p, :, :], has_high * z_high[(2 * b + 1) * bx + p, :, :])
    for p in range(planes):
        for ref in (win_s, win_h, first):
            ref[p, 0:8, :] = zero
            ref[p, end + 8 : end + 16, :] = zero
        guess[p, 8:16, :] = zero
        guess[p, end : end + 8, :] = zero

    level = Level(1, gx, gz, (bx, bz), cells, bx, (win_h, fx, fz, left, right, diag, inverse))
    row, count = (ROW - 4, bz + 8)
    level.coefs(range(1, planes - 1), row, count)
    level.second_down(win_s, first, guess, range(1, planes - 1), row, count)
    sources = level.restricted_remainder(win_s, guess, temp, range(bx - 2, 2 * bx + 2), bz)
    halves = restricted(win_h, temp, 2, range(planes), ROW - 8, bz + 16)
    for p, value in enumerate(halves):
        next_half[p, :, :] = value
    own = bz // 2
    lane = lanes_of(own) & 3
    padded = cut(next_half, range(bx // 2 + 4), 3, own + 2)
    for p, half in enumerate(padded):
        mixed = half[1 : 1 + own]
        if 0 < p < len(padded) - 1:
            value = sources[p - 1]
            iterate = first_iterate(value, padded, p, 0, own, 2, 4)
            mixed = jnp.where(lane == 0, value, jnp.where(lane == 1, mixed, iterate))
        else:
            mixed = jnp.where(lane == 1, mixed, 0.0)
        if p < bx // 2 + 2:
            to_next[p, :, :] = mixed
        if p >= 2:
            to_prev[p - 2, :, :] = mixed


def edge_rows_2(prev, here, next_, to_high, to_low):
    at = 0
    for part, first in ((prev, 0), (here, 2), (next_, 0)):
        count, rows = (part.shape[0] - first, part.shape[1])
        to_high[at : at + count, :, :] = part[first:, rows - 8 : rows, :]
        to_low[at : at + count, :, :] = part[first:, 0:8, :]
        at += count


def spread(mixed, which):
    only = jnp.where((lanes_of(mixed.shape[0]) & 3) == which, mixed, 0.0)
    only = roll(only, -which) if which else only
    twice = only + roll(only, 1)
    return twice + roll(twice, 2)


def down_2(cells, pos, prev, here, next_, z_low, z_high, win_s, win_h, guess, message, to_next, to_prev, fx, fz, left, right, diag, inverse, first, temp):
    gx, gz = (pos[0], pos[1])
    bx, bz = (prev.shape[0] - 2, prev.shape[1])
    own, planes = (bx + 2, 3 * bx + 4)
    end = ROW + bz
    zero = jnp.zeros((8, LANES), jnp.float32)
    has_low, has_high = inside_z(gz, cells[1] // bz)

    def unpack(p, start, rows, mixed, inside):
        win_s[p, start : start + rows, :] = spread(mixed, 0)
        win_h[p, start : start + rows, :] = spread(mixed, 1)
        first[p, start : start + rows, :] = inside * spread(mixed, 2)

    bricks = [(prev, p) for p in range(bx + 2)] + [(here, p + 2) for p in range(bx)] + [(next_, p) for p in range(bx + 2)]
    for p, (part, at) in enumerate(bricks):
        plane = p - own + gx * bx
        inside = jnp.where(jnp.logical_and(plane >= 0, plane < cells[0]), 1.0, 0.0)
        unpack(p, ROW, bz, part[at, :, :], inside)
        unpack(p, ROW - 8, 8, has_low * z_low[p, :, :], inside)
        unpack(p, end, 8, has_high * z_high[p, :, :], inside)
        for ref in (win_s, win_h, first):
            ref[p, 0:8, :] = zero
            ref[p, end + 8 : end + 16, :] = zero
    level = Level(2, gx, gz, (bx, bz), cells, own, (win_h, fx, fz, left, right, diag, inverse))
    row, count = (ROW - 8, bz + 16)
    level.coefs(range(own - 2, own + bx + 2), row, count)
    level.second_down(win_s, first, guess, range(own - 2, own + bx + 2), row, count)
    lane = lanes_of(count) & 3
    for out, begin in ((to_next, own - 2), (to_prev, own)):
        mixed = guess[begin, row : row + count, :]
        for p in range(1, 4):
            mixed = jnp.where(lane == p, guess[begin + p, row : row + count, :], mixed)
        out[...] = mixed
    sources = level.restricted_remainder(win_s, guess, temp, range(own, own + bx), bz)
    halves = restricted(win_h, temp, 4, range(own, own + bx), ROW, bz)
    rows = bz // 2
    cell = lax.broadcasted_iota(jnp.int32, (LANES, LANES), 0)
    lane = lax.broadcasted_iota(jnp.int32, (LANES, LANES), 1)
    pick = jnp.where(((cell >> 3) == (lane & 15)) & ((cell & 7) == 0), 1.0, 0.0)
    keep = (lanes_of(rows) >> 4) == rows_of(rows)
    for at, value in enumerate((sources[0], halves[0])):
        dense = jnp.dot(value, pick, precision=lax.Precision.HIGHEST, preferred_element_type=jnp.float32)
        message[at : at + 1, :] = jnp.sum(jnp.where(keep, dense, 0.0), axis=0, keepdims=True)


def before_z(value):
    moved = roll(value, 16)
    return jnp.where(lanes_of(8) < 16, roll(moved, 1, 0), moved)


def after_z(value):
    moved = roll(value, -16)
    return jnp.where(lanes_of(8) >= LANES - 16, roll(moved, -1, 0), moved)


def solve_coarsest(gathered, source, half, base, weights, state, update):
    planes = gathered.shape[0] // 16
    for g in range(8):
        first = 2 * planes * g
        source[pl.ds(g, planes, stride=8), :] = gathered[pl.ds(first, planes, stride=2), :]
        half[pl.ds(g, planes, stride=8), :] = gathered[pl.ds(first + 1, planes, stride=2), :]
    lane, sub = (lanes_of(8), rows_of(8))
    in_left, in_right = ((lane & 15) > 0, (lane & 15) < 15)
    in_before = (lane >= 16) | (sub > 0)
    in_after = (lane < LANES - 16) | (sub < 7)
    zero = jnp.zeros((8, LANES), jnp.float32)
    first_gain = cheb_weights(COARSE_ITERS, 0.02, 2.0)[1][0]
    for buffer in range(2):
        state[buffer, 0, :, :] = zero
        state[buffer, planes + 1, :, :] = zero

    def at(ref, p):
        return ref[8 * p : 8 * p + 8, :]

    for p in range(planes):
        center = at(half, p)
        low = at(half, p - 1) if p else zero
        high = at(half, p + 1) if p < planes - 1 else zero
        neighbours = (
            (low, None),
            (high, None),
            (before_z(center), in_before),
            (after_z(center), in_after),
            (roll(center, 1), in_left),
            (roll(center, -1), in_right),
        )
        faces = [center + (value if mask is None else jnp.where(mask, value, 0.0)) for value, mask in neighbours]
        diagonal = faces[0] + faces[1] + faces[2] + faces[3] + faces[4] + faces[5]
        inverse = 1.0 / diagonal
        for which, (face, (_, mask)) in enumerate(zip(faces, neighbours)):
            scaled = face * inverse
            base[which, p, :, :] = scaled if mask is None else jnp.where(mask, scaled, 0.0)
        scaled = 64.0 * (at(source, p) * inverse)
        base[6, p, :, :] = scaled
        start = first_gain * scaled
        update[p, :, :] = start
        state[0, p + 1, :, :] = start

    def step(index, old, new):
        carry, gain = (weights[index, 0], weights[index, 1])
        before, center = (zero, state[old, 1, :, :])
        for p in range(planes):
            after = state[old, p + 2, :, :]
            beside = base[0, p, :, :] * before + base[1, p, :, :] * after
            beside = beside + (base[2, p, :, :] * before_z(center) + base[3, p, :, :] * after_z(center))
            beside = beside + (base[4, p, :, :] * roll(center, 1) + base[5, p, :, :] * roll(center, -1))
            change = carry * update[p, :, :] + gain * (base[6, p, :, :] - center + beside)
            update[p, :, :] = change
            state[new, p + 1, :, :] = center + change
            before, center = (center, after)

    def two_steps(pair, unused):
        step(2 * pair + 1, 0, 1)
        step(2 * pair + 2, 1, 0)
        return unused

    lax.fori_loop(0, (COARSE_ITERS - 1) // 2, two_steps, 0)
    step(COARSE_ITERS - 1, 0, 1)
    return 1


def finish(cells, pos, weights, gathered, prev2, next2, s2, h2, g2, s1, h1, g1, s0, h0, g0, out, *scratch):
    gx, gz = (pos[0], pos[1])
    source3, half3, base, state, update3, coarse2, temp = scratch[:7]
    f2, f1, f0 = (scratch[7:16], scratch[16:25], scratch[25:34])
    planes3 = gathered.shape[0] // 16
    last = solve_coarsest(gathered, source3, half3, base, weights, state, update3)

    bx2, bz2 = (2, s2.shape[1] - 32)
    rows = bz2 + 8
    cell = lax.broadcasted_iota(jnp.int32, (LANES, LANES), 0)
    lane = lax.broadcasted_iota(jnp.int32, (LANES, LANES), 1)
    pick = jnp.where((cell & 15) == (lane >> 3), 1.0, 0.0)
    z3 = (rows_of(rows) >> 1) - 2
    keep = (lanes_of(rows) >> 4) == (z3 & 7)
    sub = rows_of(8)
    for q in range(5):
        plane = gx + q - 2
        inside = jnp.logical_and(plane >= 0, plane < planes3)
        value = state[last, pl.ds(jnp.clip(plane, -1, planes3) + 1, 1), :, :][0]
        picked = [jnp.sum(jnp.where(sub == gz + d, value, 0.0), axis=0, keepdims=True) for d in (-1, 0, 1)]
        wide = jnp.where(z3 < 0, picked[0], jnp.where(z3 < 8, picked[1], picked[2]))
        coarse2[q * rows : (q + 1) * rows, :] = jnp.where(keep, wide, 0.0)
    spread_out = jnp.dot(coarse2[...], pick, precision=lax.Precision.HIGHEST, preferred_element_type=jnp.float32)
    coarse2[...] = spread_out

    start, middle, update = f2[6:9]
    own = 4
    row, count = (ROW - 4, rows)
    zero = jnp.zeros((8, LANES), jnp.float32)
    for q in range(5):
        for p in (own - 4 + 2 * q, own - 3 + 2 * q):
            start[p, 8:16, :] = zero
            start[p, ROW + bz2 : ROW + bz2 + 8, :] = zero
            if q == 2:
                guess = g2[p, row : row + count, :]
            else:
                guess = spread((prev2 if q < 2 else next2)[4 : 4 + count, :], p if q < 2 else p - own - bx2)
            start[p, row : row + count, :] = guess + coarse2[q * rows : (q + 1) * rows, :]
    level = Level(2, gx, gz, (bx2, bz2), cells[2], own, (h2,) + tuple(f2[0:6]))
    level.coefs(range(own - 3, own + 5), row, count)

    bx1, bz1 = (4, s1.shape[1] - 32)
    start1, middle1, update1 = f1[6:9]

    def to_level_1(p, value):
        q = 2 * (p - own) + 4
        temp[pl.ds(0, value.shape[0], stride=2), :] = value
        temp[pl.ds(1, value.shape[0], stride=2), :] = value
        for r in (q, q + 1):
            if 1 <= r <= 10:
                start1[r, ROW - 4 : ROW + bz1 + 4, :] = (
                    g1[r, ROW - 4 : ROW + bz1 + 4, :] + temp[0 : bz1 + 8, :]
                )

    for r in range(1, 11):
        start1[r, 8:16, :] = zero
        start1[r, ROW + bz1 : ROW + bz1 + 8, :] = zero
    level.up(s2, start, middle, update, to_level_1, range(own - 2, own + 4), row, count, ROW - 2, bz2 + 4)
    level = Level(1, gx, gz, (bx1, bz1), cells[1], 4, (h1,) + tuple(f1[0:6]))
    row, count = (ROW - 4, bz1 + 8)
    level.coefs(range(2, 10), row, count)

    bx0, bz0 = (out.shape[0], out.shape[1])
    start0, middle0, update0 = f0[6:9]
    for r in range(2, 14):
        start0[r, 8:16, :] = zero
        start0[r, ROW + bz0 : ROW + bz0 + 8, :] = zero

    def to_level_0(p, value):
        q = 2 * (p - 4) + 4
        temp[pl.ds(0, value.shape[0], stride=2), :] = value
        temp[pl.ds(1, value.shape[0], stride=2), :] = value
        for r in (q, q + 1):
            start0[r, ROW - 4 : ROW + bz0 + 4, :] = g0[r, ROW - 4 : ROW + bz0 + 4, :] + temp[0 : bz0 + 8, :]

    level.up(s1, start1, middle1, update1, to_level_0, range(3, 9), row, count, ROW - 2, bz1 + 4)
    level = Level(0, gx, gz, (bx0, bz0), cells[0], 4, (h0,) + tuple(f0[0:6]))
    level.coefs(range(3, 13), ROW - 4, bz0 + 8)

    def to_out(p, value):
        out[p - 4, :, :] = value

    level.up(s0, start0, middle0, update0, to_out, range(4, 12), ROW - 4, bz0 + 8, ROW, bz0)


def f32(*shape):
    return jax.ShapeDtypeStruct(shape, jnp.float32)


def scratch(*shape):
    return pltpu.VMEM(shape, jnp.float32)


def call(kernel, name, outs, scratches, scalars, *args):
    smem = pl.BlockSpec(memory_space=pltpu.SMEM)
    vmem = pl.BlockSpec(memory_space=pltpu.VMEM)
    return pl.pallas_call(
        kernel,
        name=name,
        out_shape=outs,
        in_specs=[smem] * scalars + [vmem] * (len(args) - scalars),
        out_specs=[vmem] * len(outs),
        scratch_shapes=scratches,
        compiler_params=pltpu.CompilerParams(vmem_limit_bytes=VMEM_LIMIT),
    )(*args)


def shift(array, axis, by):
    devices = lax.axis_size(axis)
    return lax.ppermute(array, axis, [(i, i + by) for i in range(devices) if 0 <= i + by < devices])


def turn(array, axis, by):
    devices = lax.axis_size(axis)
    return lax.ppermute(array, axis, [(i, (i + by) % devices) for i in range(devices)])


def on_device(right_side, conductivity):
    nx, nz = (lax.axis_size("gx"), lax.axis_size("gz"))
    bx, bz = right_side.shape[0:2]
    cells = [(nx * bx >> level, nz * bz >> level) for level in range(4)]
    pos = jnp.stack([lax.axis_index("gx"), lax.axis_index("gz")]).astype(jnp.int32)
    weights = jnp.asarray(list(zip(*cheb_weights(COARSE_ITERS, 0.02, 2.0))), jnp.float32)

    low = shift(jnp.concatenate([right_side[bx - 3 :], conductivity[bx - 4 :]]), "gx", 1)
    high = shift(jnp.concatenate([right_side[:3], conductivity[:4]]), "gx", -1)
    planes = bx + 8
    to_high, to_low = call(
        edge_rows_0, "edge_rows_0", [f32(planes, 8, LANES)] * 2, [], 0, right_side, conductivity, low, high
    )
    z_low, z_high = (turn(to_high, "gz", 1), turn(to_low, "gz", -1))
    window = (planes, bz + 32, LANES)
    s0, h0, g0, brick1 = call(
        functools.partial(down_0, cells[0]),
        "down_0",
        [f32(*window)] * 3 + [f32(bx, bz // 2, LANES)],
        [scratch(*window)] * 7 + [scratch(bz + 16, LANES), scratch(bx // 2 + 2, bz // 2 + 8, LANES)],
        1,
        pos,
        right_side,
        conductivity,
        low,
        high,
        z_low,
        z_high,
    )

    low, high = (shift(brick1, "gx", 1), shift(brick1, "gx", -1))
    to_high, to_low = call(edge_rows, "edge_rows_1", [f32(3 * bx, 8, LANES)] * 2, [], 0, low, brick1, high)
    z_low, z_high = (turn(to_high, "gz", 1), turn(to_low, "gz", -1))
    bx, bz = (bx // 2, bz // 2)
    window1 = (3 * bx, bz + 32, LANES)
    s1, h1, g1, for_next, for_prev = call(
        functools.partial(down_1, cells[1]),
        "down_1",
        [f32(*window1)] * 3 + [f32(bx // 2 + 2, bz // 2, LANES)] * 2,
        [scratch(*window1)] * 7 + [scratch(bz + 16, LANES), scratch(bx // 2 + 4, bz // 2 + 8, LANES)],
        1,
        pos,
        brick1,
        low,
        high,
        z_low,
        z_high,
    )

    bx, bz = (bx // 2, bz // 2)
    bricks = [shift(for_next, "gx", 1), for_next, shift(for_prev, "gx", -1)]
    to_high, to_low = call(edge_rows_2, "edge_rows_2", [f32(3 * bx + 4, 8, LANES)] * 2, [], 0, *bricks)
    z_low, z_high = (turn(to_high, "gz", 1), turn(to_low, "gz", -1))
    window2 = (3 * bx + 4, bz + 32, LANES)
    s2, h2, g2, brick3, for_next, for_prev = call(
        functools.partial(down_2, cells[2]),
        "down_2",
        [f32(*window2)] * 3 + [f32(2, LANES)] + [f32(bz + 16, LANES)] * 2,
        [scratch(*window2)] * 7 + [scratch(bz + 16, LANES)],
        1,
        pos,
        *bricks,
        z_low,
        z_high,
    )

    prev2, next2 = (shift(for_next, "gx", 1), shift(for_prev, "gx", -1))

    everywhere = lax.all_to_all(jnp.broadcast_to(brick3[None], (nx, 2, LANES)), "gx", 0, 0, tiled=True)
    gathered = lax.all_gather(everywhere, "gz", axis=0).reshape(nz * 2 * nx, LANES)
    work = (
        [scratch(8 * nx, LANES)] * 2
        + [scratch(7, nx, 8, LANES), scratch(2, nx + 2, 8, LANES), scratch(nx, 8, LANES)]
        + [scratch(5 * (bz + 8), LANES), scratch(96, LANES)]
        + [scratch(*window2)] * 9
        + [scratch(*window1)] * 9
        + [scratch(*window)] * 9
    )
    (result,) = call(
        functools.partial(finish, cells), "finish", [f32(*right_side.shape)], work, 2, pos, weights, gathered,
        prev2, next2, s2, h2, g2, s1, h1, g1, s0, h0, g0,
    )
    return result


def solution(mesh):
    return jax.shard_map(
        on_device,
        mesh=mesh,
        in_specs=(P("gx", "gz", None), P("gx", "gz", None)),
        out_specs=P("gx", "gz", None),
        check_vma=False,
    )
```

```python
import functools
import math

import jax
import jax.numpy as jnp
from jax import lax
from jax.experimental import pallas as pl
from jax.experimental.pallas import tpu as pltpu
from jax.sharding import PartitionSpec as P

COARSE_ITERS = 20
LANES = 128
ROW = 16
SOLVE = (8, 16)


def cheb_weights(count, lower, upper):
    theta = 0.5 * (upper + lower)
    delta = 0.5 * (upper - lower)
    sigma = theta / delta
    rho_prev = 1.0 / sigma
    carry_terms = [0.0]
    gain_terms = [1.0 / theta]
    for step in range(1, count):
        rho_next = 1.0 / (2.0 * sigma - rho_prev)
        carry_terms.append(rho_next * rho_prev)
        gain_terms.append(2.0 * rho_next / delta)
        rho_prev = rho_next
    return (carry_terms, gain_terms)


(_, CARRY), (GAIN_FIRST, GAIN) = cheb_weights(2, 0.25, 2.0)


def lanes_of(rows):
    return lax.broadcasted_iota(jnp.int32, (rows, LANES), 1)


def rows_of(rows):
    return lax.broadcasted_iota(jnp.int32, (rows, LANES), 0)


def roll(value, shift, axis=1):
    return pltpu.roll(value, shift % value.shape[axis], axis)


def pair_sum(value, stride):
    odd = (lanes_of(value.shape[0]) & stride) != 0
    return value + jnp.where(odd, roll(value, stride), roll(value, -stride))


class View:
    def __init__(self, ref, plane, row):
        self.ref, self.plane, self.row = (ref, plane, row)

    def __getitem__(self, index):
        plane, rows, lanes = index
        return self.ref[plane - self.plane, rows.start - self.row : rows.stop - self.row, lanes]


class Level:
    def __init__(self, level, gx, gz, brick, cells, first_plane, refs, first_row=ROW):
        self.stride, self.scale, self.first_row = (2**level, 0.25**level, first_row)
        self.gx, self.gz, self.brick, self.cells, self.first_plane = (gx, gz, brick, cells, first_plane)
        self.half, self.fx, self.fz, self.left, self.right, self.diag, self.inverse = refs

    def coefs(self, planes, row, count):
        half, stride = (self.half, self.stride)
        lane = lanes_of(count)
        here = rows_of(count) + (row - self.first_row + self.gz * self.brick[1])
        first, last = (planes[0], planes[-1])
        for p in planes:
            self.fx[p, row : row + count, :] = half[p - 1, row : row + count, :] + half[p, row : row + count, :]
        p = last + 1
        self.fx[p, row : row + count, :] = half[p - 1, row : row + count, :] + half[p, row : row + count, :]
        more = count + 1
        for p in planes:
            self.fz[p, row : row + more, :] = half[p, row - 1 : row - 1 + more, :] + half[p, row : row + more, :]
        for p in planes:
            center = half[p, row : row + count, :]
            face_left = center + jnp.where(lane >= stride, roll(center, stride), 0.0)
            face_right = center + jnp.where(lane < LANES - stride, roll(center, -stride), 0.0)
            diagonal = (
                self.fx[p, row : row + count, :]
                + self.fx[p + 1, row : row + count, :]
                + self.fz[p, row : row + count, :]
                + self.fz[p, row + 1 : row + 1 + count, :]
                + face_left
                + face_right
            )
            self.left[p, row : row + count, :] = jnp.where(lane >= stride, face_left, 0.0)
            self.right[p, row : row + count, :] = jnp.where(lane < LANES - stride, face_right, 0.0)
            self.diag[p, row : row + count, :] = diagonal
            plane = p - self.first_plane + self.gx * self.brick[0]
            outside = jnp.where(jnp.logical_and(plane >= 0, plane < self.cells[0]), 0, 1 << 20)
            index = here + outside
            inside = (index >= 0) & (index < self.cells[1]) & (diagonal > 0.0)
            self.inverse[p, row : row + count, :] = jnp.where(inside, 1.0 / (self.scale * diagonal), 0.0)

    def remainder(self, source, guess, p, row, count):
        center = guess[p, row : row + count, :]
        beside = (
            self.fx[p, row : row + count, :] * guess[p - 1, row : row + count, :]
            + self.fx[p + 1, row : row + count, :] * guess[p + 1, row : row + count, :]
        )
        beside = beside + (
            self.fz[p, row : row + count, :] * guess[p, row - 1 : row - 1 + count, :]
            + self.fz[p, row + 1 : row + 1 + count, :] * guess[p, row + 1 : row + 1 + count, :]
        )
        beside = beside + (
            self.left[p, row : row + count, :] * roll(center, self.stride)
            + self.right[p, row : row + count, :] * roll(center, -self.stride)
        )
        applied = self.diag[p, row : row + count, :] * center - beside
        return source[p, row : row + count, :] - self.scale * applied

    def second_down(self, source, first, out, planes, row, count):
        for p in planes:
            rest = self.remainder(source, first, p, row, count)
            start = first[p, row : row + count, :]
            update = CARRY * start + GAIN * (self.inverse[p, row : row + count, :] * rest)
            out[p, row : row + count, :] = start + update

    def first_down(self, source, first, planes, row, count):
        for p in planes:
            first[p, row : row + count, :] = GAIN_FIRST * (
                self.inverse[p, row : row + count, :] * source[p, row : row + count, :]
            )

    def restricted_remainder(self, source, guess, temp, planes, row, rows):
        parts = []
        for p in planes[::2]:
            both = self.remainder(source, guess, p, row, rows) + self.remainder(source, guess, p + 1, row, rows)
            temp[0:rows, :] = pair_sum(both, self.stride)
            parts.append(0.125 * (temp[pl.ds(0, rows // 2, stride=2), :] + temp[pl.ds(1, rows // 2, stride=2), :]))
        return parts

    def up(self, source, start, middle, update, out, planes, row, count, out_row, out_count):
        for p in range(planes[0] - 1, planes[-1] + 2):
            first = GAIN_FIRST * (
                self.inverse[p, row : row + count, :] * self.remainder(source, start, p, row, count)
            )
            update[p, row : row + count, :] = first
            middle[p, row : row + count, :] = start[p, row : row + count, :] + first
        for p in planes:
            second = CARRY * update[p, out_row : out_row + out_count, :] + GAIN * (
                self.inverse[p, out_row : out_row + out_count, :]
                * self.remainder(source, middle, p, out_row, out_count)
            )
            out(p, middle[p, out_row : out_row + out_count, :] + second)


def restricted(half, temp, stride, planes, row, rows):
    parts = []
    for p in planes[::2]:
        both = half[p, row : row + rows, :] + half[p + 1, row : row + rows, :]
        temp[0:rows, :] = pair_sum(both, stride)
        parts.append(0.125 * (temp[pl.ds(0, rows // 2, stride=2), :] + temp[pl.ds(1, rows // 2, stride=2), :]))
    return parts


def first_iterate(source, half, p, count, level, stride):
    center = half[p][1 : 1 + count]
    lane = lanes_of(count)
    diagonal = 6.0 * center + half[p - 1][1 : 1 + count] + half[p + 1][1 : 1 + count]
    diagonal = diagonal + half[p][0:count] + half[p][2 : 2 + count]
    diagonal = diagonal + jnp.where(lane >= stride, roll(center, stride), 0.0)
    diagonal = diagonal + jnp.where(lane < LANES - stride, roll(center, -stride), 0.0)
    inverse = jnp.where(diagonal > 0.0, 1.0 / (0.25**level * diagonal), 0.0)
    return GAIN_FIRST * source * inverse


def keep_window(out, window, first_plane, first_row):
    planes, rows = out.shape[0:2]
    out[...] = window[first_plane : first_plane + planes, first_row : first_row + rows, :]


def cut(half_ref, planes, row, count):
    return [half_ref[p, row : row + count, :] for p in planes]


def edge_rows_0(source, cond, low, high, to_high, to_low):
    bx, bz = source.shape[0:2]
    zero = jnp.zeros((4, LANES), jnp.float32)
    for rows, out in ((slice(bz - 4, bz), to_high), (slice(0, 4), to_low)):
        out[0, 0:4, :] = zero
        out[bx + 7, 0:4, :] = zero
        for p in range(3):
            out[p + 1, 0:4, :] = low[p, rows, :]
            out[p + bx + 4, 0:4, :] = high[p, rows, :]
        for p in range(4):
            out[p, 4:8, :] = low[p + 3, rows, :]
            out[p + bx + 4, 4:8, :] = high[p + 3, rows, :]
        for p in range(bx):
            out[p + 4, 0:4, :] = source[p, rows, :]
            out[p + 4, 4:8, :] = cond[p, rows, :]


def down_0(cells, pos, source, cond, low, high, z_low, z_high, kept_s, kept_h, kept_g, to_next, to_prev, win_s, win_h, guess, fx, fz, left, right, diag, inverse, first, temp, next_half):
    gx, gz = (pos[0], pos[1])
    bx, bz = source.shape[0:2]
    planes = bx + 8
    zero = jnp.zeros((8, LANES), jnp.float32)
    end = ROW + bz
    has_low, has_high = inside_z(gz, cells[1] // bz)
    for p in range(planes):
        for edge in (8, end, end + 8):
            win_s[p, edge : edge + 8, :] = zero
            win_h[p, edge : edge + 8, :] = zero
            guess[p, edge : edge + 8, :] = zero
            first[p, edge : edge + 8, :] = zero
        win_s[p, ROW - 4 : ROW, :] = z_low[p, 0:4, :]
        win_s[p, end : end + 4, :] = z_high[p, 0:4, :]
        win_h[p, ROW - 4 : ROW, :] = (0.5 * has_low) * z_low[p, 4:8, :]
        win_h[p, end : end + 4, :] = (0.5 * has_high) * z_high[p, 4:8, :]
    for p in range(bx):
        win_s[p + 4, ROW:end, :] = source[p, :, :]
        win_h[p + 4, ROW:end, :] = 0.5 * cond[p, :, :]
    for p in range(3):
        win_s[p + 1, ROW:end, :] = low[p, :, :]
        win_s[p + bx + 4, ROW:end, :] = high[p, :, :]
    for p in range(4):
        win_h[p, ROW:end, :] = 0.5 * low[p + 3, :, :]
        win_h[p + bx + 4, ROW:end, :] = 0.5 * high[p + 3, :, :]

    level = Level(0, gx, gz, (bx, bz), cells, 4, (win_h, fx, fz, left, right, diag, inverse))
    row, count = (ROW - 4, bz + 8)
    level.coefs(range(1, planes - 1), row, count)
    level.first_down(win_s, first, range(1, planes - 1), row, count)
    level.second_down(win_s, first, guess, range(2, planes - 2), row, count)
    sources = level.restricted_remainder(win_s, guess, temp, range(4, 4 + bx), ROW, bz)
    halves = restricted(win_h, temp, 1, range(2, planes - 2), ROW - 8, bz + 16)
    for p, value in enumerate(halves):
        next_half[p, :, :] = value
    own = bz // 2
    odd = (lanes_of(own) & 1) == 1
    padded = cut(next_half, range(bx // 2 + 2), 3, own + 2)
    for p, value in enumerate(sources):
        mixed = jnp.where(odd, padded[p + 1][1 : 1 + own], value)
        to_next[p, :, :] = mixed
        to_prev[p, :, :] = mixed
    end = bx // 2 - 1
    to_next[end + 1, :, :] = first_iterate(sources[0], padded, 1, own, 1, 2)
    to_prev[end + 1, :, :] = first_iterate(sources[end], padded, end + 1, own, 1, 2)
    keep_window(kept_s, win_s, 3, 8)
    keep_window(kept_h, win_h, 2, 8)
    keep_window(kept_g, guess, 2, 8)


def inside_z(gz, count):
    return (jnp.where(gz > 0, 1.0, 0.0), jnp.where(gz < count - 1, 1.0, 0.0))


def edge_rows_1(low, here, high, to_high, to_low):
    at = 0
    for part, count in ((low, low.shape[0]), (here, here.shape[0] - 1), (high, high.shape[0])):
        rows = part.shape[1]
        to_high[at : at + count, :, :] = part[0:count, rows - 16 : rows, :]
        to_low[at : at + count, :, :] = part[0:count, 0:16, :]
        at += count


def down_1(cells, pos, here, low, high, z_low, z_high, kept_s, kept_h, kept_g, to_next, to_prev, win_s, win_h, guess, fx, fz, left, right, diag, inverse, first, temp, next_source, next_half):
    gx, gz = (pos[0], pos[1])
    bx, bz = (here.shape[0] - 1, here.shape[1])
    planes, base = (3 * bx, 24)
    end = base + bz
    zero = jnp.zeros((8, LANES), jnp.float32)
    has_low, has_high = inside_z(gz, cells[1] // bz)

    def unpack(p, start, rows, mixed):
        odd = (lanes_of(rows) & 1) == 1
        win_s[p, start : start + rows, :] = jnp.where(odd, roll(mixed, 1), mixed)
        win_h[p, start : start + rows, :] = jnp.where(odd, mixed, roll(mixed, -1))

    edges = 0
    for b, part in enumerate((low, here, high)):
        for p in range(bx):
            unpack(b * bx + p, base, bz, part[p, :, :])
            unpack(b * bx + p, base - 16, 16, has_low * z_low[edges + p, :, :])
            unpack(b * bx + p, end, 16, has_high * z_high[edges + p, :, :])
        edges += bx
        if b != 1:
            q = 0 if b == 0 else planes - 1
            first[q, base:end, :] = part[bx, :, :]
            first[q, base - 16 : base, :] = has_low * z_low[edges, :, :]
            first[q, end : end + 16, :] = has_high * z_high[edges, :, :]
            edges += 1
    for p in range(planes):
        for ref in (win_s, win_h):
            ref[p, 0:8, :] = zero
            ref[p, end + 16 : end + 24, :] = zero
        for ref in (first, guess):
            ref[p, 8:16, :] = zero if 0 < p < planes - 1 or ref is guess else ref[p, 8:16, :]
            ref[p, end + 8 : end + 16, :] = zero if 0 < p < planes - 1 or ref is guess else ref[p, end + 8 : end + 16, :]

    level = Level(1, gx, gz, (bx, bz), cells, bx, (win_h, fx, fz, left, right, diag, inverse), base)
    row, count = (base - 12, bz + 24)
    level.coefs(range(1, planes - 1), row, count)
    level.first_down(win_s, first, range(1, planes - 1), row, count)
    level.second_down(win_s, first, guess, range(1, planes - 1), row, count)
    own = bz // 2
    sources = level.restricted_remainder(win_s, guess, temp, range(bx - 2, 2 * bx + 2), row, count)
    halves = restricted(win_h, temp, 2, range(planes), base - 16, bz + 32)
    next_source[...] = jnp.zeros(next_source.shape, jnp.float32)
    for p, value in enumerate(sources):
        next_source[p + 1, 2 : 2 + count // 2, :] = value
    for p, value in enumerate(halves):
        next_half[p, :, :] = value
    lane = lanes_of(own + 16) & 3

    def pair(p):
        mixed = jnp.where(lane == 0, next_source[p, :, :], next_half[p, :, :])
        mixed = jnp.where(lane == 2, next_source[p + 1, :, :], mixed)
        return jnp.where(lane == 3, next_half[p + 1, :, :], mixed)

    middle = pair(2)
    to_next[0, :, :] = pair(0)
    to_next[1, :, :] = middle
    to_prev[0, :, :] = middle
    to_prev[1, :, :] = pair(4)
    keep_window(kept_s, win_s, 2, base - 8)
    keep_window(kept_h, win_h, 1, base - 8)
    keep_window(kept_g, guess, 1, base - 8)


def spread(mixed, which):
    only = jnp.where((lanes_of(mixed.shape[0]) & 3) == which, mixed, 0.0)
    only = roll(only, -which) if which else only
    twice = only + roll(only, 1)
    return twice + roll(twice, 2)


def down_2(cells, pos, prev, here, next_, kept_s, kept_h, kept_g, message, to_next, to_prev, win_s, win_h, guess, fx, fz, left, right, diag, inverse, first, temp):
    gx, gz = (pos[0], pos[1])
    bx, bz = (2, prev.shape[1] - 16)
    own, planes = (4, 10)
    end = ROW + bz
    zero = jnp.zeros((8, LANES), jnp.float32)
    pairs = (prev, 0), (prev, 1), (here, 1), (next_, 0), (next_, 1)
    for q, (part, at) in enumerate(pairs):
        mixed = part[at, :, :]
        for p in range(2):
            win_s[2 * q + p, 8 : end + 8, :] = spread(mixed, 2 * p)
            win_h[2 * q + p, 8 : end + 8, :] = spread(mixed, 2 * p + 1)
    for p in range(planes):
        for ref in (win_s, win_h, first):
            ref[p, 0:8, :] = zero
            ref[p, end + 8 : end + 16, :] = zero
    level = Level(2, gx, gz, (bx, bz), cells, own, (win_h, fx, fz, left, right, diag, inverse))
    row, count = (ROW - 8, bz + 16)
    level.coefs(range(own - 3, own + 5), row, count)
    level.first_down(win_s, first, range(own - 3, own + 5), row, count)
    level.second_down(win_s, first, guess, range(own - 2, own + 4), row, count)
    keep_window(kept_s, win_s, 1, 8)
    keep_window(kept_h, win_h, 0, 8)
    keep_window(kept_g, guess, own, 8)
    lane = lanes_of(count) & 3
    for out, begin in ((to_next, own - 2), (to_prev, own)):
        mixed = guess[begin, row : row + count, :]
        for p in range(1, 4):
            mixed = jnp.where(lane == p, guess[begin + p, row : row + count, :], mixed)
        out[...] = mixed
    sources = level.restricted_remainder(win_s, guess, temp, range(own, own + bx), ROW, bz)
    halves = restricted(win_h, temp, 4, range(own, own + bx), ROW, bz)
    rows = bz // 2
    cell = lax.broadcasted_iota(jnp.int32, (LANES, LANES), 0)
    lane = lax.broadcasted_iota(jnp.int32, (LANES, LANES), 1)
    pick = jnp.where(((cell >> 3) == (lane & 15)) & ((cell & 7) == 0), 1.0, 0.0)
    keep = (lanes_of(rows) >> 4) == rows_of(rows)
    for at, value in enumerate((sources[0], halves[0])):
        dense = jnp.dot(value, pick, precision=lax.Precision.HIGHEST, preferred_element_type=jnp.float32)
        dense = jnp.sum(jnp.where(keep, dense, 0.0), axis=0, keepdims=True)
        for device in range(message.shape[0]):
            message[device, at : at + 1, :] = dense


class Coarsest:
    def __init__(self, base, state, update):
        self.base, self.state, self.update, self.now = (base, state, update, 0)
        self.planes = update.shape[1]
        self.weights = list(zip(*cheb_weights(COARSE_ITERS, 0.02, 2.0)))
        zero = jnp.zeros((8, LANES), jnp.float32)
        for buffer in range(2):
            for b in range(3):
                state[buffer, b, 0:8, :] = zero
                state[buffer, b, self.planes + 8 : self.planes + 16, :] = zero

    def beside_z(self, values):
        lane = lanes_of(values[0].shape[0])
        ahead, back = ([roll(v, 16) for v in values], [roll(v, -16) for v in values])
        before = [jnp.where(lane < 16, ahead[max(b - 1, 0)], ahead[b]) for b in range(3)]
        after = [jnp.where(lane >= LANES - 16, back[min(b + 1, 2)], back[b]) for b in range(3)]
        return before, after

    def start(self, parts, half, flags):
        planes, zero = (self.planes, jnp.zeros((8, LANES), jnp.float32))
        gain = self.weights[0][1]
        for b in range(3):
            half[b, 0:8, :] = zero
            half[b, planes + 8 : planes + 16, :] = zero
            half[b, 8 : planes + 8, :] = flags[b] * parts[b][pl.ds(1, planes, stride=2), :]
        lane = lanes_of(8)
        in_left, in_right = ((lane & 15) > 0, (lane & 15) < 15)
        for x in range(0, planes, 8):
            centers = [half[b, x + 8 : x + 16, :] for b in range(3)]
            before, after = self.beside_z(centers)
            for b, center in enumerate(centers):
                faces = [
                    center + half[b, x + 7 : x + 15, :],
                    center + half[b, x + 9 : x + 17, :],
                    center + before[b],
                    center + after[b],
                    center + jnp.where(in_left, roll(center, 1), 0.0),
                    center + jnp.where(in_right, roll(center, -1), 0.0),
                ]
                diagonal = faces[0] + faces[1] + faces[2] + faces[3] + faces[4] + faces[5]
                inverse = flags[b] * jnp.where(diagonal > 0.0, 1.0 / diagonal, 0.0)
                faces = [face * inverse for face in faces]
                faces[4] = jnp.where(in_left, faces[4], 0.0)
                faces[5] = jnp.where(in_right, faces[5], 0.0)
                for which, face in enumerate(faces):
                    self.base[7 * b + which, x : x + 8, :] = face
                scaled = 64.0 * (parts[b][pl.ds(2 * x, 8, stride=2), :] * inverse)
                self.base[7 * b + 6, x : x + 8, :] = scaled
                self.update[b, x : x + 8, :] = gain * scaled
                self.state[self.now, b, x + 8 : x + 16, :] = gain * scaled

    def resume(self, parts, flags):
        for b in range(3):
            self.state[self.now, b, 8 : self.planes + 8, :] = flags[b] * parts[b][0, :, :]
            self.update[b, :, :] = flags[b] * parts[b][1, :, :]

    def steps(self, which):
        for index in which:
            carry, gain = self.weights[index]
            old, new = (self.now, 1 - self.now)
            for x in range(0, self.planes, 8):
                centers = [self.state[old, b, x + 8 : x + 16, :] for b in range(3)]
                before, after = self.beside_z(centers)
                for b, center in enumerate(centers):
                    face = [self.base[7 * b + k, x : x + 8, :] for k in range(7)]
                    beside = face[0] * self.state[old, b, x + 7 : x + 15, :] + face[1] * self.state[old, b, x + 9 : x + 17, :]
                    beside = beside + (face[2] * before[b] + face[3] * after[b])
                    beside = beside + (face[4] * roll(center, 1) + face[5] * roll(center, -1))
                    change = carry * self.update[b, x : x + 8, :] + gain * (face[6] - center + beside)
                    self.update[b, x : x + 8, :] = change
                    self.state[new, b, x + 8 : x + 16, :] = center + change
            self.now = new

    def leave(self, out):
        out[0, :, :] = self.state[self.now, 1, 8 : self.planes + 8, :]
        out[1, :, :] = self.update[1, :, :]


def solve_first(count, pos, low, here, high, base, out, half, state, update):
    has_low, has_high = inside_z(pos[1], count)
    level = Coarsest(base, state, update)
    level.start((low, here, high), half, (has_low, 1.0, has_high))
    level.steps(range(1, SOLVE[0]))
    level.leave(out)


def solve_next(count, pos, base, low, here, high, out, state, update):
    has_low, has_high = inside_z(pos[1], count)
    level = Coarsest(base, state, update)
    level.resume((low, here, high), (has_low, 1.0, has_high))
    level.steps(range(SOLVE[0], SOLVE[1]))
    level.leave(out)


def finish(cells, pos, base, low, here, high, prev2, next2, s2, h2, g2, s1, h1, g1, s0, h0, g0, out, *scratch):
    gx, gz = (pos[0], pos[1])
    state, update3, coarse2, temp, start2, start1, start0 = scratch[:7]
    shared, middle, update = (scratch[7:13], scratch[13], scratch[14])
    s2, h2, g2 = (View(s2, 1, 8), View(h2, 0, 8), View(g2, 4, 8))
    s1, h1, g1 = (View(s1, 2, 8), View(h1, 1, 8), View(g1, 1, 8))
    s0, h0, g0 = (View(s0, 3, 8), View(h0, 2, 8), View(g0, 2, 8))
    bz0 = out.shape[1]
    bz1, bz2 = (bz0 // 2, bz0 // 4)
    has_low, has_high = inside_z(gz, cells[0][1] // bz0)
    level = Coarsest(base, state, update3)
    level.resume((low, here, high), (has_low, 1.0, has_high))
    level.steps(range(SOLVE[1], COARSE_ITERS))
    last = level.now

    bx2 = 2
    rows = bz2 + 8
    cell = lax.broadcasted_iota(jnp.int32, (LANES, LANES), 0)
    lane = lax.broadcasted_iota(jnp.int32, (LANES, LANES), 1)
    pick = jnp.where((cell & 15) == (lane >> 3), 1.0, 0.0)
    z3 = (rows_of(rows) >> 1) - 2
    keep = (lanes_of(rows) >> 4) == (z3 & 7)
    columns = [state[last, b, pl.ds(gx + 6, 8), :] for b in range(3)]
    for q in range(5):
        picked = [column[q : q + 1, :] for column in columns]
        wide = jnp.where(z3 < 0, picked[0], jnp.where(z3 < 8, picked[1], picked[2]))
        coarse2[q * rows : (q + 1) * rows, :] = jnp.where(keep, wide, 0.0)
    spread_out = jnp.dot(coarse2[...], pick, precision=lax.Precision.HIGHEST, preferred_element_type=jnp.float32)
    coarse2[...] = spread_out

    start, own = (start2, 4)
    row, count = (ROW - 4, rows)
    zero = jnp.zeros((8, LANES), jnp.float32)
    for q in range(5):
        for p in (own - 4 + 2 * q, own - 3 + 2 * q):
            start[p, 8:16, :] = zero
            start[p, ROW + bz2 : ROW + bz2 + 8, :] = zero
            if q == 2:
                guess = g2[p, row : row + count, :]
            else:
                guess = spread((prev2 if q < 2 else next2)[4 : 4 + count, :], p if q < 2 else p - own - bx2)
            start[p, row : row + count, :] = guess + coarse2[q * rows : (q + 1) * rows, :]
    level = Level(2, gx, gz, (bx2, bz2), cells[2], own, (h2,) + tuple(shared))
    level.coefs(range(own - 3, own + 5), row, count)

    bx1 = 4

    def to_level_1(p, value):
        q = 2 * (p - own) + 4
        temp[pl.ds(0, value.shape[0], stride=2), :] = value
        temp[pl.ds(1, value.shape[0], stride=2), :] = value
        for r in (q, q + 1):
            if 1 <= r <= 10:
                start1[r, ROW - 4 : ROW + bz1 + 4, :] = (
                    g1[r, ROW - 4 : ROW + bz1 + 4, :] + temp[0 : bz1 + 8, :]
                )

    for r in range(1, 11):
        start1[r, 8:16, :] = zero
        start1[r, ROW + bz1 : ROW + bz1 + 8, :] = zero
    level.up(s2, start, middle, update, to_level_1, range(own - 2, own + 4), row, count, ROW - 2, bz2 + 4)
    level = Level(1, gx, gz, (bx1, bz1), cells[1], 4, (h1,) + tuple(shared))
    row, count = (ROW - 4, bz1 + 8)
    level.coefs(range(2, 10), row, count)

    bx0 = out.shape[0]
    for r in range(2, 14):
        start0[r, 8:16, :] = zero
        start0[r, ROW + bz0 : ROW + bz0 + 8, :] = zero

    def to_level_0(p, value):
        q = 2 * (p - 4) + 4
        temp[pl.ds(0, value.shape[0], stride=2), :] = value
        temp[pl.ds(1, value.shape[0], stride=2), :] = value
        for r in (q, q + 1):
            start0[r, ROW - 4 : ROW + bz0 + 4, :] = g0[r, ROW - 4 : ROW + bz0 + 4, :] + temp[0 : bz0 + 8, :]

    level.up(s1, start1, middle, update, to_level_0, range(3, 9), row, count, ROW - 2, bz1 + 4)
    level = Level(0, gx, gz, (bx0, bz0), cells[0], 4, (h0,) + tuple(shared))
    level.coefs(range(3, 13), ROW - 4, bz0 + 8)

    def to_out(p, value):
        out[p - 4, :, :] = value

    level.up(s0, start0, middle, update, to_out, range(4, 12), ROW - 4, bz0 + 8, ROW, bz0)


def f32(*shape):
    return jax.ShapeDtypeStruct(shape, jnp.float32)


def scratch(*shape):
    return pltpu.VMEM(shape, jnp.float32)


def call(kernel, name, outs, scratches, *args):
    smem = pl.BlockSpec(memory_space=pltpu.SMEM)
    limit = 4 * 2**20 + sum(4 * math.prod(ref.shape) for ref in scratches)
    vmem = pl.BlockSpec(memory_space=pltpu.VMEM)
    return pl.pallas_call(
        kernel,
        name=name,
        out_shape=outs,
        in_specs=[smem if arg.dtype == jnp.int32 else vmem for arg in args],
        out_specs=[vmem] * len(outs),
        scratch_shapes=scratches,
        compiler_params=pltpu.CompilerParams(vmem_limit_bytes=limit),
    )(*args)


def shift(array, axis, by):
    devices = lax.axis_size(axis)
    return lax.ppermute(array, axis, [(i, i + by) for i in range(devices) if 0 <= i + by < devices])


def turn(array, axis, by):
    devices = lax.axis_size(axis)
    return lax.ppermute(array, axis, [(i, (i + by) % devices) for i in range(devices)])


def on_device(right_side, conductivity):
    nx, nz = (lax.axis_size("gx"), lax.axis_size("gz"))
    bx, bz = right_side.shape[0:2]
    cells = [(nx * bx >> level, nz * bz >> level) for level in range(4)]
    pos = jnp.stack([lax.axis_index("gx"), lax.axis_index("gz")]).astype(jnp.int32)
    low = shift(jnp.concatenate([right_side[bx - 3 :], conductivity[bx - 4 :]]), "gx", 1)
    high = shift(jnp.concatenate([right_side[:3], conductivity[:4]]), "gx", -1)
    planes = bx + 8
    to_high, to_low = call(
        edge_rows_0, "edge_rows_0", [f32(planes, 8, LANES)] * 2, [], right_side, conductivity, low, high
    )
    z_low, z_high = (turn(to_high, "gz", 1), turn(to_low, "gz", -1))
    window = (planes, bz + 32, LANES)
    s0, h0, g0, for_next, for_prev = call(
        functools.partial(down_0, cells[0]),
        "down_0",
        [f32(bx + 2, bz + 16, LANES)] + [f32(bx + 4, bz + 16, LANES)] * 2 + [f32(bx // 2 + 1, bz // 2, LANES)] * 2,
        [scratch(*window)] * 10 + [scratch(bz + 16, LANES), scratch(bx // 2 + 2, bz // 2 + 8, LANES)],
        pos,
        right_side,
        conductivity,
        low,
        high,
        z_low,
        z_high,
    )

    bx, bz = (bx // 2, bz // 2)
    low, high = (shift(for_next, "gx", 1), shift(for_prev, "gx", -1))
    to_high, to_low = call(
        edge_rows_1, "edge_rows_1", [f32(3 * bx + 2, 16, LANES)] * 2, [], low, for_next, high
    )
    z_low, z_high = (turn(to_high, "gz", 1), turn(to_low, "gz", -1))
    window = (3 * bx, bz + 48, LANES)
    s1, h1, g1, for_next, for_prev = call(
        functools.partial(down_1, cells[1]),
        "down_1",
        [f32(bx + 4, bz + 16, LANES)] + [f32(bx + 6, bz + 16, LANES)] * 2 + [f32(2, bz // 2 + 16, LANES)] * 2,
        [scratch(*window)] * 10 + [scratch(bz + 32, LANES)] + [scratch(bx // 2 + 4, bz // 2 + 16, LANES)] * 2,
        pos,
        for_next,
        low,
        high,
        z_low,
        z_high,
    )

    bx, bz = (bx // 2, bz // 2)
    prev, next_ = (shift(for_next, "gx", 1), shift(for_prev, "gx", -1))
    window = (bx + 8, bz + 32, LANES)
    s2, h2, g2, row3, for_next, for_prev = call(
        functools.partial(down_2, cells[2]),
        "down_2",
        [f32(bx + 6, bz + 16, LANES), f32(bx + 8, bz + 16, LANES), f32(bx, bz + 16, LANES)]
        + [f32(nx, 2, LANES)]
        + [f32(bz + 16, LANES)] * 2,
        [scratch(*window)] * 10 + [scratch(bz + 16, LANES)],
        pos,
        prev,
        for_next,
        next_,
    )

    here = lax.all_to_all(row3, "gx", 0, 0, tiled=True)
    low, high = (turn(here, "gz", 1), turn(here, "gz", -1))
    blocks = [part.reshape(2 * nx, LANES) for part in (low, here, high)]
    solving = [scratch(2, 3, nx + 16, LANES), scratch(3, nx, LANES)]
    for_next, _ = lax.optimization_barrier((for_next, here))
    prev2 = shift(for_next, "gx", 1)
    base, here = call(
        functools.partial(solve_first, nz),
        "solve_first",
        [f32(21, nx, LANES), f32(2, nx, LANES)],
        [scratch(3, nx + 16, LANES)] + solving,
        pos,
        *blocks,
    )
    low, high = (turn(here, "gz", 1), turn(here, "gz", -1))
    for_prev, _ = lax.optimization_barrier((for_prev, here))
    next2 = shift(for_prev, "gx", -1)
    (here,) = call(
        functools.partial(solve_next, nz), "solve_next", [f32(2, nx, LANES)], solving, pos, base, low, here, high
    )
    low, high = (turn(here, "gz", 1), turn(here, "gz", -1))

    bx, bz = right_side.shape[0:2]
    window = (bx + 8, bz + 32, LANES)
    work = solving + [scratch(5 * (bz // 4 + 8), LANES), scratch(bz + 32, LANES)]
    work += [scratch(bx // 4 + 8, bz // 4 + 32, LANES), scratch(bx // 2 + 8, bz // 2 + 32, LANES)]
    work += [scratch(*window)] * 9
    (result,) = call(
        functools.partial(finish, cells), "finish", [f32(*right_side.shape)], work, pos, base, low, here, high,
        prev2, next2, s2, h2, g2, s1, h1, g1, s0, h0, g0,
    )
    return result


def solution(mesh):
    return jax.shard_map(
        on_device,
        mesh=mesh,
        in_specs=(P("gx", "gz", None), P("gx", "gz", None)),
        out_specs=P("gx", "gz", None),
        check_vma=False,
    )
```

```python
import functools
import math

import jax
import jax.numpy as jnp
from jax import lax
from jax.experimental import pallas as pl
from jax.experimental.pallas import tpu as pltpu
from jax.sharding import PartitionSpec as P

COARSE_ITERS = 20
LANES = 128
ROW = 16
SOLVE = (8, 16)


def cheb_weights(count, lower, upper):
    theta = 0.5 * (upper + lower)
    delta = 0.5 * (upper - lower)
    sigma = theta / delta
    rho_prev = 1.0 / sigma
    carry_terms = [0.0]
    gain_terms = [1.0 / theta]
    for step in range(1, count):
        rho_next = 1.0 / (2.0 * sigma - rho_prev)
        carry_terms.append(rho_next * rho_prev)
        gain_terms.append(2.0 * rho_next / delta)
        rho_prev = rho_next
    return (carry_terms, gain_terms)


(_, CARRY), (GAIN_FIRST, GAIN) = cheb_weights(2, 0.25, 2.0)


def lanes_of(rows):
    return lax.broadcasted_iota(jnp.int32, (rows, LANES), 1)


def rows_of(rows):
    return lax.broadcasted_iota(jnp.int32, (rows, LANES), 0)


def roll(value, shift, axis=1):
    return pltpu.roll(value, shift % value.shape[axis], axis)


def pair_sum(value, stride):
    odd = (lanes_of(value.shape[0]) & stride) != 0
    return value + jnp.where(odd, roll(value, stride), roll(value, -stride))


class View:
    def __init__(self, ref, plane, row):
        self.ref, self.plane, self.row = (ref, plane, row)

    def __getitem__(self, index):
        plane, rows, lanes = index
        return self.ref[plane - self.plane, rows.start - self.row : rows.stop - self.row, lanes]


class Level:
    def __init__(self, level, gx, gz, brick, cells, first_plane, refs, first_row=ROW):
        self.stride, self.scale, self.first_row = (2**level, 0.25**level, first_row)
        self.gx, self.gz, self.brick, self.cells, self.first_plane = (gx, gz, brick, cells, first_plane)
        self.half, self.fx, self.fz, self.left, self.right, self.diag, self.inverse = refs

    def coefs(self, planes, row, count):
        half, stride = (self.half, self.stride)
        lane = lanes_of(count)
        here = rows_of(count) + (row - self.first_row + self.gz * self.brick[1])
        first, last = (planes[0], planes[-1])
        for p in planes:
            self.fx[p, row : row + count, :] = half[p - 1, row : row + count, :] + half[p, row : row + count, :]
        p = last + 1
        self.fx[p, row : row + count, :] = half[p - 1, row : row + count, :] + half[p, row : row + count, :]
        more = count + 1
        for p in planes:
            self.fz[p, row : row + more, :] = half[p, row - 1 : row - 1 + more, :] + half[p, row : row + more, :]
        for p in planes:
            center = half[p, row : row + count, :]
            face_left = center + jnp.where(lane >= stride, roll(center, stride), 0.0)
            face_right = center + jnp.where(lane < LANES - stride, roll(center, -stride), 0.0)
            diagonal = (
                self.fx[p, row : row + count, :]
                + self.fx[p + 1, row : row + count, :]
                + self.fz[p, row : row + count, :]
                + self.fz[p, row + 1 : row + 1 + count, :]
                + face_left
                + face_right
            )
            self.left[p, row : row + count, :] = jnp.where(lane >= stride, face_left, 0.0)
            self.right[p, row : row + count, :] = jnp.where(lane < LANES - stride, face_right, 0.0)
            self.diag[p, row : row + count, :] = diagonal
            plane = p - self.first_plane + self.gx * self.brick[0]
            outside = jnp.where(jnp.logical_and(plane >= 0, plane < self.cells[0]), 0, 1 << 20)
            index = here + outside
            inside = (index >= 0) & (index < self.cells[1]) & (diagonal > 0.0)
            self.inverse[p, row : row + count, :] = jnp.where(inside, 1.0 / (self.scale * diagonal), 0.0)

    def remainder(self, source, guess, p, row, count):
        center = guess[p, row : row + count, :]
        beside = (
            self.fx[p, row : row + count, :] * guess[p - 1, row : row + count, :]
            + self.fx[p + 1, row : row + count, :] * guess[p + 1, row : row + count, :]
        )
        beside = beside + (
            self.fz[p, row : row + count, :] * guess[p, row - 1 : row - 1 + count, :]
            + self.fz[p, row + 1 : row + 1 + count, :] * guess[p, row + 1 : row + 1 + count, :]
        )
        beside = beside + (
            self.left[p, row : row + count, :] * roll(center, self.stride)
            + self.right[p, row : row + count, :] * roll(center, -self.stride)
        )
        applied = self.diag[p, row : row + count, :] * center - beside
        return source[p, row : row + count, :] - self.scale * applied

    def second_down(self, source, first, out, planes, row, count):
        for p in planes:
            rest = self.remainder(source, first, p, row, count)
            start = first[p, row : row + count, :]
            update = CARRY * start + GAIN * (self.inverse[p, row : row + count, :] * rest)
            out[p, row : row + count, :] = start + update

    def first_down(self, source, first, planes, row, count):
        for p in planes:
            first[p, row : row + count, :] = GAIN_FIRST * (
                self.inverse[p, row : row + count, :] * source[p, row : row + count, :]
            )

    def restricted_remainder(self, source, guess, temp, planes, row, rows):
        parts = []
        for p in planes[::2]:
            both = self.remainder(source, guess, p, row, rows) + self.remainder(source, guess, p + 1, row, rows)
            temp[0:rows, :] = pair_sum(both, self.stride)
            parts.append(0.125 * (temp[pl.ds(0, rows // 2, stride=2), :] + temp[pl.ds(1, rows // 2, stride=2), :]))
        return parts

    def up(self, source, start, middle, update, out, planes, row, count, out_row, out_count):
        for p in range(planes[0] - 1, planes[-1] + 2):
            first = GAIN_FIRST * (
                self.inverse[p, row : row + count, :] * self.remainder(source, start, p, row, count)
            )
            update[p, row : row + count, :] = first
            middle[p, row : row + count, :] = start[p, row : row + count, :] + first
        for p in planes:
            second = CARRY * update[p, out_row : out_row + out_count, :] + GAIN * (
                self.inverse[p, out_row : out_row + out_count, :]
                * self.remainder(source, middle, p, out_row, out_count)
            )
            out(p, middle[p, out_row : out_row + out_count, :] + second)


def restricted(half, temp, stride, planes, row, rows):
    parts = []
    for p in planes[::2]:
        both = half[p, row : row + rows, :] + half[p + 1, row : row + rows, :]
        temp[0:rows, :] = pair_sum(both, stride)
        parts.append(0.125 * (temp[pl.ds(0, rows // 2, stride=2), :] + temp[pl.ds(1, rows // 2, stride=2), :]))
    return parts


def first_iterate(source, half, p, count, level, stride):
    center = half[p][1 : 1 + count]
    lane = lanes_of(count)
    diagonal = 6.0 * center + half[p - 1][1 : 1 + count] + half[p + 1][1 : 1 + count]
    diagonal = diagonal + half[p][0:count] + half[p][2 : 2 + count]
    diagonal = diagonal + jnp.where(lane >= stride, roll(center, stride), 0.0)
    diagonal = diagonal + jnp.where(lane < LANES - stride, roll(center, -stride), 0.0)
    inverse = jnp.where(diagonal > 0.0, 1.0 / (0.25**level * diagonal), 0.0)
    return GAIN_FIRST * source * inverse


def keep_window(out, window, first_plane, first_row):
    planes, rows = out.shape[0:2]
    out[...] = window[first_plane : first_plane + planes, first_row : first_row + rows, :]


def cut(half_ref, planes, row, count):
    return [half_ref[p, row : row + count, :] for p in planes]


def edge_rows_0(source, cond, low, high, to_high, to_low):
    bx, bz = source.shape[0:2]
    zero = jnp.zeros((4, LANES), jnp.float32)
    for rows, out in ((slice(bz - 4, bz), to_high), (slice(0, 4), to_low)):
        out[0, 0:4, :] = zero
        out[bx + 7, 0:4, :] = zero
        for p in range(3):
            out[p + 1, 0:4, :] = low[p, rows, :]
            out[p + bx + 4, 0:4, :] = high[p, rows, :]
        for p in range(4):
            out[p, 4:8, :] = low[p + 3, rows, :]
            out[p + bx + 4, 4:8, :] = high[p + 3, rows, :]
        for p in range(bx):
            out[p + 4, 0:4, :] = source[p, rows, :]
            out[p + 4, 4:8, :] = cond[p, rows, :]


def down_0(cells, pos, source, cond, low, high, z_low, z_high, kept_s, kept_h, kept_g, to_next, to_prev, win_s, win_h, guess, fx, fz, left, right, diag, inverse, first, temp, next_half):
    gx, gz = (pos[0], pos[1])
    bx, bz = source.shape[0:2]
    planes = bx + 8
    zero = jnp.zeros((8, LANES), jnp.float32)
    end = ROW + bz
    has_low, has_high = inside_z(gz, cells[1] // bz)
    for p in range(planes):
        for edge in (8, end, end + 8):
            win_s[p, edge : edge + 8, :] = zero
            win_h[p, edge : edge + 8, :] = zero
            guess[p, edge : edge + 8, :] = zero
            first[p, edge : edge + 8, :] = zero
        win_s[p, ROW - 4 : ROW, :] = z_low[p, 0:4, :]
        win_s[p, end : end + 4, :] = z_high[p, 0:4, :]
        win_h[p, ROW - 4 : ROW, :] = (0.5 * has_low) * z_low[p, 4:8, :]
        win_h[p, end : end + 4, :] = (0.5 * has_high) * z_high[p, 4:8, :]
    for p in range(bx):
        win_s[p + 4, ROW:end, :] = source[p, :, :]
        win_h[p + 4, ROW:end, :] = 0.5 * cond[p, :, :]
    for p in range(3):
        win_s[p + 1, ROW:end, :] = low[p, :, :]
        win_s[p + bx + 4, ROW:end, :] = high[p, :, :]
    for p in range(4):
        win_h[p, ROW:end, :] = 0.5 * low[p + 3, :, :]
        win_h[p + bx + 4, ROW:end, :] = 0.5 * high[p + 3, :, :]

    level = Level(0, gx, gz, (bx, bz), cells, 4, (win_h, fx, fz, left, right, diag, inverse))
    row, count = (ROW - 4, bz + 8)
    level.coefs(range(1, planes - 1), row, count)
    level.first_down(win_s, first, range(1, planes - 1), row, count)
    level.second_down(win_s, first, guess, range(2, planes - 2), row, count)
    sources = level.restricted_remainder(win_s, guess, temp, range(4, 4 + bx), ROW, bz)
    halves = restricted(win_h, temp, 1, range(2, planes - 2), ROW - 8, bz + 16)
    for p, value in enumerate(halves):
        next_half[p, :, :] = value
    own = bz // 2
    odd = (lanes_of(own) & 1) == 1
    padded = cut(next_half, range(bx // 2 + 2), 3, own + 2)
    for p, value in enumerate(sources):
        mixed = jnp.where(odd, padded[p + 1][1 : 1 + own], value)
        to_next[p, :, :] = mixed
        to_prev[p, :, :] = mixed
    end = bx // 2 - 1
    to_next[end + 1, :, :] = first_iterate(sources[0], padded, 1, own, 1, 2)
    to_prev[end + 1, :, :] = first_iterate(sources[end], padded, end + 1, own, 1, 2)
    keep_window(kept_s, win_s, 3, 8)
    keep_window(kept_h, win_h, 2, 8)
    keep_window(kept_g, guess, 2, 8)


def inside_z(gz, count):
    return (jnp.where(gz > 0, 1.0, 0.0), jnp.where(gz < count - 1, 1.0, 0.0))


def edge_rows_1(low, here, high, to_high, to_low):
    at = 0
    for part, count in ((low, low.shape[0]), (here, here.shape[0] - 1), (high, high.shape[0])):
        rows = part.shape[1]
        to_high[at : at + count, :, :] = part[0:count, rows - 16 : rows, :]
        to_low[at : at + count, :, :] = part[0:count, 0:16, :]
        at += count


def down_1(cells, pos, here, low, high, z_low, z_high, kept_s, kept_h, kept_g, to_next, to_prev, win_s, win_h, guess, fx, fz, left, right, diag, inverse, first, temp, next_source, next_half):
    gx, gz = (pos[0], pos[1])
    bx, bz = (here.shape[0] - 1, here.shape[1])
    planes, base = (3 * bx, 24)
    end = base + bz
    zero = jnp.zeros((8, LANES), jnp.float32)
    has_low, has_high = inside_z(gz, cells[1] // bz)

    def unpack(p, start, rows, mixed):
        odd = (lanes_of(rows) & 1) == 1
        win_s[p, start : start + rows, :] = jnp.where(odd, roll(mixed, 1), mixed)
        win_h[p, start : start + rows, :] = jnp.where(odd, mixed, roll(mixed, -1))

    edges = 0
    for b, part in enumerate((low, here, high)):
        for p in range(bx):
            unpack(b * bx + p, base, bz, part[p, :, :])
            unpack(b * bx + p, base - 16, 16, has_low * z_low[edges + p, :, :])
            unpack(b * bx + p, end, 16, has_high * z_high[edges + p, :, :])
        edges += bx
        if b != 1:
            q = 0 if b == 0 else planes - 1
            first[q, base:end, :] = part[bx, :, :]
            first[q, base - 16 : base, :] = has_low * z_low[edges, :, :]
            first[q, end : end + 16, :] = has_high * z_high[edges, :, :]
            edges += 1
    for p in range(planes):
        for ref in (win_s, win_h):
            ref[p, 0:8, :] = zero
            ref[p, end + 16 : end + 24, :] = zero
        for ref in (first, guess):
            ref[p, 8:16, :] = zero if 0 < p < planes - 1 or ref is guess else ref[p, 8:16, :]
            ref[p, end + 8 : end + 16, :] = zero if 0 < p < planes - 1 or ref is guess else ref[p, end + 8 : end + 16, :]

    level = Level(1, gx, gz, (bx, bz), cells, bx, (win_h, fx, fz, left, right, diag, inverse), base)
    row, count = (base - 12, bz + 24)
    level.coefs(range(1, planes - 1), row, count)
    level.first_down(win_s, first, range(1, planes - 1), row, count)
    level.second_down(win_s, first, guess, range(1, planes - 1), row, count)
    own = bz // 2
    sources = level.restricted_remainder(win_s, guess, temp, range(bx - 2, 2 * bx + 2), row, count)
    halves = restricted(win_h, temp, 2, range(planes), base - 16, bz + 32)
    next_source[...] = jnp.zeros(next_source.shape, jnp.float32)
    for p, value in enumerate(sources):
        next_source[p + 1, 2 : 2 + count // 2, :] = value
    for p, value in enumerate(halves):
        next_half[p, :, :] = value
    lane = lanes_of(own + 16) & 3

    def pair(p):
        mixed = jnp.where(lane == 0, next_source[p, :, :], next_half[p, :, :])
        mixed = jnp.where(lane == 2, next_source[p + 1, :, :], mixed)
        return jnp.where(lane == 3, next_half[p + 1, :, :], mixed)

    middle = pair(2)
    to_next[0, :, :] = pair(0)
    to_next[1, :, :] = middle
    to_prev[0, :, :] = middle
    to_prev[1, :, :] = pair(4)
    keep_window(kept_s, win_s, 2, base - 8)
    keep_window(kept_h, win_h, 1, base - 8)
    keep_window(kept_g, guess, 1, base - 8)


def spread(mixed, which):
    only = jnp.where((lanes_of(mixed.shape[0]) & 3) == which, mixed, 0.0)
    only = roll(only, -which) if which else only
    twice = only + roll(only, 1)
    return twice + roll(twice, 2)


def down_2(cells, pos, prev, here, next_, kept_s, kept_h, kept_g, message, to_next, to_prev, win_s, win_h, guess, fx, fz, left, right, diag, inverse, first, temp):
    gx, gz = (pos[0], pos[1])
    bx, bz = (2, prev.shape[1] - 16)
    own, planes = (4, 10)
    end = ROW + bz
    zero = jnp.zeros((8, LANES), jnp.float32)
    pairs = (prev, 0), (prev, 1), (here, 1), (next_, 0), (next_, 1)
    for q, (part, at) in enumerate(pairs):
        mixed = part[at, :, :]
        for p in range(2):
            win_s[2 * q + p, 8 : end + 8, :] = spread(mixed, 2 * p)
            win_h[2 * q + p, 8 : end + 8, :] = spread(mixed, 2 * p + 1)
    for p in range(planes):
        for ref in (win_s, win_h, first):
            ref[p, 0:8, :] = zero
            ref[p, end + 8 : end + 16, :] = zero
    level = Level(2, gx, gz, (bx, bz), cells, own, (win_h, fx, fz, left, right, diag, inverse))
    row, count = (ROW - 8, bz + 16)
    level.coefs(range(own - 3, own + 5), row, count)
    level.first_down(win_s, first, range(own - 3, own + 5), row, count)
    level.second_down(win_s, first, guess, range(own - 2, own + 4), row, count)
    keep_window(kept_s, win_s, 1, 8)
    keep_window(kept_h, win_h, 0, 8)
    keep_window(kept_g, guess, own, 8)
    lane = lanes_of(count) & 3
    for out, begin in ((to_next, own - 2), (to_prev, own)):
        mixed = guess[begin, row : row + count, :]
        for p in range(1, 4):
            mixed = jnp.where(lane == p, guess[begin + p, row : row + count, :], mixed)
        out[...] = mixed
    sources = level.restricted_remainder(win_s, guess, temp, range(own, own + bx), ROW, bz)
    halves = restricted(win_h, temp, 4, range(own, own + bx), ROW, bz)
    rows = bz // 2
    cell = lax.broadcasted_iota(jnp.int32, (LANES, LANES), 0)
    lane = lax.broadcasted_iota(jnp.int32, (LANES, LANES), 1)
    pick = jnp.where(((cell >> 3) == (lane & 15)) & ((cell & 7) == 0), 1.0, 0.0)
    keep = (lanes_of(rows) >> 4) == rows_of(rows)
    for at, value in enumerate((sources[0], halves[0])):
        dense = jnp.dot(value, pick, precision=lax.Precision.HIGHEST, preferred_element_type=jnp.float32)
        dense = jnp.sum(jnp.where(keep, dense, 0.0), axis=0, keepdims=True)
        for device in range(message.shape[0]):
            message[device, at : at + 1, :] = dense


class Coarsest:
    def __init__(self, base, state, update):
        self.base, self.state, self.update, self.now = (base, state, update, 0)
        self.planes = update.shape[1]
        self.weights = list(zip(*cheb_weights(COARSE_ITERS, 0.02, 2.0)))
        zero = jnp.zeros((8, LANES), jnp.float32)
        for buffer in range(2):
            for b in range(3):
                state[buffer, b, 0:8, :] = zero
                state[buffer, b, self.planes + 8 : self.planes + 16, :] = zero

    def beside_z(self, values):
        lane = lanes_of(values[0].shape[0])
        ahead, back = ([roll(v, 16) for v in values], [roll(v, -16) for v in values])
        before = [jnp.where(lane < 16, ahead[max(b - 1, 0)], ahead[b]) for b in range(3)]
        after = [jnp.where(lane >= LANES - 16, back[min(b + 1, 2)], back[b]) for b in range(3)]
        return before, after

    def start(self, parts, half, flags):
        planes, zero = (self.planes, jnp.zeros((8, LANES), jnp.float32))
        gain = self.weights[0][1]
        for b in range(3):
            half[b, 0:8, :] = zero
            half[b, planes + 8 : planes + 16, :] = zero
            half[b, 8 : planes + 8, :] = flags[b] * parts[b][pl.ds(1, planes, stride=2), :]
        lane = lanes_of(8)
        in_left, in_right = ((lane & 15) > 0, (lane & 15) < 15)
        for x in range(0, planes, 8):
            centers = [half[b, x + 8 : x + 16, :] for b in range(3)]
            before, after = self.beside_z(centers)
            for b, center in enumerate(centers):
                faces = [
                    center + half[b, x + 7 : x + 15, :],
                    center + half[b, x + 9 : x + 17, :],
                    center + before[b],
                    center + after[b],
                    center + jnp.where(in_left, roll(center, 1), 0.0),
                    center + jnp.where(in_right, roll(center, -1), 0.0),
                ]
                diagonal = faces[0] + faces[1] + faces[2] + faces[3] + faces[4] + faces[5]
                inverse = flags[b] * jnp.where(diagonal > 0.0, 1.0 / diagonal, 0.0)
                faces = [face * inverse for face in faces]
                faces[4] = jnp.where(in_left, faces[4], 0.0)
                faces[5] = jnp.where(in_right, faces[5], 0.0)
                for which, face in enumerate(faces):
                    self.base[7 * b + which, x : x + 8, :] = face
                scaled = 64.0 * (parts[b][pl.ds(2 * x, 8, stride=2), :] * inverse)
                self.base[7 * b + 6, x : x + 8, :] = scaled
                self.update[b, x : x + 8, :] = gain * scaled
                self.state[self.now, b, x + 8 : x + 16, :] = gain * scaled

    def resume(self, parts, flags):
        for b in range(3):
            self.state[self.now, b, 8 : self.planes + 8, :] = flags[b] * parts[b][0, :, :]
            self.update[b, :, :] = flags[b] * parts[b][1, :, :]

    def steps(self, which):
        for index in which:
            carry, gain = self.weights[index]
            old, new = (self.now, 1 - self.now)
            for x in range(0, self.planes, 8):
                centers = [self.state[old, b, x + 8 : x + 16, :] for b in range(3)]
                before, after = self.beside_z(centers)
                for b, center in enumerate(centers):
                    face = [self.base[7 * b + k, x : x + 8, :] for k in range(7)]
                    beside = face[0] * self.state[old, b, x + 7 : x + 15, :] + face[1] * self.state[old, b, x + 9 : x + 17, :]
                    beside = beside + (face[2] * before[b] + face[3] * after[b])
                    beside = beside + (face[4] * roll(center, 1) + face[5] * roll(center, -1))
                    change = carry * self.update[b, x : x + 8, :] + gain * (face[6] - center + beside)
                    self.update[b, x : x + 8, :] = change
                    self.state[new, b, x + 8 : x + 16, :] = center + change
            self.now = new

    def leave(self, out):
        out[0, :, :] = self.state[self.now, 1, 8 : self.planes + 8, :]
        out[1, :, :] = self.update[1, :, :]


def solve_first(count, pos, low, here, high, arrived, base, out, half, state, update):
    has_low, has_high = inside_z(pos[1], count)
    level = Coarsest(base, state, update)
    level.start((low, here, high), half, (has_low, 1.0, has_high))
    level.steps(range(1, SOLVE[0]))
    level.leave(out)


def solve_next(count, pos, base, low, here, high, arrived, out, state, update):
    has_low, has_high = inside_z(pos[1], count)
    level = Coarsest(base, state, update)
    level.resume((low, here, high), (has_low, 1.0, has_high))
    level.steps(range(SOLVE[0], SOLVE[1]))
    level.leave(out)


def finish(cells, pos, base, low, here, high, prev2, next2, s2, h2, g2, s1, h1, g1, s0, h0, g0, out, *scratch):
    gx, gz = (pos[0], pos[1])
    state, update3, coarse2, temp, start2, start1, start0 = scratch[:7]
    shared, middle, update = (scratch[7:13], scratch[13], scratch[14])
    s2, h2, g2 = (View(s2, 1, 8), View(h2, 0, 8), View(g2, 4, 8))
    s1, h1, g1 = (View(s1, 2, 8), View(h1, 1, 8), View(g1, 1, 8))
    s0, h0, g0 = (View(s0, 3, 8), View(h0, 2, 8), View(g0, 2, 8))
    bz0 = out.shape[1]
    bz1, bz2 = (bz0 // 2, bz0 // 4)
    has_low, has_high = inside_z(gz, cells[0][1] // bz0)
    level = Coarsest(base, state, update3)
    level.resume((low, here, high), (has_low, 1.0, has_high))
    level.steps(range(SOLVE[1], COARSE_ITERS))
    last = level.now

    bx2 = 2
    rows = bz2 + 8
    cell = lax.broadcasted_iota(jnp.int32, (LANES, LANES), 0)
    lane = lax.broadcasted_iota(jnp.int32, (LANES, LANES), 1)
    pick = jnp.where((cell & 15) == (lane >> 3), 1.0, 0.0)
    z3 = (rows_of(rows) >> 1) - 2
    keep = (lanes_of(rows) >> 4) == (z3 & 7)
    columns = [state[last, b, pl.ds(gx + 6, 8), :] for b in range(3)]
    for q in range(5):
        picked = [column[q : q + 1, :] for column in columns]
        wide = jnp.where(z3 < 0, picked[0], jnp.where(z3 < 8, picked[1], picked[2]))
        coarse2[q * rows : (q + 1) * rows, :] = jnp.where(keep, wide, 0.0)
    spread_out = jnp.dot(coarse2[...], pick, precision=lax.Precision.HIGHEST, preferred_element_type=jnp.float32)
    coarse2[...] = spread_out

    start, own = (start2, 4)
    row, count = (ROW - 4, rows)
    zero = jnp.zeros((8, LANES), jnp.float32)
    for q in range(5):
        for p in (own - 4 + 2 * q, own - 3 + 2 * q):
            start[p, 8:16, :] = zero
            start[p, ROW + bz2 : ROW + bz2 + 8, :] = zero
            if q == 2:
                guess = g2[p, row : row + count, :]
            else:
                guess = spread((prev2 if q < 2 else next2)[4 : 4 + count, :], p if q < 2 else p - own - bx2)
            start[p, row : row + count, :] = guess + coarse2[q * rows : (q + 1) * rows, :]
    level = Level(2, gx, gz, (bx2, bz2), cells[2], own, (h2,) + tuple(shared))
    level.coefs(range(own - 3, own + 5), row, count)

    bx1 = 4

    def to_level_1(p, value):
        q = 2 * (p - own) + 4
        temp[pl.ds(0, value.shape[0], stride=2), :] = value
        temp[pl.ds(1, value.shape[0], stride=2), :] = value
        for r in (q, q + 1):
            if 1 <= r <= 10:
                start1[r, ROW - 4 : ROW + bz1 + 4, :] = (
                    g1[r, ROW - 4 : ROW + bz1 + 4, :] + temp[0 : bz1 + 8, :]
                )

    for r in range(1, 11):
        start1[r, 8:16, :] = zero
        start1[r, ROW + bz1 : ROW + bz1 + 8, :] = zero
    level.up(s2, start, middle, update, to_level_1, range(own - 2, own + 4), row, count, ROW - 2, bz2 + 4)
    level = Level(1, gx, gz, (bx1, bz1), cells[1], 4, (h1,) + tuple(shared))
    row, count = (ROW - 4, bz1 + 8)
    level.coefs(range(2, 10), row, count)

    bx0 = out.shape[0]
    for r in range(2, 14):
        start0[r, 8:16, :] = zero
        start0[r, ROW + bz0 : ROW + bz0 + 8, :] = zero

    def to_level_0(p, value):
        q = 2 * (p - 4) + 4
        temp[pl.ds(0, value.shape[0], stride=2), :] = value
        temp[pl.ds(1, value.shape[0], stride=2), :] = value
        for r in (q, q + 1):
            start0[r, ROW - 4 : ROW + bz0 + 4, :] = g0[r, ROW - 4 : ROW + bz0 + 4, :] + temp[0 : bz0 + 8, :]

    level.up(s1, start1, middle, update, to_level_0, range(3, 9), row, count, ROW - 2, bz1 + 4)
    level = Level(0, gx, gz, (bx0, bz0), cells[0], 4, (h0,) + tuple(shared))
    level.coefs(range(3, 13), ROW - 4, bz0 + 8)

    def to_out(p, value):
        out[p - 4, :, :] = value

    level.up(s0, start0, middle, update, to_out, range(4, 12), ROW - 4, bz0 + 8, ROW, bz0)


def f32(*shape):
    return jax.ShapeDtypeStruct(shape, jnp.float32)


def scratch(*shape):
    return pltpu.VMEM(shape, jnp.float32)


def call(kernel, name, outs, scratches, *args):
    smem = pl.BlockSpec(memory_space=pltpu.SMEM)
    limit = 4 * 2**20 + sum(4 * math.prod(ref.shape) for ref in scratches)
    vmem = pl.BlockSpec(memory_space=pltpu.VMEM)
    return pl.pallas_call(
        kernel,
        name=name,
        out_shape=outs,
        in_specs=[smem if arg.dtype == jnp.int32 else vmem for arg in args],
        out_specs=[vmem] * len(outs),
        scratch_shapes=scratches,
        compiler_params=pltpu.CompilerParams(vmem_limit_bytes=limit),
    )(*args)


def shift(array, axis, by):
    devices = lax.axis_size(axis)
    return lax.ppermute(array, axis, [(i, i + by) for i in range(devices) if 0 <= i + by < devices])


def turn(array, axis, by):
    devices = lax.axis_size(axis)
    return lax.ppermute(array, axis, [(i, (i + by) % devices) for i in range(devices)])


def on_device(right_side, conductivity):
    nx, nz = (lax.axis_size("gx"), lax.axis_size("gz"))
    bx, bz = right_side.shape[0:2]
    cells = [(nx * bx >> level, nz * bz >> level) for level in range(4)]
    pos = jnp.stack([lax.axis_index("gx"), lax.axis_index("gz")]).astype(jnp.int32)
    low = shift(jnp.concatenate([right_side[bx - 3 :], conductivity[bx - 4 :]]), "gx", 1)
    high = shift(jnp.concatenate([right_side[:3], conductivity[:4]]), "gx", -1)
    planes = bx + 8
    to_high, to_low = call(
        edge_rows_0, "edge_rows_0", [f32(planes, 8, LANES)] * 2, [], right_side, conductivity, low, high
    )
    z_low, z_high = (turn(to_high, "gz", 1), turn(to_low, "gz", -1))
    window = (planes, bz + 32, LANES)
    s0, h0, g0, for_next, for_prev = call(
        functools.partial(down_0, cells[0]),
        "down_0",
        [f32(bx + 2, bz + 16, LANES)] + [f32(bx + 4, bz + 16, LANES)] * 2 + [f32(bx // 2 + 1, bz // 2, LANES)] * 2,
        [scratch(*window)] * 10 + [scratch(bz + 16, LANES), scratch(bx // 2 + 2, bz // 2 + 8, LANES)],
        pos,
        right_side,
        conductivity,
        low,
        high,
        z_low,
        z_high,
    )

    bx, bz = (bx // 2, bz // 2)
    low, high = (shift(for_next, "gx", 1), shift(for_prev, "gx", -1))
    to_high, to_low = call(
        edge_rows_1, "edge_rows_1", [f32(3 * bx + 2, 16, LANES)] * 2, [], low, for_next, high
    )
    z_low, z_high = (turn(to_high, "gz", 1), turn(to_low, "gz", -1))
    window = (3 * bx, bz + 48, LANES)
    s1, h1, g1, for_next, for_prev = call(
        functools.partial(down_1, cells[1]),
        "down_1",
        [f32(bx + 4, bz + 16, LANES)] + [f32(bx + 6, bz + 16, LANES)] * 2 + [f32(2, bz // 2 + 16, LANES)] * 2,
        [scratch(*window)] * 10 + [scratch(bz + 32, LANES)] + [scratch(bx // 2 + 4, bz // 2 + 16, LANES)] * 2,
        pos,
        for_next,
        low,
        high,
        z_low,
        z_high,
    )

    bx, bz = (bx // 2, bz // 2)
    prev, next_ = (shift(for_next, "gx", 1), shift(for_prev, "gx", -1))
    window = (bx + 8, bz + 32, LANES)
    s2, h2, g2, row3, for_next, for_prev = call(
        functools.partial(down_2, cells[2]),
        "down_2",
        [f32(bx + 6, bz + 16, LANES), f32(bx + 8, bz + 16, LANES), f32(bx, bz + 16, LANES)]
        + [f32(nx, 2, LANES)]
        + [f32(bz + 16, LANES)] * 2,
        [scratch(*window)] * 10 + [scratch(bz + 16, LANES)],
        pos,
        prev,
        for_next,
        next_,
    )

    here = lax.all_to_all(row3, "gx", 0, 0, tiled=True)
    low, high = (turn(here, "gz", 1), turn(here, "gz", -1))
    blocks = [part.reshape(2 * nx, LANES) for part in (low, here, high)]
    solving = [scratch(2, 3, nx + 16, LANES), scratch(3, nx, LANES)]
    for_next, _ = lax.optimization_barrier((for_next, here))
    prev2 = shift(for_next, "gx", 1)
    base, here = call(
        functools.partial(solve_first, nz),
        "solve_first",
        [f32(21, nx, LANES), f32(2, nx, LANES)],
        [scratch(3, nx + 16, LANES)] + solving,
        pos,
        *blocks,
        prev2,
    )
    low, high = (turn(here, "gz", 1), turn(here, "gz", -1))
    for_prev, _ = lax.optimization_barrier((for_prev, here))
    next2 = shift(for_prev, "gx", -1)
    (here,) = call(
        functools.partial(solve_next, nz), "solve_next", [f32(2, nx, LANES)], solving, pos, base, low, here, high, next2
    )
    low, high = (turn(here, "gz", 1), turn(here, "gz", -1))

    bx, bz = right_side.shape[0:2]
    window = (bx + 8, bz + 32, LANES)
    work = solving + [scratch(5 * (bz // 4 + 8), LANES), scratch(bz + 32, LANES)]
    work += [scratch(bx // 4 + 8, bz // 4 + 32, LANES), scratch(bx // 2 + 8, bz // 2 + 32, LANES)]
    work += [scratch(*window)] * 9
    (result,) = call(
        functools.partial(finish, cells), "finish", [f32(*right_side.shape)], work, pos, base, low, here, high,
        prev2, next2, s2, h2, g2, s1, h1, g1, s0, h0, g0,
    )
    return result


def solution(mesh):
    return jax.shard_map(
        on_device,
        mesh=mesh,
        in_specs=(P("gx", "gz", None), P("gx", "gz", None)),
        out_specs=P("gx", "gz", None),
        check_vma=False,
    )
```

```python
import functools
import math

import jax
import jax.numpy as jnp
from jax import lax
from jax.experimental import pallas as pl
from jax.experimental.pallas import tpu as pltpu
from jax.sharding import PartitionSpec as P

COARSE_ITERS = 20
LANES = 128
ROW = 16
LATE = 8
SOLVE = (8, 16)


def cheb_weights(count, lower, upper):
    theta = 0.5 * (upper + lower)
    delta = 0.5 * (upper - lower)
    sigma = theta / delta
    rho_prev = 1.0 / sigma
    carry_terms = [0.0]
    gain_terms = [1.0 / theta]
    for step in range(1, count):
        rho_next = 1.0 / (2.0 * sigma - rho_prev)
        carry_terms.append(rho_next * rho_prev)
        gain_terms.append(2.0 * rho_next / delta)
        rho_prev = rho_next
    return (carry_terms, gain_terms)


(_, CARRY), (GAIN_FIRST, GAIN) = cheb_weights(2, 0.25, 2.0)


def lanes_of(rows):
    return lax.broadcasted_iota(jnp.int32, (rows, LANES), 1)


def rows_of(rows):
    return lax.broadcasted_iota(jnp.int32, (rows, LANES), 0)


def roll(value, shift, axis=1):
    return pltpu.roll(value, shift % value.shape[axis], axis)


def pair_sum(value, stride):
    odd = (lanes_of(value.shape[0]) & stride) != 0
    return value + jnp.where(odd, roll(value, stride), roll(value, -stride))


class Level:
    def __init__(self, level, gx, gz, brick, cells, first_plane, refs, first_row=ROW):
        self.stride, self.scale, self.first_row = (2**level, 0.25**level, first_row)
        self.gx, self.gz, self.brick, self.cells, self.first_plane = (gx, gz, brick, cells, first_plane)
        self.half, self.fx, self.fz, self.left, self.right, self.diag, self.inverse = refs

    def coefs(self, planes, row, count, source, first):
        half, stride = (self.half, self.stride)
        lane = lanes_of(count)
        in_left, in_right = (lane >= stride, lane < LANES - stride)
        here = rows_of(count) + (row - self.first_row + self.gz * self.brick[1])
        inside_rows = jnp.where((here >= 0) & (here < self.cells[1]), 1.0 / self.scale, 0.0)
        for p in planes:
            center = half[p, row : row + count, :]
            before = center + half[p - 1, row : row + count, :]
            after = center + half[p + 1, row : row + count, :]
            low = center + half[p, row - 1 : row - 1 + count, :]
            high = center + half[p, row + 1 : row + 1 + count, :]
            left = center + jnp.where(in_left, roll(center, stride), 0.0)
            right = center + jnp.where(in_right, roll(center, -stride), 0.0)
            diagonal = ((before + after) + (low + high)) + (left + right)
            plane = p - self.first_plane + self.gx * self.brick[0]
            inside = jnp.where(jnp.logical_and(plane >= 0, plane < self.cells[0]), 1.0, 0.0)
            inverse = (inside * inside_rows) * jnp.where(diagonal > 0.0, 1.0 / diagonal, 0.0)
            self.fx[p, row : row + count, :] = before
            self.fz[p, row : row + count, :] = low
            self.fz[p, row + 1 : row + 1 + count, :] = high
            self.left[p, row : row + count, :] = jnp.where(in_left, left, 0.0)
            self.right[p, row : row + count, :] = jnp.where(in_right, right, 0.0)
            self.diag[p, row : row + count, :] = diagonal
            self.inverse[p, row : row + count, :] = inverse
            first[p, row : row + count, :] = GAIN_FIRST * (inverse * source[p, row : row + count, :])
        self.fx[planes[-1] + 1, row : row + count, :] = after

    def remainder(self, source, guess, p, row, count):
        center = guess[p, row : row + count, :]
        beside = (
            self.fx[p, row : row + count, :] * guess[p - 1, row : row + count, :]
            + self.fx[p + 1, row : row + count, :] * guess[p + 1, row : row + count, :]
        )
        beside = beside + (
            self.fz[p, row : row + count, :] * guess[p, row - 1 : row - 1 + count, :]
            + self.fz[p, row + 1 : row + 1 + count, :] * guess[p, row + 1 : row + 1 + count, :]
        )
        beside = beside + (
            self.left[p, row : row + count, :] * roll(center, self.stride)
            + self.right[p, row : row + count, :] * roll(center, -self.stride)
        )
        applied = self.diag[p, row : row + count, :] * center - beside
        return source[p, row : row + count, :] - self.scale * applied

    def second_down(self, source, first, out, planes, row, count):
        for p in planes:
            rest = self.remainder(source, first, p, row, count)
            start = first[p, row : row + count, :]
            update = CARRY * start + GAIN * (self.inverse[p, row : row + count, :] * rest)
            out[p, row : row + count, :] = start + update

    def restricted_remainder(self, source, guess, temp, planes, row, rows):
        parts = []
        for p in planes[::2]:
            both = self.remainder(source, guess, p, row, rows) + self.remainder(source, guess, p + 1, row, rows)
            temp[0:rows, :] = pair_sum(both, self.stride)
            parts.append(0.125 * (temp[pl.ds(0, rows // 2, stride=2), :] + temp[pl.ds(1, rows // 2, stride=2), :]))
        return parts

    def up(self, source, start, middle, update, out, planes, row, count, out_row, out_count):
        for p in range(planes[0] - 1, planes[-1] + 2):
            first = GAIN_FIRST * (
                self.inverse[p, row : row + count, :] * self.remainder(source, start, p, row, count)
            )
            update[p, row : row + count, :] = first
            middle[p, row : row + count, :] = start[p, row : row + count, :] + first
        for p in planes:
            second = CARRY * update[p, out_row : out_row + out_count, :] + GAIN * (
                self.inverse[p, out_row : out_row + out_count, :]
                * self.remainder(source, middle, p, out_row, out_count)
            )
            out(p, middle[p, out_row : out_row + out_count, :] + second)


def restricted(half, temp, stride, planes, row, rows):
    parts = []
    for p in planes[::2]:
        both = half[p, row : row + rows, :] + half[p + 1, row : row + rows, :]
        temp[0:rows, :] = pair_sum(both, stride)
        parts.append(0.125 * (temp[pl.ds(0, rows // 2, stride=2), :] + temp[pl.ds(1, rows // 2, stride=2), :]))
    return parts


def first_iterate(source, half, p, count, level, stride):
    center = half[p][1 : 1 + count]
    lane = lanes_of(count)
    diagonal = 6.0 * center + half[p - 1][1 : 1 + count] + half[p + 1][1 : 1 + count]
    diagonal = diagonal + half[p][0:count] + half[p][2 : 2 + count]
    diagonal = diagonal + jnp.where(lane >= stride, roll(center, stride), 0.0)
    diagonal = diagonal + jnp.where(lane < LANES - stride, roll(center, -stride), 0.0)
    inverse = jnp.where(diagonal > 0.0, 1.0 / (0.25**level * diagonal), 0.0)
    return GAIN_FIRST * source * inverse


def cut(half_ref, planes, row, count):
    return [half_ref[p, row : row + count, :] for p in planes]


def edge_rows_0(source, cond, low, high, to_high, to_low):
    bx, bz = source.shape[0:2]
    zero = jnp.zeros((4, LANES), jnp.float32)
    for rows, out in ((slice(bz - 4, bz), to_high), (slice(0, 4), to_low)):
        out[0, 0:4, :] = zero
        out[bx + 5, 0:4, :] = zero
        for p in range(2):
            out[p + 1, 0:4, :] = low[p, rows, :]
            out[p + bx + 3, 0:4, :] = high[p, rows, :]
        for p in range(3):
            out[p, 4:8, :] = low[p + 2, rows, :]
            out[p + bx + 3, 4:8, :] = high[p + 2, rows, :]
        for p in range(bx):
            out[p + 3, 0:4, :] = source[p, rows, :]
            out[p + 3, 4:8, :] = cond[p, rows, :]


def inner_0(cells, pos, source, cond, low, high, win_s, win_h, guess, fx, fz, left, right, diag, inverse, first, next_source, next_half, temp):
    gx, gz = (pos[0], pos[1])
    bx, bz = source.shape[0:2]
    planes, end = (bx + 6, ROW + bz)
    zero = jnp.zeros((8, LANES), jnp.float32)
    for p in range(planes):
        for edge in (8, end, end + 8):
            win_s[p, edge : edge + 8, :] = zero
            win_h[p, edge : edge + 8, :] = zero
            guess[p, edge : edge + 8, :] = zero
            first[p, edge : edge + 8, :] = zero
    for p in range(bx):
        win_s[p + 3, ROW:end, :] = source[p, :, :]
        win_h[p + 3, ROW:end, :] = 0.5 * cond[p, :, :]
    for p in range(2):
        win_s[p + 1, ROW:end, :] = low[p, :, :]
        win_s[p + bx + 3, ROW:end, :] = high[p, :, :]
    for p in range(3):
        win_h[p, ROW:end, :] = 0.5 * low[p + 2, :, :]
        win_h[p + bx + 3, ROW:end, :] = 0.5 * high[p + 2, :, :]
    level = Level(0, gx, gz, (bx, bz), cells, 3, (win_h, fx, fz, left, right, diag, inverse))
    level.coefs(range(1, planes - 1), ROW, bz, win_s, first)
    level.second_down(win_s, first, guess, range(2, planes - 2), ROW, bz)
    for p, value in enumerate(level.restricted_remainder(win_s, guess, temp, range(3, 3 + bx), ROW, bz)):
        next_source[p, :, :] = value
    for p, value in enumerate(restricted(win_h, temp, 1, range(1, planes - 1), ROW - 8, bz + 16)):
        next_half[p, :, :] = value


def outer_0(cells, pos, z_low, z_high, *refs):
    win_s, win_h, guess, fx, fz, left, right, diag, inverse, first, next_source, next_half = refs[12:24]
    to_next, to_prev, temp = refs[24:]
    gx, gz = (pos[0], pos[1])
    planes, bx, bz = (win_s.shape[0], win_s.shape[0] - 6, win_s.shape[1] - 32)
    end = ROW + bz
    has_low, has_high = inside_z(gz, cells[1] // bz)
    for p in range(planes):
        win_s[p, ROW - 4 : ROW, :] = z_low[p, 0:4, :]
        win_s[p, end : end + 4, :] = z_high[p, 0:4, :]
        win_h[p, ROW - 4 : ROW, :] = (0.5 * has_low) * z_low[p, 4:8, :]
        win_h[p, end : end + 4, :] = (0.5 * has_high) * z_high[p, 4:8, :]
    level = Level(0, gx, gz, (bx, bz), cells, 3, (win_h, fx, fz, left, right, diag, inverse))
    strips = ROW - 4, end - 4
    for row in strips:
        level.coefs(range(1, planes - 1), row, 8, win_s, first)
    for row in strips:
        level.second_down(win_s, first, guess, range(2, planes - 2), row, 8)
    own = bz // 2
    for row, at in ((ROW, 0), (end - 8, own - 4)):
        for p, value in enumerate(level.restricted_remainder(win_s, guess, temp, range(3, 3 + bx), row, 8)):
            next_source[p, at : at + 4, :] = value
        for p, value in enumerate(restricted(win_h, temp, 1, range(1, planes - 1), row - 8 if row == ROW else end, 8)):
            at_half = 0 if row == ROW else own + 4
            next_half[p, at_half : at_half + 4, :] = value
    odd = (lanes_of(own) & 1) == 1
    for p in range(bx // 2):
        mixed = jnp.where(odd, next_half[p + 1, 4 : 4 + own, :], next_source[p, :, :])
        to_next[p, :, :] = mixed
        to_prev[p, :, :] = mixed
    padded = cut(next_half, range(bx // 2 + 2), 3, own + 2)
    last = bx // 2 - 1
    to_next[last + 1, :, :] = first_iterate(next_source[0, :, :], padded, 1, own, 1, 2)
    to_prev[last + 1, :, :] = first_iterate(next_source[last, :, :], padded, last + 1, own, 1, 2)


def inside_z(gz, count):
    return (jnp.where(gz > 0, 1.0, 0.0), jnp.where(gz < count - 1, 1.0, 0.0))


def edge_rows_1(low, here, high, to_high, to_low):
    at = 0
    for part, count in ((low, low.shape[0]), (here, here.shape[0] - 1), (high, high.shape[0])):
        rows = part.shape[1]
        to_high[at : at + count, :, :] = part[0:count, rows - 16 : rows, :]
        to_low[at : at + count, :, :] = part[0:count, 0:16, :]
        at += count


def unpack_1(win_s, win_h, p, start, rows, mixed):
    odd = (lanes_of(rows) & 1) == 1
    win_s[p, start : start + rows, :] = jnp.where(odd, roll(mixed, 1), mixed)
    win_h[p, start : start + rows, :] = jnp.where(odd, mixed, roll(mixed, -1))


def inner_1(cells, pos, here, low, high, win_s, win_h, guess, fx, fz, left, right, diag, inverse, first, next_source, next_half, temp):
    gx, gz = (pos[0], pos[1])
    bx, bz = (here.shape[0] - 1, here.shape[1])
    planes, base = (3 * bx, 24)
    end = base + bz
    zero = jnp.zeros((8, LANES), jnp.float32)
    for b, part in enumerate((low, here, high)):
        for p in range(bx):
            unpack_1(win_s, win_h, b * bx + p, base, bz, part[p, :, :])
    first[0, base:end, :] = low[bx, :, :]
    first[planes - 1, base:end, :] = high[bx, :, :]
    for p in range(planes):
        for ref in (win_s, win_h, first, guess):
            for row in (0, 8, 16, end, end + 8, end + 16):
                ref[p, row : row + 8, :] = zero
    level = Level(1, gx, gz, (bx, bz), cells, bx, (win_h, fx, fz, left, right, diag, inverse), base)
    level.coefs(range(1, planes - 1), base, bz, win_s, first)
    level.second_down(win_s, first, guess, range(1, planes - 1), base, bz)
    next_source[...] = jnp.zeros(next_source.shape, jnp.float32)
    own = bz // 2
    for p, value in enumerate(level.restricted_remainder(win_s, guess, temp, range(bx - 2, 2 * bx + 2), base, bz)):
        next_source[p + 1, 8 : 8 + own, :] = value
    for p, value in enumerate(restricted(win_h, temp, 2, range(planes), base, bz)):
        next_half[p, 8 : 8 + own, :] = value


def outer_1(cells, pos, z_low, z_high, *refs):
    win_s, win_h, guess, fx, fz, left, right, diag, inverse, first, next_source, next_half = refs[12:24]
    to_next, to_prev, temp = refs[24:]
    gx, gz = (pos[0], pos[1])
    planes, base = (win_s.shape[0], 24)
    bx, bz = (planes // 3, win_s.shape[1] - 48)
    end = base + bz
    has_low, has_high = inside_z(gz, cells[1] // bz)
    for start, ref, inside in ((base - 16, z_low, has_low), (end, z_high, has_high)):
        for p in range(planes):
            at = p if p < bx else p + 1
            unpack_1(win_s, win_h, p, start, 16, inside * ref[at, :, :])
        first[0, start : start + 16, :] = inside * ref[bx, :, :]
        first[planes - 1, start : start + 16, :] = inside * ref[planes + 1, :, :]
    level = Level(1, gx, gz, (bx, bz), cells, bx, (win_h, fx, fz, left, right, diag, inverse), base)
    strips = base - 12, end - 4
    for row in strips:
        level.coefs(range(1, planes - 1), row, 16, win_s, first)
    for row in strips:
        level.second_down(win_s, first, guess, range(1, planes - 1), row, 16)
    for row in strips:
        at = (row - base + 16) // 2
        for p, value in enumerate(level.restricted_remainder(win_s, guess, temp, range(bx - 2, 2 * bx + 2), row, 16)):
            next_source[p + 1, at : at + 8, :] = value
    for row in (base - 16, end):
        at = (row - base + 16) // 2
        for p, value in enumerate(restricted(win_h, temp, 2, range(planes), row, 16)):
            next_half[p, at : at + 8, :] = value
    lane = lanes_of(next_source.shape[1]) & 3

    def pair(p):
        mixed = jnp.where(lane == 0, next_source[p, :, :], next_half[p, :, :])
        mixed = jnp.where(lane == 2, next_source[p + 1, :, :], mixed)
        return jnp.where(lane == 3, next_half[p + 1, :, :], mixed)

    middle = pair(2)
    to_next[0, :, :] = pair(0)
    to_next[1, :, :] = middle
    to_prev[0, :, :] = middle
    to_prev[1, :, :] = pair(4)


def spread(mixed, which):
    only = jnp.where((lanes_of(mixed.shape[0]) & 3) == which, mixed, 0.0)
    only = roll(only, -which) if which else only
    twice = only + roll(only, 1)
    return twice + roll(twice, 2)


def down_2(cells, pos, prev, here, next_, guess0, win_s, guess, fx, fz, left, right, diag, inverse, message, to_next, to_prev, win_h, first, temp):
    gx, gz = (pos[0], pos[1])
    bx, bz = (2, prev.shape[1] - 16)
    own, planes = (4, 10)
    end = ROW + bz
    zero = jnp.zeros((8, LANES), jnp.float32)
    pairs = (prev, 0), (prev, 1), (here, 1), (next_, 0), (next_, 1)
    for q, (part, at) in enumerate(pairs):
        mixed = part[at, :, :]
        for p in range(2):
            win_s[2 * q + p, 8 : end + 8, :] = spread(mixed, 2 * p)
            win_h[2 * q + p, 8 : end + 8, :] = spread(mixed, 2 * p + 1)
    for p in range(planes):
        for ref in (win_s, win_h, first):
            ref[p, 0:8, :] = zero
            ref[p, end + 8 : end + 16, :] = zero
    level = Level(2, gx, gz, (bx, bz), cells, own, (win_h, fx, fz, left, right, diag, inverse))
    row, count = (ROW - 8, bz + 16)
    level.coefs(range(own - 3, own + 5), row, count, win_s, first)
    level.second_down(win_s, first, guess, range(own - 2, own + 4), row, count)
    for out, begin in ((to_next, own - 2), (to_prev, own)):
        for p in range(4):
            out[p, :, :] = guess[begin + p, row : row + count, :]
        far = guess0.shape[0] - 5 if out is to_next else 4
        for p in range(4, out.shape[0]):
            begin0 = ROW + ((p - 4) & 1) * count
            out[p, :, :] = guess0[far, begin0 : begin0 + count, :]
    sources = level.restricted_remainder(win_s, guess, temp, range(own, own + bx), ROW, bz)
    halves = restricted(win_h, temp, 4, range(own, own + bx), ROW, bz)
    rows = bz // 2
    cell = lax.broadcasted_iota(jnp.int32, (LANES, LANES), 0)
    lane = lax.broadcasted_iota(jnp.int32, (LANES, LANES), 1)
    pick = jnp.where(((cell >> 3) == (lane & 15)) & ((cell & 7) == 0), 1.0, 0.0)
    keep = (lanes_of(rows) >> 4) == rows_of(rows)
    for at, value in enumerate((sources[0], halves[0])):
        dense = jnp.dot(value, pick, precision=lax.Precision.HIGHEST, preferred_element_type=jnp.float32)
        dense = jnp.sum(jnp.where(keep, dense, 0.0), axis=0, keepdims=True)
        for device in range(message.shape[0]):
            message[device, at : at + 1, :] = dense


class Coarsest:
    def __init__(self, base, state, update):
        self.base, self.state, self.update, self.now = (base, state, update, 0)
        self.planes = update.shape[1]
        self.weights = list(zip(*cheb_weights(COARSE_ITERS, 0.02, 2.0)))
        zero = jnp.zeros((8, LANES), jnp.float32)
        for buffer in range(2):
            for b in range(3):
                state[buffer, b, 0:8, :] = zero
                state[buffer, b, self.planes + 8 : self.planes + 16, :] = zero

    def beside_z(self, values):
        lane = lanes_of(values[0].shape[0])
        ahead, back = ([roll(v, 16) for v in values], [roll(v, -16) for v in values])
        before = [jnp.where(lane < 16, ahead[max(b - 1, 0)], ahead[b]) for b in range(3)]
        after = [jnp.where(lane >= LANES - 16, back[min(b + 1, 2)], back[b]) for b in range(3)]
        return before, after

    def start(self, parts, half, flags):
        planes, zero = (self.planes, jnp.zeros((8, LANES), jnp.float32))
        gain = self.weights[0][1]
        for b in range(3):
            half[b, 0:8, :] = zero
            half[b, planes + 8 : planes + 16, :] = zero
            half[b, 8 : planes + 8, :] = flags[b] * parts[b][pl.ds(1, planes, stride=2), :]
        lane = lanes_of(8)
        in_left, in_right = ((lane & 15) > 0, (lane & 15) < 15)
        for x in range(0, planes, 8):
            centers = [half[b, x + 8 : x + 16, :] for b in range(3)]
            before, after = self.beside_z(centers)
            for b, center in enumerate(centers):
                faces = [
                    center + half[b, x + 7 : x + 15, :],
                    center + half[b, x + 9 : x + 17, :],
                    center + before[b],
                    center + after[b],
                    center + jnp.where(in_left, roll(center, 1), 0.0),
                    center + jnp.where(in_right, roll(center, -1), 0.0),
                ]
                diagonal = faces[0] + faces[1] + faces[2] + faces[3] + faces[4] + faces[5]
                inverse = flags[b] * jnp.where(diagonal > 0.0, 1.0 / diagonal, 0.0)
                faces = [face * inverse for face in faces]
                faces[4] = jnp.where(in_left, faces[4], 0.0)
                faces[5] = jnp.where(in_right, faces[5], 0.0)
                for which, face in enumerate(faces):
                    self.base[7 * b + which, x : x + 8, :] = face
                scaled = 64.0 * (parts[b][pl.ds(2 * x, 8, stride=2), :] * inverse)
                self.base[7 * b + 6, x : x + 8, :] = scaled
                self.update[b, x : x + 8, :] = gain * scaled
                self.state[self.now, b, x + 8 : x + 16, :] = gain * scaled

    def resume(self, parts, flags):
        for b in range(3):
            self.state[self.now, b, 8 : self.planes + 8, :] = flags[b] * parts[b][0, :, :]
            self.update[b, :, :] = flags[b] * parts[b][1, :, :]

    def steps(self, which):
        for index in which:
            carry, gain = self.weights[index]
            old, new = (self.now, 1 - self.now)
            for x in range(0, self.planes, 8):
                centers = [self.state[old, b, x + 8 : x + 16, :] for b in range(3)]
                before, after = self.beside_z(centers)
                for b, center in enumerate(centers):
                    face = [self.base[7 * b + k, x : x + 8, :] for k in range(7)]
                    beside = face[0] * self.state[old, b, x + 7 : x + 15, :] + face[1] * self.state[old, b, x + 9 : x + 17, :]
                    beside = beside + (face[2] * before[b] + face[3] * after[b])
                    beside = beside + (face[4] * roll(center, 1) + face[5] * roll(center, -1))
                    change = carry * self.update[b, x : x + 8, :] + gain * (face[6] - center + beside)
                    self.update[b, x : x + 8, :] = change
                    self.state[new, b, x + 8 : x + 16, :] = center + change
            self.now = new

    def leave(self, out):
        out[0, :, :] = self.state[self.now, 1, 8 : self.planes + 8, :]
        out[1, :, :] = self.update[1, :, :]


def solve_first(count, pos, low, here, high, base, out, half, state, update):
    has_low, has_high = inside_z(pos[1], count)
    level = Coarsest(base, state, update)
    level.start((low, here, high), half, (has_low, 1.0, has_high))
    level.steps(range(1, SOLVE[0]))
    level.leave(out)


def solve_next(count, pos, base, low, here, high, out, state, update):
    has_low, has_high = inside_z(pos[1], count)
    level = Coarsest(base, state, update)
    level.resume((low, here, high), (has_low, 1.0, has_high))
    level.steps(range(SOLVE[0], SOLVE[1]))
    level.leave(out)


def finish(cells, pos, base, low, here, high, prev2, next2, *refs):
    gx, gz = (pos[0], pos[1])
    (s2, g2, *coefs2), (s1, g1, *coefs1), (s0, g0, *coefs0) = (refs[0:8], refs[8:16], refs[16:24])
    out, state, update3, coarse2, temp, start2, start1, start0, middle, update = refs[24:]
    bz0 = out.shape[1]
    bz1, bz2 = (bz0 // 2, bz0 // 4)
    has_low, has_high = inside_z(gz, cells[0][1] // bz0)
    level = Coarsest(base, state, update3)
    level.resume((low, here, high), (has_low, 1.0, has_high))
    level.steps(range(SOLVE[1], COARSE_ITERS))
    last = level.now

    bx2 = 2
    rows = bz2 + 8
    cell = lax.broadcasted_iota(jnp.int32, (LANES, LANES), 0)
    lane = lax.broadcasted_iota(jnp.int32, (LANES, LANES), 1)
    pick = jnp.where((cell & 15) == (lane >> 3), 1.0, 0.0)
    z3 = (rows_of(rows) >> 1) - 2
    keep = (lanes_of(rows) >> 4) == (z3 & 7)
    columns = [state[last, b, pl.ds(gx + 6, 8), :] for b in range(3)]
    for q in range(5):
        picked = [column[q : q + 1, :] for column in columns]
        wide = jnp.where(z3 < 0, picked[0], jnp.where(z3 < 8, picked[1], picked[2]))
        coarse2[q * rows : (q + 1) * rows, :] = jnp.where(keep, wide, 0.0)
    spread_out = jnp.dot(coarse2[...], pick, precision=lax.Precision.HIGHEST, preferred_element_type=jnp.float32)
    coarse2[...] = spread_out

    start, own = (start2, 4)
    row, count = (ROW - 4, rows)
    zero = jnp.zeros((8, LANES), jnp.float32)
    for q in range(5):
        for p in (own - 4 + 2 * q, own - 3 + 2 * q):
            start[p, 8:16, :] = zero
            start[p, ROW + bz2 : ROW + bz2 + 8, :] = zero
            if q == 2:
                guess = g2[p, row : row + count, :]
            else:
                guess = (prev2 if q < 2 else next2)[p if q < 2 else p - own - bx2, 4 : 4 + count, :]
            start[p, row : row + count, :] = guess + coarse2[q * rows : (q + 1) * rows, :]
    level = Level(2, gx, gz, (bx2, bz2), cells[2], own, (None, *coefs2))

    bx1, base1 = (4, 24)

    def to_level_1(p, value):
        q = 2 * (p - own) + 4
        temp[pl.ds(0, value.shape[0], stride=2), :] = value
        temp[pl.ds(1, value.shape[0], stride=2), :] = value
        for r in (q, q + 1):
            if 1 <= r <= 10:
                start1[r, base1 - 4 : base1 + bz1 + 4, :] = (
                    g1[r, base1 - 4 : base1 + bz1 + 4, :] + temp[0 : bz1 + 8, :]
                )

    for r in range(1, 11):
        start1[r, base1 - 8 : base1, :] = zero
        start1[r, base1 + bz1 : base1 + bz1 + 8, :] = zero
    level.up(s2, start, middle, update, to_level_1, range(own - 2, own + 4), row, count, ROW - 2, bz2 + 4)
    level = Level(1, gx, gz, (bx1, bz1), cells[1], 4, (None, *coefs1), base1)
    row, count = (base1 - 4, bz1 + 8)

    bx0 = out.shape[0]
    for r in range(1, 13):
        start0[r, 8:16, :] = zero
        start0[r, ROW + bz0 : ROW + bz0 + 8, :] = zero

    def to_level_0(p, value):
        q = 2 * (p - 4) + 3
        temp[pl.ds(0, value.shape[0], stride=2), :] = value
        temp[pl.ds(1, value.shape[0], stride=2), :] = value
        for r in (q, q + 1):
            if r in (1, 12):
                for part in range(2):
                    begin = ROW + part * (bz0 // 2)
                    start0[r, begin : begin + bz0 // 2, :] = (prev2 if r == 1 else next2)[4 + part, :, :] + temp[
                        begin - ROW + 4 : begin - ROW + 4 + bz0 // 2, :
                    ]
                continue
            start0[r, ROW - 4 : ROW + bz0 + 4, :] = g0[r, ROW - 4 : ROW + bz0 + 4, :] + temp[0 : bz0 + 8, :]

    level.up(s1, start1, middle, update, to_level_0, range(3, 9), row, count, base1 - 2, bz1 + 4)
    level = Level(0, gx, gz, (bx0, bz0), cells[0], 3, (None, *coefs0))

    def to_out(p, value):
        out[p - 3, :, :] = value

    level.up(s0, start0, middle, update, to_out, range(3, 11), ROW - 4, bz0 + 8, ROW, bz0)


def f32(*shape):
    return jax.ShapeDtypeStruct(shape, jnp.float32)


def scratch(*shape):
    return pltpu.VMEM(shape, jnp.float32)


def call(kernel, name, outs, scratches, *args, aliases={}):
    smem = pl.BlockSpec(memory_space=pltpu.SMEM)
    limit = 4 * 2**20 + sum(4 * math.prod(ref.shape) for ref in [*scratches, *outs, *args])
    vmem = pl.BlockSpec(memory_space=pltpu.VMEM)
    return pl.pallas_call(
        kernel,
        name=name,
        out_shape=outs,
        in_specs=[smem if arg.dtype == jnp.int32 else vmem for arg in args],
        out_specs=[vmem] * len(outs),
        scratch_shapes=scratches,
        input_output_aliases=aliases,
        compiler_params=pltpu.CompilerParams(vmem_limit_bytes=limit),
    )(*args)


def shift(array, axis, by):
    devices = lax.axis_size(axis)
    return lax.ppermute(array, axis, [(i, i + by) for i in range(devices) if 0 <= i + by < devices])


def turn(array, axis, by):
    devices = lax.axis_size(axis)
    return lax.ppermute(array, axis, [(i, (i + by) % devices) for i in range(devices)])


def on_device(right_side, conductivity):
    nx, nz = (lax.axis_size("gx"), lax.axis_size("gz"))
    bx, bz = right_side.shape[0:2]
    cells = [(nx * bx >> level, nz * bz >> level) for level in range(4)]
    pos = jnp.stack([lax.axis_index("gx"), lax.axis_index("gz")]).astype(jnp.int32)
    for_next = jnp.concatenate([right_side[bx - 2 :], conductivity[bx - 3 :]])
    for_prev = jnp.concatenate([right_side[:2], conductivity[:3]])
    low, high = (shift(for_next, "gx", 1), shift(for_prev, "gx", -1))
    planes = bx + 6
    to_high, to_low = call(
        edge_rows_0, "edge_rows_0", [f32(planes, 8, LANES)] * 2, [], right_side, conductivity, low, high
    )
    z_low, z_high = (turn(to_high, "gz", 1), turn(to_low, "gz", -1))
    window = (planes, bz + 32, LANES)
    half1 = (bx // 2 + 2, bz // 2 + 8, LANES)
    arrays = call(
        functools.partial(inner_0, cells[0]),
        "inner_0",
        [f32(*window)] * 10 + [f32(bx // 2, bz // 2, LANES), f32(*half1)],
        [scratch(bz + 16, LANES)],
        pos,
        right_side,
        conductivity,
        low,
        high,
    )
    *arrays, for_next, for_prev = call(
        functools.partial(outer_0, cells[0]),
        "outer_0",
        [f32(*array.shape) for array in arrays] + [f32(bx // 2 + 1, bz // 2, LANES)] * 2,
        [scratch(16, LANES)],
        pos,
        z_low,
        z_high,
        *arrays,
        aliases={i + 3: i for i in range(12)},
    )
    kept0 = (arrays[0], arrays[2], *arrays[3:9])

    bx, bz = (bx // 2, bz // 2)
    low, high = (shift(for_next, "gx", 1), shift(for_prev, "gx", -1))
    to_high, to_low = call(
        edge_rows_1, "edge_rows_1", [f32(3 * bx + 2, 16, LANES)] * 2, [], low, for_next, high
    )
    z_low, z_high = (turn(to_high, "gz", 1), turn(to_low, "gz", -1))
    window = (3 * bx, bz + 48, LANES)
    half2 = (bx // 2 + 4, bz // 2 + 16, LANES)
    arrays1 = call(
        functools.partial(inner_1, cells[1]),
        "inner_1",
        [f32(*window)] * 10 + [f32(*half2)] * 2,
        [scratch(bz, LANES)],
        pos,
        for_next,
        low,
        high,
    )
    *arrays1, for_next, for_prev = call(
        functools.partial(outer_1, cells[1]),
        "outer_1",
        [f32(*array.shape) for array in arrays1] + [f32(2, bz // 2 + 16, LANES)] * 2,
        [scratch(16, LANES)],
        pos,
        z_low,
        z_high,
        *arrays1,
        aliases={i + 3: i for i in range(12)},
    )
    kept1 = (arrays1[0], arrays1[2], *arrays1[3:9])

    bx, bz = (bx // 2, bz // 2)
    prev, next_ = (shift(for_next, "gx", 1), shift(for_prev, "gx", -1))
    window = (bx + 8, bz + 32, LANES)
    *kept2, row3, for_next, for_prev = call(
        functools.partial(down_2, cells[2]),
        "down_2",
        [f32(*window)] * 8 + [f32(nx, 2, LANES)] + [f32(LATE, bz + 16, LANES)] * 2,
        [scratch(*window)] * 2 + [scratch(bz + 16, LANES)],
        pos,
        prev,
        for_next,
        next_,
        arrays[2],
    )

    here = lax.all_to_all(row3, "gx", 0, 0, tiled=True)
    low, high = (turn(here, "gz", 1), turn(here, "gz", -1))
    blocks = [part.reshape(2 * nx, LANES) for part in (low, here, high)]
    solving = [scratch(2, 3, nx + 16, LANES), scratch(3, nx, LANES)]
    for_next, _ = lax.optimization_barrier((for_next, here))
    prev2 = shift(for_next, "gx", 1)
    base, here = call(
        functools.partial(solve_first, nz),
        "solve_first",
        [f32(21, nx, LANES), f32(2, nx, LANES)],
        [scratch(3, nx + 16, LANES)] + solving,
        pos,
        *blocks,
    )
    low, high = (turn(here, "gz", 1), turn(here, "gz", -1))
    for_prev, _ = lax.optimization_barrier((for_prev, here))
    next2 = shift(for_prev, "gx", -1)
    (here,) = call(
        functools.partial(solve_next, nz), "solve_next", [f32(2, nx, LANES)], solving, pos, base, low, here, high
    )
    low, high = (turn(here, "gz", 1), turn(here, "gz", -1))

    bx, bz = right_side.shape[0:2]
    window = (bx + 6, bz + 32, LANES)
    work = solving + [scratch(5 * (bz // 4 + 8), LANES), scratch(bz + 32, LANES)]
    work += [scratch(bx // 4 + 8, bz // 4 + 32, LANES), scratch(bx // 2 + 8, bz // 2 + 48, LANES)]
    work += [scratch(*window)] * 3
    (result,) = call(
        functools.partial(finish, cells), "finish", [f32(*right_side.shape)], work, pos, base, low, here, high,
        prev2, next2, *kept2, *kept1, *kept0,
    )
    return result


def solution(mesh):
    return jax.shard_map(
        on_device,
        mesh=mesh,
        in_specs=(P("gx", "gz", None), P("gx", "gz", None)),
        out_specs=P("gx", "gz", None),
        check_vma=False,
    )
```

```python
import functools
import math

import jax
import jax.numpy as jnp
from jax import lax
from jax.experimental import pallas as pl
from jax.experimental.pallas import tpu as pltpu
from jax.sharding import PartitionSpec as P

COARSE_ITERS = 20
LANES = 128
ROW = 16
LATE = 8
SOLVE = (8, 16)


def cheb_weights(count, lower, upper):
    theta = 0.5 * (upper + lower)
    delta = 0.5 * (upper - lower)
    sigma = theta / delta
    rho_prev = 1.0 / sigma
    carry_terms = [0.0]
    gain_terms = [1.0 / theta]
    for step in range(1, count):
        rho_next = 1.0 / (2.0 * sigma - rho_prev)
        carry_terms.append(rho_next * rho_prev)
        gain_terms.append(2.0 * rho_next / delta)
        rho_prev = rho_next
    return (carry_terms, gain_terms)


(_, CARRY), (GAIN_FIRST, GAIN) = cheb_weights(2, 0.25, 2.0)


def lanes_of(rows):
    return lax.broadcasted_iota(jnp.int32, (rows, LANES), 1)


def rows_of(rows):
    return lax.broadcasted_iota(jnp.int32, (rows, LANES), 0)


def roll(value, shift, axis=1):
    return pltpu.roll(value, shift % value.shape[axis], axis)


def pair_sum(value, stride):
    odd = (lanes_of(value.shape[0]) & stride) != 0
    return value + jnp.where(odd, roll(value, stride), roll(value, -stride))


class Level:
    def __init__(self, level, gx, gz, brick, cells, first_plane, refs, first_row=ROW):
        self.stride, self.scale, self.first_row = (2**level, 0.25**level, first_row)
        self.gx, self.gz, self.brick, self.cells, self.first_plane = (gx, gz, brick, cells, first_plane)
        self.half, self.fx, self.fz, self.left, self.right, self.diag, self.inverse = refs

    def coefs(self, planes, row, count, source, first):
        half, stride = (self.half, self.stride)
        lane = lanes_of(count)
        in_left, in_right = (lane >= stride, lane < LANES - stride)
        here = rows_of(count) + (row - self.first_row + self.gz * self.brick[1])
        inside_rows = jnp.where((here >= 0) & (here < self.cells[1]), 1.0 / self.scale, 0.0)
        for p in planes:
            center = half[p, row : row + count, :]
            before = center + half[p - 1, row : row + count, :]
            after = center + half[p + 1, row : row + count, :]
            low = center + half[p, row - 1 : row - 1 + count, :]
            high = center + half[p, row + 1 : row + 1 + count, :]
            left = center + jnp.where(in_left, roll(center, stride), 0.0)
            right = center + jnp.where(in_right, roll(center, -stride), 0.0)
            diagonal = ((before + after) + (low + high)) + (left + right)
            plane = p - self.first_plane + self.gx * self.brick[0]
            inside = jnp.where(jnp.logical_and(plane >= 0, plane < self.cells[0]), 1.0, 0.0)
            inverse = (inside * inside_rows) * jnp.where(diagonal > 0.0, 1.0 / diagonal, 0.0)
            self.fx[p, row : row + count, :] = before
            self.fz[p, row : row + count, :] = low
            self.fz[p, row + 1 : row + 1 + count, :] = high
            self.left[p, row : row + count, :] = jnp.where(in_left, left, 0.0)
            self.right[p, row : row + count, :] = jnp.where(in_right, right, 0.0)
            self.diag[p, row : row + count, :] = diagonal
            self.inverse[p, row : row + count, :] = inverse
            first[p, row : row + count, :] = GAIN_FIRST * (inverse * source[p, row : row + count, :])
        self.fx[planes[-1] + 1, row : row + count, :] = after

    def remainder(self, source, guess, p, row, count):
        center = guess[p, row : row + count, :]
        beside = (
            self.fx[p, row : row + count, :] * guess[p - 1, row : row + count, :]
            + self.fx[p + 1, row : row + count, :] * guess[p + 1, row : row + count, :]
        )
        beside = beside + (
            self.fz[p, row : row + count, :] * guess[p, row - 1 : row - 1 + count, :]
            + self.fz[p, row + 1 : row + 1 + count, :] * guess[p, row + 1 : row + 1 + count, :]
        )
        beside = beside + (
            self.left[p, row : row + count, :] * roll(center, self.stride)
            + self.right[p, row : row + count, :] * roll(center, -self.stride)
        )
        applied = self.diag[p, row : row + count, :] * center - beside
        return source[p, row : row + count, :] - self.scale * applied

    def second_down(self, source, first, out, planes, row, count):
        for p in planes:
            rest = self.remainder(source, first, p, row, count)
            start = first[p, row : row + count, :]
            update = CARRY * start + GAIN * (self.inverse[p, row : row + count, :] * rest)
            out[p, row : row + count, :] = start + update

    def restricted_remainder(self, source, guess, temp, planes, row, rows):
        parts = []
        for p in planes[::2]:
            both = self.remainder(source, guess, p, row, rows) + self.remainder(source, guess, p + 1, row, rows)
            temp[0:rows, :] = pair_sum(both, self.stride)
            parts.append(0.125 * (temp[pl.ds(0, rows // 2, stride=2), :] + temp[pl.ds(1, rows // 2, stride=2), :]))
        return parts

    def up(self, source, start, middle, update, out, planes, row, count, out_row, out_count):
        for p in range(planes[0] - 1, planes[-1] + 2):
            first = GAIN_FIRST * (
                self.inverse[p, row : row + count, :] * self.remainder(source, start, p, row, count)
            )
            update[p, row : row + count, :] = first
            middle[p, row : row + count, :] = start[p, row : row + count, :] + first
        for p in planes:
            second = CARRY * update[p, out_row : out_row + out_count, :] + GAIN * (
                self.inverse[p, out_row : out_row + out_count, :]
                * self.remainder(source, middle, p, out_row, out_count)
            )
            out(p, middle[p, out_row : out_row + out_count, :] + second)


def restricted(half, temp, stride, planes, row, rows):
    parts = []
    for p in planes[::2]:
        both = half[p, row : row + rows, :] + half[p + 1, row : row + rows, :]
        temp[0:rows, :] = pair_sum(both, stride)
        parts.append(0.125 * (temp[pl.ds(0, rows // 2, stride=2), :] + temp[pl.ds(1, rows // 2, stride=2), :]))
    return parts


def first_iterate(source, half, p, count, level, stride):
    center = half[p][1 : 1 + count]
    lane = lanes_of(count)
    diagonal = 6.0 * center + half[p - 1][1 : 1 + count] + half[p + 1][1 : 1 + count]
    diagonal = diagonal + half[p][0:count] + half[p][2 : 2 + count]
    diagonal = diagonal + jnp.where(lane >= stride, roll(center, stride), 0.0)
    diagonal = diagonal + jnp.where(lane < LANES - stride, roll(center, -stride), 0.0)
    inverse = jnp.where(diagonal > 0.0, 1.0 / (0.25**level * diagonal), 0.0)
    return GAIN_FIRST * source * inverse


def cut(half_ref, planes, row, count):
    return [half_ref[p, row : row + count, :] for p in planes]


def edge_rows_0(source, cond, low, high, to_high, to_low):
    bx, bz = source.shape[0:2]
    zero = jnp.zeros((4, LANES), jnp.float32)
    for rows, out in ((slice(bz - 4, bz), to_high), (slice(0, 4), to_low)):
        out[0, 0:4, :] = zero
        out[bx + 5, 0:4, :] = zero
        for p in range(2):
            out[p + 1, 0:4, :] = low[p, rows, :]
            out[p + bx + 3, 0:4, :] = high[p, rows, :]
        for p in range(3):
            out[p, 4:8, :] = low[p + 2, rows, :]
            out[p + bx + 3, 4:8, :] = high[p + 2, rows, :]
        for p in range(bx):
            out[p + 3, 0:4, :] = source[p, rows, :]
            out[p + 3, 4:8, :] = cond[p, rows, :]


def inner_0(cells, source, cond, low, high, win_s, win_h, guess, fx, fz, left, right, diag, inverse, first, next_source, next_half, temp):
    gx, gz = (lax.axis_index("gx"), lax.axis_index("gz"))
    bx, bz = source.shape[0:2]
    planes, end = (bx + 6, ROW + bz)
    zero = jnp.zeros((8, LANES), jnp.float32)
    for p in range(planes):
        for edge in (8, end, end + 8):
            win_s[p, edge : edge + 8, :] = zero
            win_h[p, edge : edge + 8, :] = zero
            guess[p, edge : edge + 8, :] = zero
            first[p, edge : edge + 8, :] = zero
    for p in range(bx):
        win_s[p + 3, ROW:end, :] = source[p, :, :]
        win_h[p + 3, ROW:end, :] = 0.5 * cond[p, :, :]
    for p in range(2):
        win_s[p + 1, ROW:end, :] = low[p, :, :]
        win_s[p + bx + 3, ROW:end, :] = high[p, :, :]
    for p in range(3):
        win_h[p, ROW:end, :] = 0.5 * low[p + 2, :, :]
        win_h[p + bx + 3, ROW:end, :] = 0.5 * high[p + 2, :, :]
    level = Level(0, gx, gz, (bx, bz), cells, 3, (win_h, fx, fz, left, right, diag, inverse))
    level.coefs(range(1, planes - 1), ROW, bz, win_s, first)
    level.second_down(win_s, first, guess, range(2, planes - 2), ROW, bz)
    for p, value in enumerate(level.restricted_remainder(win_s, guess, temp, range(3, 3 + bx), ROW, bz)):
        next_source[p, :, :] = value
    for p, value in enumerate(restricted(win_h, temp, 1, range(1, planes - 1), ROW - 8, bz + 16)):
        next_half[p, :, :] = value


def outer_0(cells, z_low, z_high, *refs):
    win_s, win_h, guess, fx, fz, left, right, diag, inverse, first, next_source, next_half = refs[12:24]
    to_next, to_prev, temp = refs[24:]
    gx, gz = (lax.axis_index("gx"), lax.axis_index("gz"))
    planes, bx, bz = (win_s.shape[0], win_s.shape[0] - 6, win_s.shape[1] - 32)
    end = ROW + bz
    has_low, has_high = inside_z(gz, cells[1] // bz)
    for p in range(planes):
        win_s[p, ROW - 4 : ROW, :] = z_low[p, 0:4, :]
        win_s[p, end : end + 4, :] = z_high[p, 0:4, :]
        win_h[p, ROW - 4 : ROW, :] = (0.5 * has_low) * z_low[p, 4:8, :]
        win_h[p, end : end + 4, :] = (0.5 * has_high) * z_high[p, 4:8, :]
    level = Level(0, gx, gz, (bx, bz), cells, 3, (win_h, fx, fz, left, right, diag, inverse))
    strips = ROW - 4, end - 4
    for row in strips:
        level.coefs(range(1, planes - 1), row, 8, win_s, first)
    for row in strips:
        level.second_down(win_s, first, guess, range(2, planes - 2), row, 8)
    own = bz // 2
    for row, at in ((ROW, 0), (end - 8, own - 4)):
        for p, value in enumerate(level.restricted_remainder(win_s, guess, temp, range(3, 3 + bx), row, 8)):
            next_source[p, at : at + 4, :] = value
        for p, value in enumerate(restricted(win_h, temp, 1, range(1, planes - 1), row - 8 if row == ROW else end, 8)):
            at_half = 0 if row == ROW else own + 4
            next_half[p, at_half : at_half + 4, :] = value
    odd = (lanes_of(own) & 1) == 1
    padded = cut(next_half, range(bx // 2 + 2), 3, own + 2)
    last = bx // 2 - 1
    for p in range(bx // 2):
        mixed = jnp.where(odd, padded[p + 1][1 : 1 + own], next_source[p, :, :])
        to_next[p, :, :] = mixed
        to_prev[p, :, :] = mixed
    for p, out in ((0, to_next), (last, to_prev)):
        iterate = first_iterate(next_source[p, :, :], padded, p + 1, own, 1, 2)
        out[p, :, :] = jnp.where(odd, padded[p + 1][1 : 1 + own], iterate)


def inside_z(gz, count):
    return (jnp.where(gz > 0, 1.0, 0.0), jnp.where(gz < count - 1, 1.0, 0.0))


def edge_rows_1(low, to_next, to_prev, high, to_high, to_low):
    bx, rows = low.shape[0:2]
    own = [to_prev] * (bx - 1) + [to_next]
    planes = [(low, p) for p in range(bx)] + list(zip(own, range(bx))) + [(high, p) for p in range(bx)]
    for at, (part, p) in enumerate(planes):
        to_high[at, :, :] = part[p, rows - 16 : rows, :]
        to_low[at, :, :] = part[p, 0:16, :]


def unpack_1(win_s, win_h, p, start, rows, mixed):
    odd = (lanes_of(rows) & 1) == 1
    win_s[p, start : start + rows, :] = jnp.where(odd, roll(mixed, 1), mixed)
    win_h[p, start : start + rows, :] = jnp.where(odd, mixed, roll(mixed, -1))


def inner_1(cells, source, half, low, high, win_s, win_h, guess, fx, fz, left, right, diag, inverse, first, next_source, next_half, temp):
    gx, gz = (lax.axis_index("gx"), lax.axis_index("gz"))
    bx, bz = source.shape[0:2]
    planes, base = (3 * bx, 24)
    end = base + bz
    zero = jnp.zeros((8, LANES), jnp.float32)
    for p in range(bx):
        unpack_1(win_s, win_h, p, base, bz, low[p, :, :])
        unpack_1(win_s, win_h, 2 * bx + p, base, bz, high[p, :, :])
        win_s[bx + p, base:end, :] = source[p, :, :]
        win_h[bx + p, base:end, :] = half[p + 1, 4 : 4 + bz, :]
    for p in (0, planes - 1):
        first[p, base:end, :] = win_s[p, base:end, :]
    for p in range(planes):
        for ref in (win_s, win_h, first, guess):
            for row in (0, 8, 16, end, end + 8, end + 16):
                ref[p, row : row + 8, :] = zero
    level = Level(1, gx, gz, (bx, bz), cells, bx, (win_h, fx, fz, left, right, diag, inverse), base)
    level.coefs(range(1, planes - 1), base, bz, win_s, first)
    level.second_down(win_s, first, guess, range(1, planes - 1), base, bz)
    next_source[...] = jnp.zeros(next_source.shape, jnp.float32)
    own = bz // 2
    for p, value in enumerate(level.restricted_remainder(win_s, guess, temp, range(bx - 2, 2 * bx + 2), base, bz)):
        next_source[p + 1, 8 : 8 + own, :] = value
    for p, value in enumerate(restricted(win_h, temp, 2, range(planes), base, bz)):
        next_half[p, 8 : 8 + own, :] = value


def outer_1(cells, z_low, z_high, *refs):
    win_s, win_h, guess, fx, fz, left, right, diag, inverse, first, next_source, next_half = refs[12:24]
    to_next, to_prev, temp = refs[24:]
    gx, gz = (lax.axis_index("gx"), lax.axis_index("gz"))
    planes, base = (win_s.shape[0], 24)
    bx, bz = (planes // 3, win_s.shape[1] - 48)
    end = base + bz
    has_low, has_high = inside_z(gz, cells[1] // bz)
    for start, ref, inside in ((base - 16, z_low, has_low), (end, z_high, has_high)):
        for p in range(planes):
            unpack_1(win_s, win_h, p, start, 16, inside * ref[p, :, :])
        for p in (0, planes - 1):
            first[p, start : start + 16, :] = win_s[p, start : start + 16, :]
    level = Level(1, gx, gz, (bx, bz), cells, bx, (win_h, fx, fz, left, right, diag, inverse), base)
    strips = base - 12, end - 4
    for row in strips:
        level.coefs(range(1, planes - 1), row, 16, win_s, first)
    for row in strips:
        level.second_down(win_s, first, guess, range(1, planes - 1), row, 16)
    for row in strips:
        at = (row - base + 16) // 2
        for p, value in enumerate(level.restricted_remainder(win_s, guess, temp, range(bx - 2, 2 * bx + 2), row, 16)):
            next_source[p + 1, at : at + 8, :] = value
    for row in (base - 16, end):
        at = (row - base + 16) // 2
        for p, value in enumerate(restricted(win_h, temp, 2, range(planes), row, 16)):
            next_half[p, at : at + 8, :] = value
    lane = lanes_of(next_source.shape[1]) & 3

    def pair(p):
        mixed = jnp.where(lane == 0, next_source[p, :, :], next_half[p, :, :])
        mixed = jnp.where(lane == 2, next_source[p + 1, :, :], mixed)
        return jnp.where(lane == 3, next_half[p + 1, :, :], mixed)

    middle = pair(2)
    to_next[0, :, :] = pair(0)
    to_next[1, :, :] = middle
    to_prev[0, :, :] = middle
    to_prev[1, :, :] = pair(4)


def spread(mixed, which):
    only = jnp.where((lanes_of(mixed.shape[0]) & 3) == which, mixed, 0.0)
    only = roll(only, -which) if which else only
    twice = only + roll(only, 1)
    return twice + roll(twice, 2)


def down_2(cells, prev, here, next_, guess0, win_s, guess, fx, fz, left, right, diag, inverse, message, to_next, to_prev, win_h, first, temp):
    gx, gz = (lax.axis_index("gx"), lax.axis_index("gz"))
    bx, bz = (2, prev.shape[1] - 16)
    own, planes = (4, 10)
    end = ROW + bz
    zero = jnp.zeros((8, LANES), jnp.float32)
    pairs = (prev, 0), (prev, 1), (here, 1), (next_, 0), (next_, 1)
    for q, (part, at) in enumerate(pairs):
        mixed = part[at, :, :]
        for p in range(2):
            win_s[2 * q + p, 8 : end + 8, :] = spread(mixed, 2 * p)
            win_h[2 * q + p, 8 : end + 8, :] = spread(mixed, 2 * p + 1)
    for p in range(planes):
        for ref in (win_s, win_h, first):
            ref[p, 0:8, :] = zero
            ref[p, end + 8 : end + 16, :] = zero
    level = Level(2, gx, gz, (bx, bz), cells, own, (win_h, fx, fz, left, right, diag, inverse))
    row, count = (ROW - 8, bz + 16)
    level.coefs(range(own - 3, own + 5), row, count, win_s, first)
    level.second_down(win_s, first, guess, range(own - 2, own + 4), row, count)
    for out, begin in ((to_next, own - 2), (to_prev, own)):
        for p in range(4):
            out[p, :, :] = guess[begin + p, row : row + count, :]
        far = guess0.shape[0] - 5 if out is to_next else 4
        for p in range(4, out.shape[0]):
            begin0 = ROW + ((p - 4) & 1) * count
            out[p, :, :] = guess0[far, begin0 : begin0 + count, :]
    sources = level.restricted_remainder(win_s, guess, temp, range(own, own + bx), ROW, bz)
    halves = restricted(win_h, temp, 4, range(own, own + bx), ROW, bz)
    rows = bz // 2
    cell = lax.broadcasted_iota(jnp.int32, (LANES, LANES), 0)
    lane = lax.broadcasted_iota(jnp.int32, (LANES, LANES), 1)
    pick = jnp.where(((cell >> 3) == (lane & 15)) & ((cell & 7) == 0), 1.0, 0.0)
    keep = (lanes_of(rows) >> 4) == rows_of(rows)
    both = jnp.concatenate([sources[0], halves[0]])
    both = jnp.dot(both, pick, precision=lax.Precision.HIGHEST, preferred_element_type=jnp.float32)
    for at in range(2):
        dense = jnp.sum(jnp.where(keep, both[at * rows : (at + 1) * rows], 0.0), axis=0, keepdims=True)
        for device in range(message.shape[0]):
            message[device, at : at + 1, :] = dense


class Coarsest:
    def __init__(self, base, state, update):
        self.base, self.state, self.update, self.now = (base, state, update, 0)
        self.planes = update.shape[1]
        self.weights = list(zip(*cheb_weights(COARSE_ITERS, 0.02, 2.0)))
        zero = jnp.zeros((8, LANES), jnp.float32)
        for buffer in range(2):
            for b in range(3):
                state[buffer, b, 0:8, :] = zero
                state[buffer, b, self.planes + 8 : self.planes + 16, :] = zero

    def beside_z(self, values):
        lane = lanes_of(values[0].shape[0])
        ahead, back = ([roll(v, 16) for v in values], [roll(v, -16) for v in values])
        before = [jnp.where(lane < 16, ahead[max(b - 1, 0)], ahead[b]) for b in range(3)]
        after = [jnp.where(lane >= LANES - 16, back[min(b + 1, 2)], back[b]) for b in range(3)]
        return before, after

    def start(self, parts, half, flags):
        planes, zero = (self.planes, jnp.zeros((8, LANES), jnp.float32))
        gain = self.weights[0][1]
        for b in range(3):
            half[b, 0:8, :] = zero
            half[b, planes + 8 : planes + 16, :] = zero
            half[b, 8 : planes + 8, :] = flags[b] * parts[b][pl.ds(1, planes, stride=2), :]
        lane = lanes_of(8)
        in_left, in_right = ((lane & 15) > 0, (lane & 15) < 15)
        for x in range(0, planes, 8):
            centers = [half[b, x + 8 : x + 16, :] for b in range(3)]
            before, after = self.beside_z(centers)
            for b, center in enumerate(centers):
                faces = [
                    center + half[b, x + 7 : x + 15, :],
                    center + half[b, x + 9 : x + 17, :],
                    center + before[b],
                    center + after[b],
                    center + jnp.where(in_left, roll(center, 1), 0.0),
                    center + jnp.where(in_right, roll(center, -1), 0.0),
                ]
                diagonal = faces[0] + faces[1] + faces[2] + faces[3] + faces[4] + faces[5]
                inverse = flags[b] * jnp.where(diagonal > 0.0, 1.0 / diagonal, 0.0)
                faces = [face * inverse for face in faces]
                faces[4] = jnp.where(in_left, faces[4], 0.0)
                faces[5] = jnp.where(in_right, faces[5], 0.0)
                for which, face in enumerate(faces):
                    self.base[7 * b + which, x : x + 8, :] = face
                scaled = 64.0 * (parts[b][pl.ds(2 * x, 8, stride=2), :] * inverse)
                self.base[7 * b + 6, x : x + 8, :] = scaled
                self.update[b, x : x + 8, :] = gain * scaled
                self.state[self.now, b, x + 8 : x + 16, :] = gain * scaled

    def resume(self, parts, flags):
        for b in range(3):
            self.state[self.now, b, 8 : self.planes + 8, :] = flags[b] * parts[b][0, :, :]
            self.update[b, :, :] = flags[b] * parts[b][1, :, :]

    def steps(self, which, keep):
        for index in which:
            blocks = range(3) if keep or index < which[-1] else (1,)
            carry, gain = self.weights[index]
            old, new = (self.now, 1 - self.now)
            for x in range(0, self.planes, 8):
                centers = [self.state[old, b, x + 8 : x + 16, :] for b in range(3)]
                before, after = self.beside_z(centers)
                for b in blocks:
                    center = centers[b]
                    face = [self.base[7 * b + k, x : x + 8, :] for k in range(7)]
                    beside = face[0] * self.state[old, b, x + 7 : x + 15, :] + face[1] * self.state[old, b, x + 9 : x + 17, :]
                    beside = beside + (face[2] * before[b] + face[3] * after[b])
                    beside = beside + (face[4] * roll(center, 1) + face[5] * roll(center, -1))
                    change = carry * self.update[b, x : x + 8, :] + gain * (face[6] - center + beside)
                    self.update[b, x : x + 8, :] = change
                    self.state[new, b, x + 8 : x + 16, :] = center + change
            self.now = new

    def leave(self, out):
        out[0, :, :] = self.state[self.now, 1, 8 : self.planes + 8, :]
        out[1, :, :] = self.update[1, :, :]


def solve_first(count, low, here, high, base, out, half, state, update):
    has_low, has_high = inside_z(lax.axis_index("gz"), count)
    level = Coarsest(base, state, update)
    level.start((low, here, high), half, (has_low, 1.0, has_high))
    level.steps(range(1, SOLVE[0]), False)
    level.leave(out)


def solve_next(count, base, low, here, high, out, state, update):
    has_low, has_high = inside_z(lax.axis_index("gz"), count)
    level = Coarsest(base, state, update)
    level.resume((low, here, high), (has_low, 1.0, has_high))
    level.steps(range(SOLVE[0], SOLVE[1]), False)
    level.leave(out)


def finish(cells, base, low, here, high, prev2, next2, *refs):
    gx, gz = (lax.axis_index("gx"), lax.axis_index("gz"))
    (s2, g2, *coefs2), (s1, g1, *coefs1), (s0, g0, *coefs0) = (refs[0:8], refs[8:16], refs[16:24])
    out, state, update3, coarse2, temp, start2, start1, start0, middle, update = refs[24:]
    bz0 = out.shape[1]
    bz1, bz2 = (bz0 // 2, bz0 // 4)
    has_low, has_high = inside_z(gz, cells[0][1] // bz0)
    level = Coarsest(base, state, update3)
    level.resume((low, here, high), (has_low, 1.0, has_high))
    level.steps(range(SOLVE[1], COARSE_ITERS), True)
    last = level.now

    bx2 = 2
    rows = bz2 + 8
    cell = lax.broadcasted_iota(jnp.int32, (LANES, LANES), 0)
    lane = lax.broadcasted_iota(jnp.int32, (LANES, LANES), 1)
    pick = jnp.where((cell & 15) == (lane >> 3), 1.0, 0.0)
    z3 = (rows_of(rows) >> 1) - 2
    keep = (lanes_of(rows) >> 4) == (z3 & 7)
    columns = [state[last, b, pl.ds(gx + 6, 8), :] for b in range(3)]
    for q in range(5):
        picked = [column[q : q + 1, :] for column in columns]
        wide = jnp.where(z3 < 0, picked[0], jnp.where(z3 < 8, picked[1], picked[2]))
        coarse2[q * rows : (q + 1) * rows, :] = jnp.where(keep, wide, 0.0)
    spread_out = jnp.dot(coarse2[...], pick, precision=lax.Precision.HIGHEST, preferred_element_type=jnp.float32)
    coarse2[...] = spread_out

    start, own = (start2, 4)
    row, count = (ROW - 4, rows)
    zero = jnp.zeros((8, LANES), jnp.float32)
    for q in range(5):
        for p in (own - 4 + 2 * q, own - 3 + 2 * q):
            start[p, 8:16, :] = zero
            start[p, ROW + bz2 : ROW + bz2 + 8, :] = zero
            if q == 2:
                guess = g2[p, row : row + count, :]
            else:
                guess = (prev2 if q < 2 else next2)[p if q < 2 else p - own - bx2, 4 : 4 + count, :]
            start[p, row : row + count, :] = guess + coarse2[q * rows : (q + 1) * rows, :]
    level = Level(2, gx, gz, (bx2, bz2), cells[2], own, (None, *coefs2))

    bx1, base1 = (4, 24)

    def to_level_1(p, value):
        q = 2 * (p - own) + 4
        temp[pl.ds(0, value.shape[0], stride=2), :] = value
        temp[pl.ds(1, value.shape[0], stride=2), :] = value
        for r in (q, q + 1):
            if 1 <= r <= 10:
                start1[r, base1 - 4 : base1 + bz1 + 4, :] = (
                    g1[r, base1 - 4 : base1 + bz1 + 4, :] + temp[0 : bz1 + 8, :]
                )

    for r in range(1, 11):
        start1[r, base1 - 8 : base1, :] = zero
        start1[r, base1 + bz1 : base1 + bz1 + 8, :] = zero
    level.up(s2, start, middle, update, to_level_1, range(own - 2, own + 4), row, count, ROW - 2, bz2 + 4)
    level = Level(1, gx, gz, (bx1, bz1), cells[1], 4, (None, *coefs1), base1)
    row, count = (base1 - 4, bz1 + 8)

    bx0 = out.shape[0]
    for r in range(1, 13):
        start0[r, 8:16, :] = zero
        start0[r, ROW + bz0 : ROW + bz0 + 8, :] = zero

    def to_level_0(p, value):
        q = 2 * (p - 4) + 3
        temp[pl.ds(0, value.shape[0], stride=2), :] = value
        temp[pl.ds(1, value.shape[0], stride=2), :] = value
        for r in (q, q + 1):
            if r in (1, 12):
                for part in range(2):
                    begin = ROW + part * (bz0 // 2)
                    start0[r, begin : begin + bz0 // 2, :] = (prev2 if r == 1 else next2)[4 + part, :, :] + temp[
                        begin - ROW + 4 : begin - ROW + 4 + bz0 // 2, :
                    ]
                continue
            start0[r, ROW - 4 : ROW + bz0 + 4, :] = g0[r, ROW - 4 : ROW + bz0 + 4, :] + temp[0 : bz0 + 8, :]

    level.up(s1, start1, middle, update, to_level_0, range(3, 9), row, count, base1 - 2, bz1 + 4)
    level = Level(0, gx, gz, (bx0, bz0), cells[0], 3, (None, *coefs0))

    def to_out(p, value):
        out[p - 3, :, :] = value

    level.up(s0, start0, middle, update, to_out, range(3, 11), ROW - 4, bz0 + 8, ROW, bz0)


def f32(*shape):
    return jax.ShapeDtypeStruct(shape, jnp.float32)


def scratch(*shape):
    return pltpu.VMEM(shape, jnp.float32)


def call(kernel, name, outs, scratches, *args, aliases={}):
    limit = 4 * 2**20 + sum(4 * math.prod(ref.shape) for ref in [*scratches, *outs, *args])
    vmem = pl.BlockSpec(memory_space=pltpu.VMEM)
    return pl.pallas_call(
        kernel,
        name=name,
        out_shape=outs,
        in_specs=[vmem] * len(args),
        out_specs=[vmem] * len(outs),
        scratch_shapes=scratches,
        input_output_aliases=aliases,
        compiler_params=pltpu.CompilerParams(vmem_limit_bytes=limit),
    )(*args)


def shift(array, axis, by):
    devices = lax.axis_size(axis)
    return lax.ppermute(array, axis, [(i, i + by) for i in range(devices) if 0 <= i + by < devices])


def turn(array, axis, by):
    devices = lax.axis_size(axis)
    return lax.ppermute(array, axis, [(i, (i + by) % devices) for i in range(devices)])


def on_device(right_side, conductivity):
    nx, nz = (lax.axis_size("gx"), lax.axis_size("gz"))
    bx, bz = right_side.shape[0:2]
    cells = [(nx * bx >> level, nz * bz >> level) for level in range(4)]
    for_next = jnp.concatenate([right_side[bx - 2 :], conductivity[bx - 3 :]])
    for_prev = jnp.concatenate([right_side[:2], conductivity[:3]])
    low, high = (shift(for_next, "gx", 1), shift(for_prev, "gx", -1))
    planes = bx + 6
    to_high, to_low = call(
        edge_rows_0, "edge_rows_0", [f32(planes, 8, LANES)] * 2, [], right_side, conductivity, low, high
    )
    z_low, z_high = (turn(to_high, "gz", 1), turn(to_low, "gz", -1))
    window = (planes, bz + 32, LANES)
    half1 = (bx // 2 + 2, bz // 2 + 8, LANES)
    arrays = call(
        functools.partial(inner_0, cells[0]),
        "inner_0",
        [f32(*window)] * 10 + [f32(bx // 2, bz // 2, LANES), f32(*half1)],
        [scratch(bz + 16, LANES)],
        right_side,
        conductivity,
        low,
        high,
    )
    *arrays, for_next, for_prev = call(
        functools.partial(outer_0, cells[0]),
        "outer_0",
        [f32(*array.shape) for array in arrays] + [f32(bx // 2, bz // 2, LANES)] * 2,
        [scratch(16, LANES)],
        z_low,
        z_high,
        *arrays,
        aliases={i + 2: i for i in range(12)},
    )
    kept0 = (arrays[0], arrays[2], *arrays[3:9])

    bx, bz = (bx // 2, bz // 2)
    low, high = (shift(for_next, "gx", 1), shift(for_prev, "gx", -1))
    to_high, to_low = call(
        edge_rows_1, "edge_rows_1", [f32(3 * bx, 16, LANES)] * 2, [], low, for_next, for_prev, high
    )
    z_low, z_high = (turn(to_high, "gz", 1), turn(to_low, "gz", -1))
    window = (3 * bx, bz + 48, LANES)
    half2 = (bx // 2 + 4, bz // 2 + 16, LANES)
    arrays1 = call(
        functools.partial(inner_1, cells[1]),
        "inner_1",
        [f32(*window)] * 10 + [f32(*half2)] * 2,
        [scratch(bz, LANES)],
        arrays[10],
        arrays[11],
        low,
        high,
    )
    *arrays1, for_next, for_prev = call(
        functools.partial(outer_1, cells[1]),
        "outer_1",
        [f32(*array.shape) for array in arrays1] + [f32(2, bz // 2 + 16, LANES)] * 2,
        [scratch(16, LANES)],
        z_low,
        z_high,
        *arrays1,
        aliases={i + 2: i for i in range(12)},
    )
    kept1 = (arrays1[0], arrays1[2], *arrays1[3:9])

    bx, bz = (bx // 2, bz // 2)
    prev, next_ = (shift(for_next, "gx", 1), shift(for_prev, "gx", -1))
    window = (bx + 8, bz + 32, LANES)
    *kept2, row3, for_next, for_prev = call(
        functools.partial(down_2, cells[2]),
        "down_2",
        [f32(*window)] * 8 + [f32(nx, 2, LANES)] + [f32(LATE, bz + 16, LANES)] * 2,
        [scratch(*window)] * 2 + [scratch(bz + 16, LANES)],
        prev,
        for_next,
        next_,
        arrays[2],
    )

    here = lax.all_to_all(row3, "gx", 0, 0, tiled=True)
    low, high = (turn(here, "gz", 1), turn(here, "gz", -1))
    blocks = [part.reshape(2 * nx, LANES) for part in (low, here, high)]
    solving = [scratch(2, 3, nx + 16, LANES), scratch(3, nx, LANES)]
    for_next, _ = lax.optimization_barrier((for_next, here))
    prev2 = shift(for_next, "gx", 1)
    base, here = call(
        functools.partial(solve_first, nz),
        "solve_first",
        [f32(21, nx, LANES), f32(2, nx, LANES)],
        [scratch(3, nx + 16, LANES)] + solving,
        *blocks,
    )
    low, high = (turn(here, "gz", 1), turn(here, "gz", -1))
    for_prev, _ = lax.optimization_barrier((for_prev, here))
    next2 = shift(for_prev, "gx", -1)
    (here,) = call(
        functools.partial(solve_next, nz), "solve_next", [f32(2, nx, LANES)], solving, base, low, here, high
    )
    low, high = (turn(here, "gz", 1), turn(here, "gz", -1))

    bx, bz = right_side.shape[0:2]
    window = (bx + 6, bz + 32, LANES)
    work = solving + [scratch(5 * (bz // 4 + 8), LANES), scratch(bz + 32, LANES)]
    work += [scratch(bx // 4 + 8, bz // 4 + 32, LANES), scratch(bx // 2 + 8, bz // 2 + 48, LANES)]
    work += [scratch(*window)] * 3
    (result,) = call(
        functools.partial(finish, cells), "finish", [f32(*right_side.shape)], work, base, low, here, high,
        prev2, next2, *kept2, *kept1, *kept0,
    )
    return result


def solution(mesh):
    return jax.shard_map(
        on_device,
        mesh=mesh,
        in_specs=(P("gx", "gz", None), P("gx", "gz", None)),
        out_specs=P("gx", "gz", None),
        check_vma=False,
    )
```

```python
import functools
import math

import jax
import jax.numpy as jnp
from jax import lax
from jax.experimental import pallas as pl
from jax.experimental.pallas import tpu as pltpu
from jax.sharding import PartitionSpec as P

COARSE_ITERS = 20
LANES = 128
ROW = 16
EDGE = 13
LATE = 3
WIDTHS = ((22, 48), (14, 32), (6, 16))
SOLVE = (8, 16)


def cheb_weights(count, lower, upper):
    theta = 0.5 * (upper + lower)
    delta = 0.5 * (upper - lower)
    sigma = theta / delta
    rho_prev = 1.0 / sigma
    carry_terms = [0.0]
    gain_terms = [1.0 / theta]
    for step in range(1, count):
        rho_next = 1.0 / (2.0 * sigma - rho_prev)
        carry_terms.append(rho_next * rho_prev)
        gain_terms.append(2.0 * rho_next / delta)
        rho_prev = rho_next
    return (carry_terms, gain_terms)


(_, CARRY), (GAIN_FIRST, GAIN) = cheb_weights(2, 0.25, 2.0)


def lanes_of(rows):
    return lax.broadcasted_iota(jnp.int32, (rows, LANES), 1)


def rows_of(rows):
    return lax.broadcasted_iota(jnp.int32, (rows, LANES), 0)


def roll(value, shift, axis=1):
    return pltpu.roll(value, shift % value.shape[axis], axis)


def pair_sum(value, stride):
    odd = (lanes_of(value.shape[0]) & stride) != 0
    return value + jnp.where(odd, roll(value, stride), roll(value, -stride))


class Level:
    def __init__(self, level, gx, gz, brick, cells, first_plane, refs, first_row=ROW):
        self.stride, self.scale, self.first_row = (2**level, 0.25**level, first_row)
        self.gx, self.gz, self.brick, self.cells, self.first_plane = (gx, gz, brick, cells, first_plane)
        self.half, self.fx, self.fz, self.left, self.right, self.diag, self.inverse = refs

    def coefs(self, planes, row, count, source, first):
        half, stride = (self.half, self.stride)
        lane = lanes_of(count)
        in_left, in_right = (lane >= stride, lane < LANES - stride)
        here = rows_of(count) + (row - self.first_row + self.gz * self.brick[1])
        inside_rows = jnp.where((here >= 0) & (here < self.cells[1]), 1.0 / self.scale, 0.0)
        for p in planes:
            center = half[p, row : row + count, :]
            before = center + half[p - 1, row : row + count, :]
            after = center + half[p + 1, row : row + count, :]
            low = center + half[p, row - 1 : row - 1 + count, :]
            high = center + half[p, row + 1 : row + 1 + count, :]
            left = center + jnp.where(in_left, roll(center, stride), 0.0)
            right = center + jnp.where(in_right, roll(center, -stride), 0.0)
            diagonal = ((before + after) + (low + high)) + (left + right)
            plane = p - self.first_plane + self.gx * self.brick[0]
            inside = jnp.where(jnp.logical_and(plane >= 0, plane < self.cells[0]), 1.0, 0.0)
            inverse = (inside * inside_rows) * jnp.where(diagonal > 0.0, 1.0 / diagonal, 0.0)
            self.fx[p, row : row + count, :] = before
            self.fz[p, row : row + count, :] = low
            self.fz[p, row + 1 : row + 1 + count, :] = high
            self.left[p, row : row + count, :] = jnp.where(in_left, left, 0.0)
            self.right[p, row : row + count, :] = jnp.where(in_right, right, 0.0)
            self.diag[p, row : row + count, :] = diagonal
            self.inverse[p, row : row + count, :] = inverse
            first[p, row : row + count, :] = GAIN_FIRST * (inverse * source[p, row : row + count, :])
        self.fx[planes[-1] + 1, row : row + count, :] = after

    def remainder(self, source, guess, p, row, count):
        center = guess[p, row : row + count, :]
        beside = (
            self.fx[p, row : row + count, :] * guess[p - 1, row : row + count, :]
            + self.fx[p + 1, row : row + count, :] * guess[p + 1, row : row + count, :]
        )
        beside = beside + (
            self.fz[p, row : row + count, :] * guess[p, row - 1 : row - 1 + count, :]
            + self.fz[p, row + 1 : row + 1 + count, :] * guess[p, row + 1 : row + 1 + count, :]
        )
        beside = beside + (
            self.left[p, row : row + count, :] * roll(center, self.stride)
            + self.right[p, row : row + count, :] * roll(center, -self.stride)
        )
        applied = self.diag[p, row : row + count, :] * center - beside
        return source[p, row : row + count, :] - self.scale * applied

    def second_down(self, source, first, out, planes, row, count):
        for p in planes:
            rest = self.remainder(source, first, p, row, count)
            start = first[p, row : row + count, :]
            update = CARRY * start + GAIN * (self.inverse[p, row : row + count, :] * rest)
            out[p, row : row + count, :] = start + update

    def restricted_remainder(self, source, guess, temp, planes, row, rows):
        parts = []
        for p in planes[::2]:
            both = self.remainder(source, guess, p, row, rows) + self.remainder(source, guess, p + 1, row, rows)
            temp[0:rows, :] = pair_sum(both, self.stride)
            parts.append(0.125 * (temp[pl.ds(0, rows // 2, stride=2), :] + temp[pl.ds(1, rows // 2, stride=2), :]))
        return parts

    def up(self, source, start, middle, update, out, planes, row, count, out_row, out_count):
        for p in range(planes[0] - 1, planes[-1] + 2):
            first = GAIN_FIRST * (
                self.inverse[p, row : row + count, :] * self.remainder(source, start, p, row, count)
            )
            update[p, row : row + count, :] = first
            middle[p, row : row + count, :] = start[p, row : row + count, :] + first
        for p in planes:
            second = CARRY * update[p, out_row : out_row + out_count, :] + GAIN * (
                self.inverse[p, out_row : out_row + out_count, :]
                * self.remainder(source, middle, p, out_row, out_count)
            )
            out(p, middle[p, out_row : out_row + out_count, :] + second)


def restricted(half, temp, stride, planes, row, rows):
    parts = []
    for p in planes[::2]:
        both = half[p, row : row + rows, :] + half[p + 1, row : row + rows, :]
        temp[0:rows, :] = pair_sum(both, stride)
        parts.append(0.125 * (temp[pl.ds(0, rows // 2, stride=2), :] + temp[pl.ds(1, rows // 2, stride=2), :]))
    return parts


def first_iterate(source, half, p, count, level, stride):
    center = half[p][1 : 1 + count]
    lane = lanes_of(count)
    diagonal = 6.0 * center + half[p - 1][1 : 1 + count] + half[p + 1][1 : 1 + count]
    diagonal = diagonal + half[p][0:count] + half[p][2 : 2 + count]
    diagonal = diagonal + jnp.where(lane >= stride, roll(center, stride), 0.0)
    diagonal = diagonal + jnp.where(lane < LANES - stride, roll(center, -stride), 0.0)
    inverse = jnp.where(diagonal > 0.0, 1.0 / (0.25**level * diagonal), 0.0)
    return GAIN_FIRST * source * inverse


def cut(half_ref, planes, row, count):
    return [half_ref[p, row : row + count, :] for p in planes]


def edge_spec_0(bx):
    spec, at = ([], 0)
    for p in range(bx + 6):
        away = max(3 - p, p - bx - 2, 0)
        spec.append((p, at, 3 - away, 4 - away))
        at += 7 - 2 * away
    return spec, at


def edge_rows_0(source, cond, low, high, to_high, to_low):
    bx, bz = source.shape[0:2]
    spec, length = edge_spec_0(bx)
    for p, at, few, many in spec:
        if p < 3:
            (part, q), (other, r) = ((low, p - 1), (low, p + 2))
        elif p < bx + 3:
            (part, q), (other, r) = ((source, p - 3), (cond, p - 3))
        else:
            (part, q), (other, r) = ((high, p - bx - 3), (high, p - bx - 1))
        if few:
            to_high[at : at + few, :] = part[q, bz - few : bz, :]
            to_low[at : at + few, :] = part[q, 0:few, :]
        to_high[at + few : at + few + many, :] = other[r, bz - many : bz, :]
        to_low[at + few : at + few + many, :] = other[r, 0:many, :]
    rest = to_high.shape[0] - length
    for out in (to_high, to_low):
        out[length : length + rest, :] = jnp.zeros((rest, LANES), jnp.float32)


def inner_0(cells, source, cond, low, high, win_s, win_h, guess, fx, fz, left, right, diag, inverse, first, next_source, next_half, temp):
    gx, gz = (lax.axis_index("gx"), lax.axis_index("gz"))
    bx, bz = source.shape[0:2]
    planes, end = (bx + 6, ROW + bz)
    zero = jnp.zeros((8, LANES), jnp.float32)
    for p in range(planes):
        for edge in (8, end, end + 8):
            win_s[p, edge : edge + 8, :] = zero
            win_h[p, edge : edge + 8, :] = zero
            guess[p, edge : edge + 8, :] = zero
            first[p, edge : edge + 8, :] = zero
    for p in range(bx):
        win_s[p + 3, ROW:end, :] = source[p, :, :]
        win_h[p + 3, ROW:end, :] = 0.5 * cond[p, :, :]
    for p in range(2):
        win_s[p + 1, ROW:end, :] = low[p, :, :]
        win_s[p + bx + 3, ROW:end, :] = high[p, :, :]
    for p in range(3):
        win_h[p, ROW:end, :] = 0.5 * low[p + 2, :, :]
        win_h[p + bx + 3, ROW:end, :] = 0.5 * high[p + 2, :, :]
    level = Level(0, gx, gz, (bx, bz), cells, 3, (win_h, fx, fz, left, right, diag, inverse))
    level.coefs(range(1, planes - 1), ROW, bz, win_s, first)
    level.second_down(win_s, first, guess, range(2, planes - 2), ROW, bz)
    for p, value in enumerate(level.restricted_remainder(win_s, guess, temp, range(3, 3 + bx), ROW, bz)):
        next_source[p, :, :] = value
    for p, value in enumerate(restricted(win_h, temp, 1, range(1, planes - 1), ROW - 8, bz + 16)):
        next_half[p, :, :] = value


def outer_0(cells, z_low, z_high, *refs):
    win_s, win_h, guess, fx, fz, left, right, diag, inverse, first, next_source, next_half = refs[12:24]
    to_next, to_prev, temp = refs[24:]
    gx, gz = (lax.axis_index("gx"), lax.axis_index("gz"))
    planes, bx, bz = (win_s.shape[0], win_s.shape[0] - 6, win_s.shape[1] - 32)
    end = ROW + bz
    has_low, has_high = inside_z(gz, cells[1] // bz)
    for p, at, few, many in edge_spec_0(bx)[0]:
        if few:
            win_s[p, ROW - few : ROW, :] = z_low[at : at + few, :]
            win_s[p, end : end + few, :] = z_high[at : at + few, :]
        win_h[p, ROW - many : ROW, :] = (0.5 * has_low) * z_low[at + few : at + few + many, :]
        win_h[p, end : end + many, :] = (0.5 * has_high) * z_high[at + few : at + few + many, :]
    level = Level(0, gx, gz, (bx, bz), cells, 3, (win_h, fx, fz, left, right, diag, inverse))
    strips = ROW - 4, end - 4
    for row in strips:
        level.coefs(range(1, planes - 1), row, 8, win_s, first)
    for row in strips:
        level.second_down(win_s, first, guess, range(2, planes - 2), row, 8)
    own = bz // 2
    for row, at in ((ROW, 0), (end - 8, own - 4)):
        for p, value in enumerate(level.restricted_remainder(win_s, guess, temp, range(3, 3 + bx), row, 8)):
            next_source[p, at : at + 4, :] = value
        for p, value in enumerate(restricted(win_h, temp, 1, range(1, planes - 1), row - 8 if row == ROW else end, 8)):
            at_half = 0 if row == ROW else own + 4
            next_half[p, at_half : at_half + 4, :] = value
    odd = (lanes_of(own) & 1) == 1
    padded = cut(next_half, range(bx // 2 + 2), 3, own + 2)
    last = bx // 2 - 1
    for p in range(bx // 2):
        mixed = jnp.where(odd, padded[p + 1][1 : 1 + own], next_source[p, :, :])
        to_next[p, :, :] = mixed
        to_prev[p, :, :] = mixed
    for p, out in ((0, to_next), (last, to_prev)):
        iterate = first_iterate(next_source[p, :, :], padded, p + 1, own, 1, 2)
        out[p, :, :] = jnp.where(odd, padded[p + 1][1 : 1 + own], iterate)


def inside_z(gz, count):
    return (jnp.where(gz > 0, 1.0, 0.0), jnp.where(gz < count - 1, 1.0, 0.0))


def edge_rows_1(low, to_next, to_prev, high, to_high, to_low):
    bx, rows = low.shape[0:2]
    own = [to_prev] * (bx - 1) + [to_next]
    planes = [(low, p) for p in range(bx)] + list(zip(own, range(bx))) + [(high, p) for p in range(bx)]
    for at, (part, p) in enumerate(planes):
        to_high[EDGE * at : EDGE * (at + 1), :] = part[p, rows - EDGE : rows, :]
        to_low[EDGE * at : EDGE * (at + 1), :] = part[p, 0:EDGE, :]
    used, whole = (EDGE * len(planes), to_high.shape[0])
    for out in (to_high, to_low):
        out[used:whole, :] = jnp.zeros((whole - used, LANES), jnp.float32)


def unpack_1(win_s, win_h, p, start, rows, mixed):
    odd = (lanes_of(rows) & 1) == 1
    win_s[p, start : start + rows, :] = jnp.where(odd, roll(mixed, 1), mixed)
    win_h[p, start : start + rows, :] = jnp.where(odd, mixed, roll(mixed, -1))


def inner_1(cells, source, half, low, high, win_s, win_h, guess, fx, fz, left, right, diag, inverse, first, next_source, next_half, temp):
    gx, gz = (lax.axis_index("gx"), lax.axis_index("gz"))
    bx, bz = source.shape[0:2]
    planes, base = (3 * bx, 24)
    end = base + bz
    zero = jnp.zeros((8, LANES), jnp.float32)
    for p in range(bx):
        unpack_1(win_s, win_h, p, base, bz, low[p, :, :])
        unpack_1(win_s, win_h, 2 * bx + p, base, bz, high[p, :, :])
        win_s[bx + p, base:end, :] = source[p, :, :]
        win_h[bx + p, base:end, :] = half[p + 1, 4 : 4 + bz, :]
    for p in (0, planes - 1):
        first[p, base:end, :] = win_s[p, base:end, :]
    for p in range(planes):
        for ref in (win_s, win_h, first, guess):
            for row in (0, 8, 16, end, end + 8, end + 16):
                ref[p, row : row + 8, :] = zero
    level = Level(1, gx, gz, (bx, bz), cells, bx, (win_h, fx, fz, left, right, diag, inverse), base)
    level.coefs(range(1, planes - 1), base, bz, win_s, first)
    level.second_down(win_s, first, guess, range(1, planes - 1), base, bz)
    next_source[...] = jnp.zeros(next_source.shape, jnp.float32)
    own = bz // 2
    for p, value in enumerate(level.restricted_remainder(win_s, guess, temp, range(bx - 2, 2 * bx + 2), base, bz)):
        next_source[p + 1, 8 : 8 + own, :] = value
    for p, value in enumerate(restricted(win_h, temp, 2, range(planes), base, bz)):
        next_half[p, 8 : 8 + own, :] = value


def outer_1(cells, z_low, z_high, *refs):
    win_s, win_h, guess, fx, fz, left, right, diag, inverse, first, next_source, next_half = refs[12:24]
    to_next, to_prev, temp = refs[24:]
    gx, gz = (lax.axis_index("gx"), lax.axis_index("gz"))
    planes, base = (win_s.shape[0], 24)
    bx, bz = (planes // 3, win_s.shape[1] - 48)
    end = base + bz
    has_low, has_high = inside_z(gz, cells[1] // bz)
    for start, ref, inside in ((base - EDGE, z_low, has_low), (end, z_high, has_high)):
        for p in range(planes):
            unpack_1(win_s, win_h, p, start, EDGE, inside * ref[EDGE * p : EDGE * (p + 1), :])
        for p in (0, planes - 1):
            first[p, start : start + EDGE, :] = win_s[p, start : start + EDGE, :]
    level = Level(1, gx, gz, (bx, bz), cells, bx, (win_h, fx, fz, left, right, diag, inverse), base)
    strips = base - 12, end - 4
    for row in strips:
        level.coefs(range(1, planes - 1), row, 16, win_s, first)
    for row in strips:
        level.second_down(win_s, first, guess, range(1, planes - 1), row, 16)
    for row in strips:
        at = (row - base + 16) // 2
        for p, value in enumerate(level.restricted_remainder(win_s, guess, temp, range(bx - 2, 2 * bx + 2), row, 16)):
            next_source[p + 1, at : at + 8, :] = value
    for row in (base - 16, end):
        at = (row - base + 16) // 2
        for p, value in enumerate(restricted(win_h, temp, 2, range(planes), row, 16)):
            next_half[p, at : at + 8, :] = value
    lane = lanes_of(next_source.shape[1]) & 3

    def pair(p):
        mixed = jnp.where(lane == 0, next_source[p, :, :], next_half[p, :, :])
        mixed = jnp.where(lane == 2, next_source[p + 1, :, :], mixed)
        return jnp.where(lane == 3, next_half[p + 1, :, :], mixed)

    middle = pair(2)
    to_next[0, :, :] = pair(0)
    to_next[1, :, :] = middle
    to_prev[0, :, :] = middle
    to_prev[1, :, :] = pair(4)


def spread(mixed, which):
    only = jnp.where((lanes_of(mixed.shape[0]) & 3) == which, mixed, 0.0)
    only = roll(only, -which) if which else only
    twice = only + roll(only, 1)
    return twice + roll(twice, 2)


def down_2(cells, prev, here, next_, guess0, win_s, guess, fx, fz, left, right, diag, inverse, message, to_next, to_prev, win_h, first, temp):
    gx, gz = (lax.axis_index("gx"), lax.axis_index("gz"))
    bx, bz = (2, prev.shape[1] - 16)
    own, planes = (4, 10)
    end = ROW + bz
    zero = jnp.zeros((8, LANES), jnp.float32)
    pairs = (prev, 0), (prev, 1), (here, 1), (next_, 0), (next_, 1)
    for q, (part, at) in enumerate(pairs):
        mixed = part[at, :, :]
        for p in range(2):
            win_s[2 * q + p, 8 : end + 8, :] = spread(mixed, 2 * p)
            win_h[2 * q + p, 8 : end + 8, :] = spread(mixed, 2 * p + 1)
    for p in range(planes):
        for ref in (win_s, win_h, first):
            ref[p, 0:8, :] = zero
            ref[p, end + 8 : end + 16, :] = zero
    level = Level(2, gx, gz, (bx, bz), cells, own, (win_h, fx, fz, left, right, diag, inverse))
    row, count = (ROW - 8, bz + 16)
    level.coefs(range(own - 3, own + 5), row, count, win_s, first)
    level.second_down(win_s, first, guess, range(own - 2, own + 4), row, count)
    lane = lanes_of(count) & 3
    for out, begin in ((to_next, own - 2), (to_prev, own)):
        mixed = guess[begin, row : row + count, :]
        for p in range(1, 4):
            mixed = jnp.where(lane == p, guess[begin + p, row : row + count, :], mixed)
        out[0, :, :] = mixed
        far = guess0.shape[0] - 5 if out is to_next else 4
        for p in range(1, LATE):
            begin0 = ROW + (p - 1) * count
            out[p, :, :] = guess0[far, begin0 : begin0 + count, :]
    sources = level.restricted_remainder(win_s, guess, temp, range(own, own + bx), ROW, bz)
    halves = restricted(win_h, temp, 4, range(own, own + bx), ROW, bz)
    rows = bz // 2
    cell = lax.broadcasted_iota(jnp.int32, (LANES, LANES), 0)
    lane = lax.broadcasted_iota(jnp.int32, (LANES, LANES), 1)
    pick = jnp.where(((cell >> 3) == (lane & 15)) & ((cell & 7) == 0), 1.0, 0.0)
    keep = (lanes_of(rows) >> 4) == rows_of(rows)
    both = jnp.concatenate([sources[0], halves[0]])
    both = jnp.dot(both, pick, precision=lax.Precision.HIGHEST, preferred_element_type=jnp.float32)
    for at in range(2):
        dense = jnp.sum(jnp.where(keep, both[at * rows : (at + 1) * rows], 0.0), axis=0, keepdims=True)
        for device in range(message.shape[0]):
            message[device, at : at + 1, :] = dense


def part_of_x(which, planes):
    before, width = WIDTHS[which]
    width = min(width, planes)
    return (jnp.clip(lax.axis_index("gx") - before, 0, planes - width), width)


class Coarsest:
    def __init__(self, base, state, update):
        self.base, self.state, self.update, self.now = (base, state, update, 0)
        self.planes = update.shape[1]
        self.weights = list(zip(*cheb_weights(COARSE_ITERS, 0.02, 2.0)))
        zero = jnp.zeros((8, LANES), jnp.float32)
        for buffer in range(2):
            for b in range(3):
                state[buffer, b, 0:8, :] = zero
                state[buffer, b, self.planes + 8 : self.planes + 16, :] = zero

    def beside_z(self, values):
        lane = lanes_of(values[0].shape[0])
        ahead, back = ([roll(v, 16) for v in values], [roll(v, -16) for v in values])
        before = [jnp.where(lane < 16, ahead[max(b - 1, 0)], ahead[b]) for b in range(3)]
        after = [jnp.where(lane >= LANES - 16, back[min(b + 1, 2)], back[b]) for b in range(3)]
        return before, after

    def start(self, parts, half, flags):
        planes, zero = (self.planes, jnp.zeros((8, LANES), jnp.float32))
        gain = self.weights[0][1]
        for b in range(3):
            half[b, 0:8, :] = zero
            half[b, planes + 8 : planes + 16, :] = zero
            half[b, 8 : planes + 8, :] = flags[b] * parts[b][pl.ds(1, planes, stride=2), :]
        lane = lanes_of(8)
        in_left, in_right = ((lane & 15) > 0, (lane & 15) < 15)
        for x in range(0, planes, 8):
            centers = [half[b, x + 8 : x + 16, :] for b in range(3)]
            before, after = self.beside_z(centers)
            for b, center in enumerate(centers):
                faces = [
                    center + half[b, x + 7 : x + 15, :],
                    center + half[b, x + 9 : x + 17, :],
                    center + before[b],
                    center + after[b],
                    center + jnp.where(in_left, roll(center, 1), 0.0),
                    center + jnp.where(in_right, roll(center, -1), 0.0),
                ]
                diagonal = faces[0] + faces[1] + faces[2] + faces[3] + faces[4] + faces[5]
                inverse = flags[b] * jnp.where(diagonal > 0.0, 1.0 / diagonal, 0.0)
                faces = [face * inverse for face in faces]
                faces[4] = jnp.where(in_left, faces[4], 0.0)
                faces[5] = jnp.where(in_right, faces[5], 0.0)
                for which, face in enumerate(faces):
                    self.base[7 * b + which, x : x + 8, :] = face
                scaled = 64.0 * (parts[b][pl.ds(2 * x, 8, stride=2), :] * inverse)
                self.base[7 * b + 6, x : x + 8, :] = scaled
                self.update[b, x : x + 8, :] = gain * scaled
                self.state[self.now, b, x + 8 : x + 16, :] = gain * scaled

    def resume(self, parts, flags):
        for b in range(3):
            self.state[self.now, b, 8 : self.planes + 8, :] = flags[b] * parts[b][0, :, :]
            self.update[b, :, :] = flags[b] * parts[b][1, :, :]

    def steps(self, which, keep):
        for index in which:
            blocks = range(3) if keep or index < which[-1] else (1,)
            carry, gain = self.weights[index]
            old, new = (self.now, 1 - self.now)
            for x in range(0, self.planes, 8):
                centers = [self.state[old, b, x + 8 : x + 16, :] for b in range(3)]
                before, after = self.beside_z(centers)
                for b in blocks:
                    center = centers[b]
                    face = [self.base[7 * b + k, x : x + 8, :] for k in range(7)]
                    beside = face[0] * self.state[old, b, x + 7 : x + 15, :] + face[1] * self.state[old, b, x + 9 : x + 17, :]
                    beside = beside + (face[2] * before[b] + face[3] * after[b])
                    beside = beside + (face[4] * roll(center, 1) + face[5] * roll(center, -1))
                    change = carry * self.update[b, x : x + 8, :] + gain * (face[6] - center + beside)
                    self.update[b, x : x + 8, :] = change
                    self.state[new, b, x + 8 : x + 16, :] = center + change
            self.now = new

    def leave(self, out, skip):
        count = out.shape[1]
        out[0, :, :] = self.state[self.now, 1, pl.ds(skip + 8, count), :]
        out[1, :, :] = self.update[1, pl.ds(skip, count), :]


def window_3(planes, whole, out):
    first, width = part_of_x(0, planes)
    out[...] = whole[pl.ds(2 * first, 2 * width), :]


def narrow(planes, base, second, third):
    first = part_of_x(0, planes)[0]
    for which, out in ((1, second), (2, third)):
        begin, width = part_of_x(which, planes)
        for k in range(base.shape[0]):
            out[k, :, :] = base[k, pl.ds(begin - first, width), :]


def solve_first(count, planes, low, here, high, base, out, half, state, update):
    has_low, has_high = inside_z(lax.axis_index("gz"), count)
    level = Coarsest(base, state, update)
    level.start((low, here, high), half, (has_low, 1.0, has_high))
    level.steps(range(1, SOLVE[0]), False)
    level.leave(out, part_of_x(1, planes)[0] - part_of_x(0, planes)[0])


def solve_next(count, planes, base, low, here, high, out, state, update):
    has_low, has_high = inside_z(lax.axis_index("gz"), count)
    level = Coarsest(base, state, update)
    level.resume((low, here, high), (has_low, 1.0, has_high))
    level.steps(range(SOLVE[0], SOLVE[1]), False)
    level.leave(out, part_of_x(2, planes)[0] - part_of_x(1, planes)[0])


def finish(cells, base, low, here, high, prev2, next2, *refs):
    gx, gz = (lax.axis_index("gx"), lax.axis_index("gz"))
    (s2, g2, *coefs2), (s1, g1, *coefs1), (s0, g0, *coefs0) = (refs[0:8], refs[8:16], refs[16:24])
    out, state, update3, coarse2, temp, start2, start1, start0, middle, update = refs[24:]
    bz0 = out.shape[1]
    bz1, bz2 = (bz0 // 2, bz0 // 4)
    has_low, has_high = inside_z(gz, cells[0][1] // bz0)
    level = Coarsest(base, state, update3)
    level.resume((low, here, high), (has_low, 1.0, has_high))
    level.steps(range(SOLVE[1], COARSE_ITERS), True)
    last = level.now

    bx2 = 2
    rows = bz2 + 8
    cell = lax.broadcasted_iota(jnp.int32, (LANES, LANES), 0)
    lane = lax.broadcasted_iota(jnp.int32, (LANES, LANES), 1)
    pick = jnp.where((cell & 15) == (lane >> 3), 1.0, 0.0)
    z3 = (rows_of(rows) >> 1) - 2
    keep = (lanes_of(rows) >> 4) == (z3 & 7)
    local = gx - part_of_x(2, cells[3][0])[0]
    columns = [state[last, b, pl.ds(local + 6, 8), :] for b in range(3)]
    for q in range(5):
        picked = [column[q : q + 1, :] for column in columns]
        wide = jnp.where(z3 < 0, picked[0], jnp.where(z3 < 8, picked[1], picked[2]))
        coarse2[q * rows : (q + 1) * rows, :] = jnp.where(keep, wide, 0.0)
    spread_out = jnp.dot(coarse2[...], pick, precision=lax.Precision.HIGHEST, preferred_element_type=jnp.float32)
    coarse2[...] = spread_out

    start, own = (start2, 4)
    row, count = (ROW - 4, rows)
    zero = jnp.zeros((8, LANES), jnp.float32)
    for q in range(5):
        for p in (own - 4 + 2 * q, own - 3 + 2 * q):
            start[p, 8:16, :] = zero
            start[p, ROW + bz2 : ROW + bz2 + 8, :] = zero
            if q == 2:
                guess = g2[p, row : row + count, :]
            else:
                guess = spread((prev2 if q < 2 else next2)[0, 4 : 4 + count, :], p if q < 2 else p - own - bx2)
            start[p, row : row + count, :] = guess + coarse2[q * rows : (q + 1) * rows, :]
    level = Level(2, gx, gz, (bx2, bz2), cells[2], own, (None, *coefs2))

    bx1, base1 = (4, 24)

    def to_level_1(p, value):
        q = 2 * (p - own) + 4
        temp[pl.ds(0, value.shape[0], stride=2), :] = value
        temp[pl.ds(1, value.shape[0], stride=2), :] = value
        for r in (q, q + 1):
            if 1 <= r <= 10:
                start1[r, base1 - 4 : base1 + bz1 + 4, :] = (
                    g1[r, base1 - 4 : base1 + bz1 + 4, :] + temp[0 : bz1 + 8, :]
                )

    for r in range(1, 11):
        start1[r, base1 - 8 : base1, :] = zero
        start1[r, base1 + bz1 : base1 + bz1 + 8, :] = zero
    level.up(s2, start, middle, update, to_level_1, range(own - 2, own + 4), row, count, ROW - 2, bz2 + 4)
    level = Level(1, gx, gz, (bx1, bz1), cells[1], 4, (None, *coefs1), base1)
    row, count = (base1 - 4, bz1 + 8)

    bx0 = out.shape[0]
    for r in range(1, 13):
        start0[r, 8:16, :] = zero
        start0[r, ROW + bz0 : ROW + bz0 + 8, :] = zero

    def to_level_0(p, value):
        q = 2 * (p - 4) + 3
        temp[pl.ds(0, value.shape[0], stride=2), :] = value
        temp[pl.ds(1, value.shape[0], stride=2), :] = value
        for r in (q, q + 1):
            if r in (1, 12):
                for part in range(2):
                    begin = ROW + part * (bz0 // 2)
                    start0[r, begin : begin + bz0 // 2, :] = (prev2 if r == 1 else next2)[1 + part, :, :] + temp[
                        begin - ROW + 4 : begin - ROW + 4 + bz0 // 2, :
                    ]
                continue
            start0[r, ROW - 4 : ROW + bz0 + 4, :] = g0[r, ROW - 4 : ROW + bz0 + 4, :] + temp[0 : bz0 + 8, :]

    level.up(s1, start1, middle, update, to_level_0, range(3, 9), row, count, base1 - 2, bz1 + 4)
    level = Level(0, gx, gz, (bx0, bz0), cells[0], 3, (None, *coefs0))

    def to_out(p, value):
        out[p - 3, :, :] = value

    level.up(s0, start0, middle, update, to_out, range(3, 11), ROW - 4, bz0 + 8, ROW, bz0)


def f32(*shape):
    return jax.ShapeDtypeStruct(shape, jnp.float32)


def scratch(*shape):
    return pltpu.VMEM(shape, jnp.float32)


def call(kernel, name, outs, scratches, *args, aliases={}):
    limit = 4 * 2**20 + sum(4 * math.prod(ref.shape) for ref in [*scratches, *outs, *args])
    vmem = pl.BlockSpec(memory_space=pltpu.VMEM)
    return pl.pallas_call(
        kernel,
        name=name,
        out_shape=outs,
        in_specs=[vmem] * len(args),
        out_specs=[vmem] * len(outs),
        scratch_shapes=scratches,
        input_output_aliases=aliases,
        compiler_params=pltpu.CompilerParams(vmem_limit_bytes=limit),
    )(*args)


def shift(array, axis, by):
    devices = lax.axis_size(axis)
    return lax.ppermute(array, axis, [(i, i + by) for i in range(devices) if 0 <= i + by < devices])


def turn(array, axis, by):
    devices = lax.axis_size(axis)
    return lax.ppermute(array, axis, [(i, (i + by) % devices) for i in range(devices)])


def on_device(right_side, conductivity):
    nx, nz = (lax.axis_size("gx"), lax.axis_size("gz"))
    bx, bz = right_side.shape[0:2]
    cells = [(nx * bx >> level, nz * bz >> level) for level in range(4)]
    for_next = jnp.concatenate([right_side[bx - 2 :], conductivity[bx - 3 :]])
    for_prev = jnp.concatenate([right_side[:2], conductivity[:3]])
    low, high = (shift(for_next, "gx", 1), shift(for_prev, "gx", -1))
    planes = bx + 6
    to_high, to_low = call(
        edge_rows_0, "edge_rows_0", [f32(-(-edge_spec_0(bx)[1] // 8) * 8, LANES)] * 2, [], right_side, conductivity, low, high
    )
    z_low, z_high = (turn(to_high, "gz", 1), turn(to_low, "gz", -1))
    window = (planes, bz + 32, LANES)
    half1 = (bx // 2 + 2, bz // 2 + 8, LANES)
    arrays = call(
        functools.partial(inner_0, cells[0]),
        "inner_0",
        [f32(*window)] * 10 + [f32(bx // 2, bz // 2, LANES), f32(*half1)],
        [scratch(bz + 16, LANES)],
        right_side,
        conductivity,
        low,
        high,
    )
    *arrays, for_next, for_prev = call(
        functools.partial(outer_0, cells[0]),
        "outer_0",
        [f32(*array.shape) for array in arrays] + [f32(bx // 2, bz // 2, LANES)] * 2,
        [scratch(16, LANES)],
        z_low,
        z_high,
        *arrays,
        aliases={i + 2: i for i in range(12)},
    )
    kept0 = (arrays[0], arrays[2], *arrays[3:9])

    bx, bz = (bx // 2, bz // 2)
    low, high = (shift(for_next, "gx", 1), shift(for_prev, "gx", -1))
    to_high, to_low = call(
        edge_rows_1, "edge_rows_1", [f32(-(-3 * bx * EDGE // 8) * 8, LANES)] * 2, [], low, for_next, for_prev, high
    )
    z_low, z_high = (turn(to_high, "gz", 1), turn(to_low, "gz", -1))
    window = (3 * bx, bz + 48, LANES)
    half2 = (bx // 2 + 4, bz // 2 + 16, LANES)
    arrays1 = call(
        functools.partial(inner_1, cells[1]),
        "inner_1",
        [f32(*window)] * 10 + [f32(*half2)] * 2,
        [scratch(bz, LANES)],
        arrays[10],
        arrays[11],
        low,
        high,
    )
    *arrays1, for_next, for_prev = call(
        functools.partial(outer_1, cells[1]),
        "outer_1",
        [f32(*array.shape) for array in arrays1] + [f32(2, bz // 2 + 16, LANES)] * 2,
        [scratch(16, LANES)],
        z_low,
        z_high,
        *arrays1,
        aliases={i + 2: i for i in range(12)},
    )
    kept1 = (arrays1[0], arrays1[2], *arrays1[3:9])

    bx, bz = (bx // 2, bz // 2)
    prev, next_ = (shift(for_next, "gx", 1), shift(for_prev, "gx", -1))
    window = (bx + 8, bz + 32, LANES)
    *kept2, row3, for_next, for_prev = call(
        functools.partial(down_2, cells[2]),
        "down_2",
        [f32(*window)] * 8 + [f32(nx, 2, LANES)] + [f32(LATE, bz + 16, LANES)] * 2,
        [scratch(*window)] * 2 + [scratch(bz + 16, LANES)],
        prev,
        for_next,
        next_,
        arrays[2],
    )

    here = lax.all_to_all(row3, "gx", 0, 0, tiled=True).reshape(2 * nx, LANES)
    widths = [part_of_x(which, nx)[1] for which in range(3)]
    for_next, _ = lax.optimization_barrier((for_next, here))
    prev2 = shift(for_next, "gx", 1)
    (here,) = call(functools.partial(window_3, nx), "window_3", [f32(2 * widths[0], LANES)], [], here)
    low, high = (turn(here, "gz", 1), turn(here, "gz", -1))
    solving = [[scratch(2, 3, width + 16, LANES), scratch(3, width, LANES)] for width in widths]
    base, here = call(
        functools.partial(solve_first, nz, nx),
        "solve_first",
        [f32(21, widths[0], LANES), f32(2, widths[1], LANES)],
        [scratch(3, widths[0] + 16, LANES)] + solving[0],
        low,
        here,
        high,
    )
    low, high = (turn(here, "gz", 1), turn(here, "gz", -1))
    for_prev, _ = lax.optimization_barrier((for_prev, here))
    next2 = shift(for_prev, "gx", -1)
    base2, base3 = call(
        functools.partial(narrow, nx), "narrow", [f32(21, width, LANES) for width in widths[1:]], [], base
    )
    (here,) = call(
        functools.partial(solve_next, nz, nx),
        "solve_next",
        [f32(2, widths[2], LANES)],
        solving[1],
        base2,
        low,
        here,
        high,
    )
    low, high = (turn(here, "gz", 1), turn(here, "gz", -1))

    bx, bz = right_side.shape[0:2]
    window = (bx + 6, bz + 32, LANES)
    work = solving[2] + [scratch(5 * (bz // 4 + 8), LANES), scratch(bz + 32, LANES)]
    work += [scratch(bx // 4 + 8, bz // 4 + 32, LANES), scratch(bx // 2 + 8, bz // 2 + 48, LANES)]
    work += [scratch(*window)] * 3
    (result,) = call(
        functools.partial(finish, cells), "finish", [f32(*right_side.shape)], work, base3, low, here, high,
        prev2, next2, *kept2, *kept1, *kept0,
    )
    return result


def solution(mesh):
    return jax.shard_map(
        on_device,
        mesh=mesh,
        in_specs=(P("gx", "gz", None), P("gx", "gz", None)),
        out_specs=P("gx", "gz", None),
        check_vma=False,
    )
```

```python
import functools
import math

import jax
import jax.numpy as jnp
from jax import lax
from jax.experimental import pallas as pl
from jax.experimental.pallas import tpu as pltpu
from jax.sharding import PartitionSpec as P

COARSE_ITERS = 20
LANES = 128
ROW = 16
EDGE = 13
LATE = 3
WIDTHS = ((22, 48), (14, 32), (6, 16))
SOLVE = (8, 16)


def cheb_weights(count, lower, upper):
    theta = 0.5 * (upper + lower)
    delta = 0.5 * (upper - lower)
    sigma = theta / delta
    rho_prev = 1.0 / sigma
    carry_terms = [0.0]
    gain_terms = [1.0 / theta]
    for step in range(1, count):
        rho_next = 1.0 / (2.0 * sigma - rho_prev)
        carry_terms.append(rho_next * rho_prev)
        gain_terms.append(2.0 * rho_next / delta)
        rho_prev = rho_next
    return (carry_terms, gain_terms)


(_, CARRY), (GAIN_FIRST, GAIN) = cheb_weights(2, 0.25, 2.0)


def lanes_of(rows):
    return lax.broadcasted_iota(jnp.int32, (rows, LANES), 1)


def rows_of(rows):
    return lax.broadcasted_iota(jnp.int32, (rows, LANES), 0)


def roll(value, shift, axis=1):
    return pltpu.roll(value, shift % value.shape[axis], axis)


def pair_sum(value, stride):
    odd = (lanes_of(value.shape[0]) & stride) != 0
    return value + jnp.where(odd, roll(value, stride), roll(value, -stride))


class Level:
    def __init__(self, level, gx, gz, brick, cells, first_plane, refs, first_row=ROW):
        self.stride, self.scale, self.first_row = (2**level, 0.25**level, first_row)
        self.gx, self.gz, self.brick, self.cells, self.first_plane = (gx, gz, brick, cells, first_plane)
        self.half, self.fx, self.fz, self.left, self.right, self.diag, self.inverse = refs

    def coefs(self, planes, row, count, source, first):
        half, stride = (self.half, self.stride)
        lane = lanes_of(count)
        in_left, in_right = (lane >= stride, lane < LANES - stride)
        here = rows_of(count) + (row - self.first_row + self.gz * self.brick[1])
        inside_rows = jnp.where((here >= 0) & (here < self.cells[1]), 1.0 / self.scale, 0.0)
        for p in planes:
            center = half[p, row : row + count, :]
            before = center + half[p - 1, row : row + count, :]
            after = center + half[p + 1, row : row + count, :]
            low = center + half[p, row - 1 : row - 1 + count, :]
            high = center + half[p, row + 1 : row + 1 + count, :]
            left = center + jnp.where(in_left, roll(center, stride), 0.0)
            right = center + jnp.where(in_right, roll(center, -stride), 0.0)
            diagonal = ((before + after) + (low + high)) + (left + right)
            plane = p - self.first_plane + self.gx * self.brick[0]
            inside = jnp.where(jnp.logical_and(plane >= 0, plane < self.cells[0]), 1.0, 0.0)
            inverse = (inside * inside_rows) * jnp.where(diagonal > 0.0, 1.0 / diagonal, 0.0)
            self.fx[p, row : row + count, :] = before
            self.fz[p, row : row + count, :] = low
            self.fz[p, row + 1 : row + 1 + count, :] = high
            self.left[p, row : row + count, :] = jnp.where(in_left, left, 0.0)
            self.right[p, row : row + count, :] = jnp.where(in_right, right, 0.0)
            self.diag[p, row : row + count, :] = diagonal
            self.inverse[p, row : row + count, :] = inverse
            first[p, row : row + count, :] = GAIN_FIRST * (inverse * source[p, row : row + count, :])
        self.fx[planes[-1] + 1, row : row + count, :] = after

    def remainder(self, source, guess, p, row, count):
        center = guess[p, row : row + count, :]
        beside = (
            self.fx[p, row : row + count, :] * guess[p - 1, row : row + count, :]
            + self.fx[p + 1, row : row + count, :] * guess[p + 1, row : row + count, :]
        )
        beside = beside + (
            self.fz[p, row : row + count, :] * guess[p, row - 1 : row - 1 + count, :]
            + self.fz[p, row + 1 : row + 1 + count, :] * guess[p, row + 1 : row + 1 + count, :]
        )
        beside = beside + (
            self.left[p, row : row + count, :] * roll(center, self.stride)
            + self.right[p, row : row + count, :] * roll(center, -self.stride)
        )
        applied = self.diag[p, row : row + count, :] * center - beside
        return source[p, row : row + count, :] - self.scale * applied

    def second_down(self, source, first, out, planes, row, count):
        for p in planes:
            rest = self.remainder(source, first, p, row, count)
            start = first[p, row : row + count, :]
            update = CARRY * start + GAIN * (self.inverse[p, row : row + count, :] * rest)
            out[p, row : row + count, :] = start + update

    def restricted_remainder(self, source, guess, temp, planes, row, rows):
        parts = []
        for p in planes[::2]:
            both = self.remainder(source, guess, p, row, rows) + self.remainder(source, guess, p + 1, row, rows)
            temp[0:rows, :] = pair_sum(both, self.stride)
            parts.append(0.125 * (temp[pl.ds(0, rows // 2, stride=2), :] + temp[pl.ds(1, rows // 2, stride=2), :]))
        return parts

    def up(self, source, start, middle, update, out, planes, row, count, out_row, out_count):
        for p in range(planes[0] - 1, planes[-1] + 2):
            first = GAIN_FIRST * (
                self.inverse[p, row : row + count, :] * self.remainder(source, start, p, row, count)
            )
            update[p, row : row + count, :] = first
            middle[p, row : row + count, :] = start[p, row : row + count, :] + first
        for p in planes:
            second = CARRY * update[p, out_row : out_row + out_count, :] + GAIN * (
                self.inverse[p, out_row : out_row + out_count, :]
                * self.remainder(source, middle, p, out_row, out_count)
            )
            out(p, middle[p, out_row : out_row + out_count, :] + second)


def restricted(half, temp, stride, planes, row, rows):
    parts = []
    for p in planes[::2]:
        both = half[p, row : row + rows, :] + half[p + 1, row : row + rows, :]
        temp[0:rows, :] = pair_sum(both, stride)
        parts.append(0.125 * (temp[pl.ds(0, rows // 2, stride=2), :] + temp[pl.ds(1, rows // 2, stride=2), :]))
    return parts


def first_iterate(source, half, p, count, level, stride):
    center = half[p][1 : 1 + count]
    lane = lanes_of(count)
    diagonal = 6.0 * center + half[p - 1][1 : 1 + count] + half[p + 1][1 : 1 + count]
    diagonal = diagonal + half[p][0:count] + half[p][2 : 2 + count]
    diagonal = diagonal + jnp.where(lane >= stride, roll(center, stride), 0.0)
    diagonal = diagonal + jnp.where(lane < LANES - stride, roll(center, -stride), 0.0)
    inverse = jnp.where(diagonal > 0.0, 1.0 / (0.25**level * diagonal), 0.0)
    return GAIN_FIRST * source * inverse


def cut(half_ref, planes, row, count):
    return [half_ref[p, row : row + count, :] for p in planes]


def edge_spec_0(bx):
    spec, at = ([], 0)
    for p in range(bx + 6):
        away = max(3 - p, p - bx - 2, 0)
        spec.append((p, at, 3 - away, 4 - away))
        at += 7 - 2 * away
    return spec, at


def edge_rows_0(source, cond, low, high, to_high, to_low):
    bx, bz = source.shape[0:2]
    spec, length = edge_spec_0(bx)
    for p, at, few, many in spec:
        if p < 3:
            (part, q), (other, r) = ((low, p - 1), (low, p + 2))
        elif p < bx + 3:
            (part, q), (other, r) = ((source, p - 3), (cond, p - 3))
        else:
            (part, q), (other, r) = ((high, p - bx - 3), (high, p - bx - 1))
        if few:
            to_high[at : at + few, :] = part[q, bz - few : bz, :]
            to_low[at : at + few, :] = part[q, 0:few, :]
        to_high[at + few : at + few + many, :] = other[r, bz - many : bz, :]
        to_low[at + few : at + few + many, :] = other[r, 0:many, :]
    rest = to_high.shape[0] - length
    for out in (to_high, to_low):
        out[length : length + rest, :] = jnp.zeros((rest, LANES), jnp.float32)


def inner_0(cells, source, cond, low, high, win_s, win_h, guess, fx, fz, left, right, diag, inverse, first, next_source, next_half, temp):
    gx, gz = (lax.axis_index("gx"), lax.axis_index("gz"))
    bx, bz = source.shape[0:2]
    planes, end = (bx + 6, ROW + bz)
    zero = jnp.zeros((8, LANES), jnp.float32)
    for p in range(planes):
        for edge in (8, end, end + 8):
            win_s[p, edge : edge + 8, :] = zero
            win_h[p, edge : edge + 8, :] = zero
            guess[p, edge : edge + 8, :] = zero
            first[p, edge : edge + 8, :] = zero
    for p in range(bx):
        win_s[p + 3, ROW:end, :] = source[p, :, :]
        win_h[p + 3, ROW:end, :] = 0.5 * cond[p, :, :]
    for p in range(2):
        win_s[p + 1, ROW:end, :] = low[p, :, :]
        win_s[p + bx + 3, ROW:end, :] = high[p, :, :]
    for p in range(3):
        win_h[p, ROW:end, :] = 0.5 * low[p + 2, :, :]
        win_h[p + bx + 3, ROW:end, :] = 0.5 * high[p + 2, :, :]
    level = Level(0, gx, gz, (bx, bz), cells, 3, (win_h, fx, fz, left, right, diag, inverse))
    level.coefs(range(1, planes - 1), ROW, bz, win_s, first)
    level.second_down(win_s, first, guess, range(2, planes - 2), ROW, bz)
    for p, value in enumerate(level.restricted_remainder(win_s, guess, temp, range(3, 3 + bx), ROW, bz)):
        next_source[p, :, :] = value
    for p, value in enumerate(restricted(win_h, temp, 1, range(1, planes - 1), ROW - 8, bz + 16)):
        next_half[p, :, :] = value


def outer_0(cells, z_low, z_high, *refs):
    win_s, win_h, guess, fx, fz, left, right, diag, inverse, first, next_source, next_half = refs[12:24]
    to_next, to_prev, temp = refs[24:]
    gx, gz = (lax.axis_index("gx"), lax.axis_index("gz"))
    planes, bx, bz = (win_s.shape[0], win_s.shape[0] - 6, win_s.shape[1] - 32)
    end = ROW + bz
    has_low, has_high = inside_z(gz, cells[1] // bz)
    for p, at, few, many in edge_spec_0(bx)[0]:
        if few:
            win_s[p, ROW - few : ROW, :] = z_low[at : at + few, :]
            win_s[p, end : end + few, :] = z_high[at : at + few, :]
        win_h[p, ROW - many : ROW, :] = (0.5 * has_low) * z_low[at + few : at + few + many, :]
        win_h[p, end : end + many, :] = (0.5 * has_high) * z_high[at + few : at + few + many, :]
    level = Level(0, gx, gz, (bx, bz), cells, 3, (win_h, fx, fz, left, right, diag, inverse))
    strips = ROW - 4, end - 4
    for row in strips:
        level.coefs(range(1, planes - 1), row, 8, win_s, first)
    for row in strips:
        level.second_down(win_s, first, guess, range(2, planes - 2), row, 8)
    own = bz // 2
    for row, at in ((ROW, 0), (end - 8, own - 4)):
        for p, value in enumerate(level.restricted_remainder(win_s, guess, temp, range(3, 3 + bx), row, 8)):
            next_source[p, at : at + 4, :] = value
        for p, value in enumerate(restricted(win_h, temp, 1, range(1, planes - 1), row - 8 if row == ROW else end, 8)):
            at_half = 0 if row == ROW else own + 4
            next_half[p, at_half : at_half + 4, :] = value
    odd = (lanes_of(own) & 1) == 1
    padded = cut(next_half, range(bx // 2 + 2), 3, own + 2)
    last = bx // 2 - 1
    for p in range(bx // 2):
        mixed = jnp.where(odd, padded[p + 1][1 : 1 + own], next_source[p, :, :])
        to_next[p, :, :] = mixed
        to_prev[p, :, :] = mixed
    for p, out in ((0, to_next), (last, to_prev)):
        iterate = first_iterate(next_source[p, :, :], padded, p + 1, own, 1, 2)
        out[p, :, :] = jnp.where(odd, padded[p + 1][1 : 1 + own], iterate)


def inside_z(gz, count):
    return (jnp.where(gz > 0, 1.0, 0.0), jnp.where(gz < count - 1, 1.0, 0.0))


def edge_rows_1(low, to_next, to_prev, high, to_high, to_low):
    bx, rows = low.shape[0:2]
    own = [to_prev] * (bx - 1) + [to_next]
    planes = [(low, p) for p in range(bx)] + list(zip(own, range(bx))) + [(high, p) for p in range(bx)]
    for at, (part, p) in enumerate(planes):
        to_high[EDGE * at : EDGE * (at + 1), :] = part[p, rows - EDGE : rows, :]
        to_low[EDGE * at : EDGE * (at + 1), :] = part[p, 0:EDGE, :]
    used, whole = (EDGE * len(planes), to_high.shape[0])
    for out in (to_high, to_low):
        out[used:whole, :] = jnp.zeros((whole - used, LANES), jnp.float32)


def unpack_1(win_s, win_h, p, start, rows, mixed):
    odd = (lanes_of(rows) & 1) == 1
    win_s[p, start : start + rows, :] = jnp.where(odd, roll(mixed, 1), mixed)
    win_h[p, start : start + rows, :] = jnp.where(odd, mixed, roll(mixed, -1))


def inner_1(cells, source, half, low, high, win_s, win_h, guess, fx, fz, left, right, diag, inverse, first, next_source, next_half, temp):
    gx, gz = (lax.axis_index("gx"), lax.axis_index("gz"))
    bx, bz = source.shape[0:2]
    planes, base = (3 * bx, 24)
    end = base + bz
    zero = jnp.zeros((8, LANES), jnp.float32)
    for p in range(bx):
        unpack_1(win_s, win_h, p, base, bz, low[p, :, :])
        unpack_1(win_s, win_h, 2 * bx + p, base, bz, high[p, :, :])
        win_s[bx + p, base:end, :] = source[p, :, :]
        win_h[bx + p, base:end, :] = half[p + 1, 4 : 4 + bz, :]
    for p in (0, planes - 1):
        first[p, base:end, :] = win_s[p, base:end, :]
    for p in range(planes):
        for ref in (win_s, win_h, first, guess):
            for row in (0, 8, 16, end, end + 8, end + 16):
                ref[p, row : row + 8, :] = zero
    level = Level(1, gx, gz, (bx, bz), cells, bx, (win_h, fx, fz, left, right, diag, inverse), base)
    level.coefs(range(1, planes - 1), base, bz, win_s, first)
    level.second_down(win_s, first, guess, range(1, planes - 1), base, bz)
    next_source[...] = jnp.zeros(next_source.shape, jnp.float32)
    own = bz // 2
    for p, value in enumerate(level.restricted_remainder(win_s, guess, temp, range(bx - 2, 2 * bx + 2), base, bz)):
        next_source[p + 1, 8 : 8 + own, :] = value
    for p, value in enumerate(restricted(win_h, temp, 2, range(planes), base, bz)):
        next_half[p, 8 : 8 + own, :] = value


def outer_1(cells, z_low, z_high, *refs):
    win_s, win_h, guess, fx, fz, left, right, diag, inverse, first, next_source, next_half = refs[12:24]
    to_next, to_prev, temp = refs[24:]
    gx, gz = (lax.axis_index("gx"), lax.axis_index("gz"))
    planes, base = (win_s.shape[0], 24)
    bx, bz = (planes // 3, win_s.shape[1] - 48)
    end = base + bz
    has_low, has_high = inside_z(gz, cells[1] // bz)
    for start, ref, inside in ((base - EDGE, z_low, has_low), (end, z_high, has_high)):
        for p in range(planes):
            unpack_1(win_s, win_h, p, start, EDGE, inside * ref[EDGE * p : EDGE * (p + 1), :])
        for p in (0, planes - 1):
            first[p, start : start + EDGE, :] = win_s[p, start : start + EDGE, :]
    level = Level(1, gx, gz, (bx, bz), cells, bx, (win_h, fx, fz, left, right, diag, inverse), base)
    strips = base - 12, end - 4
    for row in strips:
        level.coefs(range(1, planes - 1), row, 16, win_s, first)
    for row in strips:
        level.second_down(win_s, first, guess, range(1, planes - 1), row, 16)
    for row in strips:
        at = (row - base + 16) // 2
        for p, value in enumerate(level.restricted_remainder(win_s, guess, temp, range(bx - 2, 2 * bx + 2), row, 16)):
            next_source[p + 1, at : at + 8, :] = value
    for row in (base - 16, end):
        at = (row - base + 16) // 2
        for p, value in enumerate(restricted(win_h, temp, 2, range(planes), row, 16)):
            next_half[p, at : at + 8, :] = value
    lane = lanes_of(next_source.shape[1]) & 3

    def pair(p):
        mixed = jnp.where(lane == 0, next_source[p, :, :], next_half[p, :, :])
        mixed = jnp.where(lane == 2, next_source[p + 1, :, :], mixed)
        return jnp.where(lane == 3, next_half[p + 1, :, :], mixed)

    middle = pair(2)
    to_next[0, :, :] = pair(0)
    to_next[1, :, :] = middle
    to_prev[0, :, :] = middle
    to_prev[1, :, :] = pair(4)


def spread(mixed, which):
    only = jnp.where((lanes_of(mixed.shape[0]) & 3) == which, mixed, 0.0)
    only = roll(only, -which) if which else only
    twice = only + roll(only, 1)
    return twice + roll(twice, 2)


def down_2(cells, prev, here, next_, guess0, win_s, guess, fx, fz, left, right, diag, inverse, message, to_next, to_prev, win_h, first, temp):
    gx, gz = (lax.axis_index("gx"), lax.axis_index("gz"))
    bx, bz = (2, prev.shape[1] - 16)
    own, planes = (4, 10)
    end = ROW + bz
    zero = jnp.zeros((8, LANES), jnp.float32)
    pairs = (prev, 0), (prev, 1), (here, 1), (next_, 0), (next_, 1)
    for q, (part, at) in enumerate(pairs):
        mixed = part[at, :, :]
        for p in range(2):
            win_s[2 * q + p, 8 : end + 8, :] = spread(mixed, 2 * p)
            win_h[2 * q + p, 8 : end + 8, :] = spread(mixed, 2 * p + 1)
    for p in range(planes):
        for ref in (win_s, win_h, first):
            ref[p, 0:8, :] = zero
            ref[p, end + 8 : end + 16, :] = zero
    level = Level(2, gx, gz, (bx, bz), cells, own, (win_h, fx, fz, left, right, diag, inverse))
    row, count = (ROW - 8, bz + 16)
    level.coefs(range(own - 3, own + 5), row, count, win_s, first)
    level.second_down(win_s, first, guess, range(own - 2, own + 4), row, count)
    lane = lanes_of(count) & 3
    for out, begin in ((to_next, own - 2), (to_prev, own)):
        mixed = guess[begin, row : row + count, :]
        for p in range(1, 4):
            mixed = jnp.where(lane == p, guess[begin + p, row : row + count, :], mixed)
        out[0, :, :] = mixed
        far = guess0.shape[0] - 5 if out is to_next else 4
        for p in range(1, LATE):
            begin0 = ROW + (p - 1) * count
            out[p, :, :] = guess0[far, begin0 : begin0 + count, :]
    sources = level.restricted_remainder(win_s, guess, temp, range(own, own + bx), ROW, bz)
    halves = restricted(win_h, temp, 4, range(own, own + bx), ROW, bz)
    rows = bz // 2
    cell = lax.broadcasted_iota(jnp.int32, (LANES, LANES), 0)
    lane = lax.broadcasted_iota(jnp.int32, (LANES, LANES), 1)
    pick = jnp.where(((cell >> 3) == (lane & 15)) & ((cell & 7) == 0), 1.0, 0.0)
    keep = (lanes_of(rows) >> 4) == rows_of(rows)
    both = jnp.concatenate([sources[0], halves[0]])
    both = jnp.dot(both, pick, precision=lax.Precision.HIGHEST, preferred_element_type=jnp.float32)
    for at in range(2):
        dense = jnp.sum(jnp.where(keep, both[at * rows : (at + 1) * rows], 0.0), axis=0, keepdims=True)
        for device in range(message.shape[0]):
            message[device, at : at + 1, :] = dense


def part_of_x(which, planes):
    before, width = WIDTHS[which]
    width = min(width, planes)
    return (jnp.clip(lax.axis_index("gx") - before, 0, planes - width), width)


class Coarsest:
    def __init__(self, base, state, update):
        self.base, self.state, self.update, self.now = (base, state, update, 0)
        self.planes = update.shape[1]
        self.weights = list(zip(*cheb_weights(COARSE_ITERS, 0.02, 2.0)))
        zero = jnp.zeros((8, LANES), jnp.float32)
        for buffer in range(2):
            for b in range(3):
                state[buffer, b, 0:8, :] = zero
                state[buffer, b, self.planes + 8 : self.planes + 16, :] = zero

    def beside_z(self, values):
        lane = lanes_of(values[0].shape[0])
        ahead, back = ([roll(v, 16) for v in values], [roll(v, -16) for v in values])
        before = [jnp.where(lane < 16, ahead[max(b - 1, 0)], ahead[b]) for b in range(3)]
        after = [jnp.where(lane >= LANES - 16, back[min(b + 1, 2)], back[b]) for b in range(3)]
        return before, after

    def start(self, parts, half, flags):
        planes, zero = (self.planes, jnp.zeros((8, LANES), jnp.float32))
        gain = self.weights[0][1]
        for b in range(3):
            half[b, 0:8, :] = zero
            half[b, planes + 8 : planes + 16, :] = zero
            half[b, 8 : planes + 8, :] = flags[b] * parts[b][pl.ds(1, planes, stride=2), :]
        lane = lanes_of(8)
        in_left, in_right = ((lane & 15) > 0, (lane & 15) < 15)
        for x in range(0, planes, 8):
            centers = [half[b, x + 8 : x + 16, :] for b in range(3)]
            before, after = self.beside_z(centers)
            for b, center in enumerate(centers):
                faces = [
                    center + half[b, x + 7 : x + 15, :],
                    center + half[b, x + 9 : x + 17, :],
                    center + before[b],
                    center + after[b],
                    center + jnp.where(in_left, roll(center, 1), 0.0),
                    center + jnp.where(in_right, roll(center, -1), 0.0),
                ]
                diagonal = faces[0] + faces[1] + faces[2] + faces[3] + faces[4] + faces[5]
                inverse = flags[b] * jnp.where(diagonal > 0.0, 1.0 / diagonal, 0.0)
                faces = [face * inverse for face in faces]
                faces[4] = jnp.where(in_left, faces[4], 0.0)
                faces[5] = jnp.where(in_right, faces[5], 0.0)
                for which, face in enumerate(faces):
                    self.base[7 * b + which, x : x + 8, :] = face
                scaled = 64.0 * (parts[b][pl.ds(2 * x, 8, stride=2), :] * inverse)
                self.base[7 * b + 6, x : x + 8, :] = scaled
                self.update[b, x : x + 8, :] = gain * scaled
                self.state[self.now, b, x + 8 : x + 16, :] = gain * scaled

    def resume(self, parts, flags):
        for b in range(3):
            self.state[self.now, b, 8 : self.planes + 8, :] = flags[b] * parts[b][0, :, :]
            self.update[b, :, :] = flags[b] * parts[b][1, :, :]

    def steps(self, which, keep):
        for index in which:
            blocks = range(3) if keep or index < which[-1] else (1,)
            carry, gain = self.weights[index]
            old, new = (self.now, 1 - self.now)
            for x in range(0, self.planes, 8):
                centers = [self.state[old, b, x + 8 : x + 16, :] for b in range(3)]
                before, after = self.beside_z(centers)
                for b in blocks:
                    center = centers[b]
                    face = [self.base[7 * b + k, x : x + 8, :] for k in range(7)]
                    beside = face[0] * self.state[old, b, x + 7 : x + 15, :] + face[1] * self.state[old, b, x + 9 : x + 17, :]
                    beside = beside + (face[2] * before[b] + face[3] * after[b])
                    beside = beside + (face[4] * roll(center, 1) + face[5] * roll(center, -1))
                    change = carry * self.update[b, x : x + 8, :] + gain * (face[6] - center + beside)
                    self.update[b, x : x + 8, :] = change
                    self.state[new, b, x + 8 : x + 16, :] = center + change
            self.now = new

    def leave(self, out, skip):
        count = out.shape[1]
        out[0, :, :] = self.state[self.now, 1, pl.ds(skip + 8, count), :]
        out[1, :, :] = self.update[1, pl.ds(skip, count), :]


def window_3(planes, whole, out):
    first, width = part_of_x(0, planes)
    out[...] = whole[pl.ds(2 * first, 2 * width), :]


def narrow(planes, base, second, third):
    first = part_of_x(0, planes)[0]
    for which, out in ((1, second), (2, third)):
        begin, width = part_of_x(which, planes)
        for k in range(base.shape[0]):
            out[k, :, :] = base[k, pl.ds(begin - first, width), :]


def solve_first(count, planes, low, here, high, base, out, half, state, update):
    has_low, has_high = inside_z(lax.axis_index("gz"), count)
    level = Coarsest(base, state, update)
    level.start((low, here, high), half, (has_low, 1.0, has_high))
    level.steps(range(1, SOLVE[0]), False)
    level.leave(out, part_of_x(1, planes)[0] - part_of_x(0, planes)[0])


def solve_next(count, planes, base, low, here, high, out, state, update):
    has_low, has_high = inside_z(lax.axis_index("gz"), count)
    level = Coarsest(base, state, update)
    level.resume((low, here, high), (has_low, 1.0, has_high))
    level.steps(range(SOLVE[0], SOLVE[1]), False)
    level.leave(out, part_of_x(2, planes)[0] - part_of_x(1, planes)[0])


def finish(cells, base, low, here, high, prev2, next2, *refs):
    gx, gz = (lax.axis_index("gx"), lax.axis_index("gz"))
    (s2, g2, *coefs2), (s1, g1, *coefs1), (s0, g0, *coefs0) = (refs[0:8], refs[8:16], refs[16:24])
    out, state, update3, coarse2, temp, start2, start1, start0, middle, update, result, sent = refs[24:]
    bz0 = out.shape[1]
    bz1, bz2 = (bz0 // 2, bz0 // 4)
    has_low, has_high = inside_z(gz, cells[0][1] // bz0)
    level = Coarsest(base, state, update3)
    level.resume((low, here, high), (has_low, 1.0, has_high))
    level.steps(range(SOLVE[1], COARSE_ITERS), True)
    last = level.now

    bx2 = 2
    rows = bz2 + 8
    cell = lax.broadcasted_iota(jnp.int32, (LANES, LANES), 0)
    lane = lax.broadcasted_iota(jnp.int32, (LANES, LANES), 1)
    pick = jnp.where((cell & 15) == (lane >> 3), 1.0, 0.0)
    z3 = (rows_of(rows) >> 1) - 2
    keep = (lanes_of(rows) >> 4) == (z3 & 7)
    local = gx - part_of_x(2, cells[3][0])[0]
    columns = [state[last, b, pl.ds(local + 6, 8), :] for b in range(3)]
    for q in range(5):
        picked = [column[q : q + 1, :] for column in columns]
        wide = jnp.where(z3 < 0, picked[0], jnp.where(z3 < 8, picked[1], picked[2]))
        coarse2[q * rows : (q + 1) * rows, :] = jnp.where(keep, wide, 0.0)
    spread_out = jnp.dot(coarse2[...], pick, precision=lax.Precision.HIGHEST, preferred_element_type=jnp.float32)
    coarse2[...] = spread_out

    start, own = (start2, 4)
    row, count = (ROW - 4, rows)
    zero = jnp.zeros((8, LANES), jnp.float32)
    for q in range(5):
        for p in (own - 4 + 2 * q, own - 3 + 2 * q):
            start[p, 8:16, :] = zero
            start[p, ROW + bz2 : ROW + bz2 + 8, :] = zero
            if q == 2:
                guess = g2[p, row : row + count, :]
            else:
                guess = spread((prev2 if q < 2 else next2)[0, 4 : 4 + count, :], p if q < 2 else p - own - bx2)
            start[p, row : row + count, :] = guess + coarse2[q * rows : (q + 1) * rows, :]
    level = Level(2, gx, gz, (bx2, bz2), cells[2], own, (None, *coefs2))

    bx1, base1 = (4, 24)

    def to_level_1(p, value):
        q = 2 * (p - own) + 4
        temp[pl.ds(0, value.shape[0], stride=2), :] = value
        temp[pl.ds(1, value.shape[0], stride=2), :] = value
        for r in (q, q + 1):
            if 1 <= r <= 10:
                start1[r, base1 - 4 : base1 + bz1 + 4, :] = (
                    g1[r, base1 - 4 : base1 + bz1 + 4, :] + temp[0 : bz1 + 8, :]
                )

    for r in range(1, 11):
        start1[r, base1 - 8 : base1, :] = zero
        start1[r, base1 + bz1 : base1 + bz1 + 8, :] = zero
    level.up(s2, start, middle, update, to_level_1, range(own - 2, own + 4), row, count, ROW - 2, bz2 + 4)
    level = Level(1, gx, gz, (bx1, bz1), cells[1], 4, (None, *coefs1), base1)
    row, count = (base1 - 4, bz1 + 8)

    bx0 = out.shape[0]
    for r in range(1, 13):
        start0[r, 8:16, :] = zero
        start0[r, ROW + bz0 : ROW + bz0 + 8, :] = zero

    def to_level_0(p, value):
        q = 2 * (p - 4) + 3
        temp[pl.ds(0, value.shape[0], stride=2), :] = value
        temp[pl.ds(1, value.shape[0], stride=2), :] = value
        for r in (q, q + 1):
            if r in (1, 12):
                for part in range(2):
                    begin = ROW + part * (bz0 // 2)
                    start0[r, begin : begin + bz0 // 2, :] = (prev2 if r == 1 else next2)[1 + part, :, :] + temp[
                        begin - ROW + 4 : begin - ROW + 4 + bz0 // 2, :
                    ]
                continue
            start0[r, ROW - 4 : ROW + bz0 + 4, :] = g0[r, ROW - 4 : ROW + bz0 + 4, :] + temp[0 : bz0 + 8, :]

    level.up(s1, start1, middle, update, to_level_0, range(3, 9), row, count, base1 - 2, bz1 + 4)
    level = Level(0, gx, gz, (bx0, bz0), cells[0], 3, (None, *coefs0))

    copies = [pltpu.make_async_copy(result.at[p], out.at[p], sent.at[p]) for p in range(bx0)]

    def to_out(p, value):
        result[p - 3, :, :] = value
        copies[p - 3].start()

    level.up(s0, start0, middle, update, to_out, range(3, 11), ROW - 4, bz0 + 8, ROW, bz0)
    for copy in copies:
        copy.wait()


def f32(*shape):
    return jax.ShapeDtypeStruct(shape, jnp.float32)


def scratch(*shape):
    return pltpu.VMEM(shape, jnp.float32)


def call(kernel, name, outs, scratches, *args, aliases={}, space=pltpu.VMEM, semaphores=()):
    limit = 4 * 2**20 + sum(4 * math.prod(ref.shape) for ref in [*scratches, *outs, *args])
    vmem = pl.BlockSpec(memory_space=pltpu.VMEM)
    return pl.pallas_call(
        kernel,
        name=name,
        out_shape=outs,
        in_specs=[vmem] * len(args),
        out_specs=[pl.BlockSpec(memory_space=space)] * len(outs),
        scratch_shapes=[*scratches, *semaphores],
        input_output_aliases=aliases,
        compiler_params=pltpu.CompilerParams(vmem_limit_bytes=limit),
    )(*args)


def shift(array, axis, by):
    devices = lax.axis_size(axis)
    return lax.ppermute(array, axis, [(i, i + by) for i in range(devices) if 0 <= i + by < devices])


def turn(array, axis, by):
    devices = lax.axis_size(axis)
    return lax.ppermute(array, axis, [(i, (i + by) % devices) for i in range(devices)])


def on_device(right_side, conductivity):
    nx, nz = (lax.axis_size("gx"), lax.axis_size("gz"))
    bx, bz = right_side.shape[0:2]
    cells = [(nx * bx >> level, nz * bz >> level) for level in range(4)]
    for_next = jnp.concatenate([right_side[bx - 2 :], conductivity[bx - 3 :]])
    for_prev = jnp.concatenate([right_side[:2], conductivity[:3]])
    low, high = (shift(for_next, "gx", 1), shift(for_prev, "gx", -1))
    planes = bx + 6
    to_high, to_low = call(
        edge_rows_0, "edge_rows_0", [f32(-(-edge_spec_0(bx)[1] // 8) * 8, LANES)] * 2, [], right_side, conductivity, low, high
    )
    z_low, z_high = (turn(to_high, "gz", 1), turn(to_low, "gz", -1))
    window = (planes, bz + 32, LANES)
    half1 = (bx // 2 + 2, bz // 2 + 8, LANES)
    arrays = call(
        functools.partial(inner_0, cells[0]),
        "inner_0",
        [f32(*window)] * 10 + [f32(bx // 2, bz // 2, LANES), f32(*half1)],
        [scratch(bz + 16, LANES)],
        right_side,
        conductivity,
        low,
        high,
    )
    *arrays, for_next, for_prev = call(
        functools.partial(outer_0, cells[0]),
        "outer_0",
        [f32(*array.shape) for array in arrays] + [f32(bx // 2, bz // 2, LANES)] * 2,
        [scratch(16, LANES)],
        z_low,
        z_high,
        *arrays,
        aliases={i + 2: i for i in range(12)},
    )
    kept0 = (arrays[0], arrays[2], *arrays[3:9])

    bx, bz = (bx // 2, bz // 2)
    low, high = (shift(for_next, "gx", 1), shift(for_prev, "gx", -1))
    to_high, to_low = call(
        edge_rows_1, "edge_rows_1", [f32(-(-3 * bx * EDGE // 8) * 8, LANES)] * 2, [], low, for_next, for_prev, high
    )
    z_low, z_high = (turn(to_high, "gz", 1), turn(to_low, "gz", -1))
    window = (3 * bx, bz + 48, LANES)
    half2 = (bx // 2 + 4, bz // 2 + 16, LANES)
    arrays1 = call(
        functools.partial(inner_1, cells[1]),
        "inner_1",
        [f32(*window)] * 10 + [f32(*half2)] * 2,
        [scratch(bz, LANES)],
        arrays[10],
        arrays[11],
        low,
        high,
    )
    *arrays1, for_next, for_prev = call(
        functools.partial(outer_1, cells[1]),
        "outer_1",
        [f32(*array.shape) for array in arrays1] + [f32(2, bz // 2 + 16, LANES)] * 2,
        [scratch(16, LANES)],
        z_low,
        z_high,
        *arrays1,
        aliases={i + 2: i for i in range(12)},
    )
    kept1 = (arrays1[0], arrays1[2], *arrays1[3:9])

    bx, bz = (bx // 2, bz // 2)
    prev, next_ = (shift(for_next, "gx", 1), shift(for_prev, "gx", -1))
    window = (bx + 8, bz + 32, LANES)
    *kept2, row3, for_next, for_prev = call(
        functools.partial(down_2, cells[2]),
        "down_2",
        [f32(*window)] * 8 + [f32(nx, 2, LANES)] + [f32(LATE, bz + 16, LANES)] * 2,
        [scratch(*window)] * 2 + [scratch(bz + 16, LANES)],
        prev,
        for_next,
        next_,
        arrays[2],
    )

    here = lax.all_to_all(row3, "gx", 0, 0, tiled=True).reshape(2 * nx, LANES)
    widths = [part_of_x(which, nx)[1] for which in range(3)]
    for_next, _ = lax.optimization_barrier((for_next, here))
    prev2 = shift(for_next, "gx", 1)
    (here,) = call(functools.partial(window_3, nx), "window_3", [f32(2 * widths[0], LANES)], [], here)
    low, high = (turn(here, "gz", 1), turn(here, "gz", -1))
    solving = [[scratch(2, 3, width + 16, LANES), scratch(3, width, LANES)] for width in widths]
    base, here = call(
        functools.partial(solve_first, nz, nx),
        "solve_first",
        [f32(21, widths[0], LANES), f32(2, widths[1], LANES)],
        [scratch(3, widths[0] + 16, LANES)] + solving[0],
        low,
        here,
        high,
    )
    low, high = (turn(here, "gz", 1), turn(here, "gz", -1))
    for_prev, _ = lax.optimization_barrier((for_prev, here))
    next2 = shift(for_prev, "gx", -1)
    base2, base3 = call(
        functools.partial(narrow, nx), "narrow", [f32(21, width, LANES) for width in widths[1:]], [], base
    )
    (here,) = call(
        functools.partial(solve_next, nz, nx),
        "solve_next",
        [f32(2, widths[2], LANES)],
        solving[1],
        base2,
        low,
        here,
        high,
    )
    low, high = (turn(here, "gz", 1), turn(here, "gz", -1))

    bx, bz = right_side.shape[0:2]
    window = (bx + 6, bz + 32, LANES)
    work = solving[2] + [scratch(5 * (bz // 4 + 8), LANES), scratch(bz + 32, LANES)]
    work += [scratch(bx // 4 + 8, bz // 4 + 32, LANES), scratch(bx // 2 + 8, bz // 2 + 48, LANES)]
    work += [scratch(*window)] * 3 + [scratch(*right_side.shape)]
    (result,) = call(
        functools.partial(finish, cells), "finish", [f32(*right_side.shape)], work, base3, low, here, high,
        prev2, next2, *kept2, *kept1, *kept0, space=pl.ANY, semaphores=[pltpu.SemaphoreType.DMA((bx,))],
    )
    return result


def solution(mesh):
    return jax.shard_map(
        on_device,
        mesh=mesh,
        in_specs=(P("gx", "gz", None), P("gx", "gz", None)),
        out_specs=P("gx", "gz", None),
        check_vma=False,
    )
```
